512 devices in a mesh: tile: 128 (over y, z, x_hi), date: 4 (over x_lo, core).
Axes of the slice: x: 4 (x_hi: 2, x_lo: 2; x = x_hi * 2 + x_lo), y: 8, z: 8, core: 2. Of those that a mesh axis runs over, the one named last changes fastest.
Arguments:
- inputs: bfloat16 [128, 4, 12, 8, 8, 192], P('tile', 'date'), may hold values from -74 to 74
- state: bfloat16 [128, 4, 12, 8, 8, 192], P('tile', 'date'), may hold values from -1 to 1
- cotangent: bfloat16 [128, 4, 12, 8, 8, 192], P('tile', 'date'), may hold values from -6 to 6
- adjacency: int32 [12, 4, 2], replicated, may hold values from 0 to 11, as said below
- taps: bfloat16 [2, 3, 192], replicated, may hold values from -3.5 to 3.5
- gain: bfloat16 [192], replicated, may hold values from 0.099609375 to 1.8984375
- w_up: bfloat16 [192, 768], replicated, may hold values from -0.4375 to 0.4375
- b_up: bfloat16 [768], replicated, may hold values from -3 to 3
- w_down: bfloat16 [768, 192], replicated, may hold values from -0.21875 to 0.21875
- b_down: bfloat16 [192], replicated, may hold values from -3 to 3
- w_gates: bfloat16 [384, 384], replicated, may hold values from -0.3125 to 0.3125
- b_gates: bfloat16 [384], replicated, may hold values from -3 to 3
- w_cand: bfloat16 [384, 192], replicated, may hold values from -0.3125 to 0.3125
- b_cand: bfloat16 [192], replicated, may hold values from -3 to 3
Outputs:
- new_state: bfloat16 [128, 4, 12, 8, 8, 192], P('tile', 'date')
- grad_input: bfloat16 [128, 4, 12, 8, 8, 192], P('tile', 'date')
- grad_taps: bfloat16 [2, 3, 192], replicated
- grad_gain: bfloat16 [192], replicated
- grad_up: bfloat16 [192, 768], replicated
- grad_bup: bfloat16 [768], replicated
- grad_down: bfloat16 [768, 192], replicated
- grad_bdown: bfloat16 [192], replicated
- grad_gates: bfloat16 [384, 384], replicated
- grad_bgates: bfloat16 [384], replicated
- grad_cand: bfloat16 [384, 192], replicated
- grad_bcand: bfloat16 [192], replicated
The draws below stay inside these ranges and needn't reach their ends.
Inputs may be any that keep to these rules, and one draw needn't show every extreme that they name: adjacency[f, e] = (n, k): edge e of face f borders edge k of face n, pixel a along e lying beside pixel a along k; k is the opposite edge (e + 2) mod 4, or else the first row is joined to the first column, or the last column to the last row; the pairing is symmetric, and the faces are those of the HEALPix base in some numbering.
All inputs are finite; a program needn't handle non-finite values.
Results may differ from the reference program's by a relative error of at most 0.012.
Values may be sent and summed in bfloat16 or wider, within the bound.
A program may use at most 64 MiB of HBM per device.

```python
import math
import jax
import jax.numpy as jnp
import numpy as np
from jax import lax

C = 192
FF = 768
FACES = 12
P_SIZE = 8
Q = 8
F = 64
PIXELS = 393216
N_TILE = 128
N_DATE = 4


def canonical_table():
    base_table = np.zeros((12, 4, 2), dtype=np.int32)
    for sector in range(4):
        later = (sector + 1) % 4
        earlier = (sector + 3) % 4
        base_table[sector] = [[later, 3], [4 + sector, 3], [4 + earlier, 0], [earlier, 0]]
        base_table[4 + sector] = [[later, 2], [8 + later, 3], [8 + sector, 0], [sector, 1]]
        base_table[8 + sector] = [[4 + sector, 2], [8 + later, 2], [8 + earlier, 1], [4 + earlier, 1]]
    return base_table


def draw_adjacency(key, part):
    key = jax.random.fold_in(key, 7)
    relabel_order = jax.random.permutation(key, 12).astype(jnp.int32)
    base_table = jnp.asarray(canonical_table())
    relabelled = jnp.stack([relabel_order[base_table[:, :, 0]], base_table[:, :, 1]], axis=-1)
    return jnp.zeros_like(relabelled).at[relabel_order].set(relabelled)


def draw_inputs(key, part):
    key = jax.random.fold_in(key, 11)
    first_key, second_key, third_key = jax.random.split(key, 3)
    shape = (N_TILE, N_DATE, FACES, P_SIZE, P_SIZE, C)
    values = jnp.clip(jax.random.normal(first_key, shape, jnp.float32), -6.0, 6.0)
    channel_scale = jnp.exp(jax.random.uniform(second_key, (C,), jnp.float32, math.log(0.35), math.log(3.5)))
    pixel_scale = jnp.exp(jax.random.uniform(third_key, (N_TILE, N_DATE, FACES, P_SIZE, P_SIZE, 1), jnp.float32, math.log(0.35), math.log(3.5)))
    return (values * channel_scale * pixel_scale).astype(jnp.bfloat16)


def levels(own_key, shape, cuts, smallest, largest):
    loudness = 1.0
    for position, parts in cuts:
        steps = jax.random.uniform(jax.random.fold_in(jax.random.fold_in(own_key, 6), position), (parts,), jnp.float32, smallest / len(cuts), largest / len(cuts))
        loudness = loudness * jnp.repeat(jnp.exp(steps), shape[position] // parts).reshape((-1,) + (1,) * (len(shape) - 1 - position))
    return loudness


def bell_draw(key, shape, scale, limit, cuts=(), held_as=jnp.bfloat16):
    entries = scale * jax.random.normal(key, shape, jnp.float32)
    if cuts:
        entries = entries * levels(key, shape, cuts, -0.22, 0.18)
    return jnp.clip(entries, -limit, limit).astype(held_as)


def setup_inputs(seed: int = 0) -> dict:
    seeds = jax.random.split(jax.random.key(seed), 15)
    inputs = draw_inputs(jax.random.fold_in(seeds[14], 71), 0)
    state = jnp.clip(jax.random.uniform(seeds[1], (N_TILE, N_DATE, FACES, P_SIZE, P_SIZE, C), jnp.float32, -1.0, 1.0) * levels(seeds[1], (N_TILE, N_DATE, FACES, P_SIZE, P_SIZE, C), ((0, 128), (1, 4)), -0.4, 0.0), -1.0, 1.0).astype(jnp.bfloat16)
    cotangent = bell_draw(seeds[2], (N_TILE, N_DATE, FACES, P_SIZE, P_SIZE, C), 1.0, 6.0, ((0, 128), (1, 4)))
    adjacency = draw_adjacency(jax.random.fold_in(seeds[14], 71), 0)
    taps = bell_draw(seeds[4], (2, 3, C), 3 ** -0.5, 3.5)
    gain = jnp.clip(1.0 + 0.18 * jax.random.normal(seeds[5], (C,), jnp.float32), 0.099609375, 1.8984375).astype(jnp.bfloat16)
    w_up = bell_draw(seeds[6], (C, FF), C ** -0.5, 0.4375)
    b_up = bell_draw(seeds[7], (FF,), 0.5, 3.0)
    w_down = bell_draw(seeds[8], (FF, C), FF ** -0.5, 0.21875)
    b_down = bell_draw(seeds[9], (C,), 0.5, 3.0)
    w_gates = bell_draw(seeds[10], (2 * C, 2 * C), (2 * C) ** -0.5, 0.3125)
    b_gates = bell_draw(seeds[11], (2 * C,), 0.5, 3.0)
    w_cand = bell_draw(seeds[12], (2 * C, C), (2 * C) ** -0.5, 0.3125)
    b_cand = bell_draw(seeds[13], (C,), 0.5, 3.0)
    return {"inputs": inputs, "state": state, "cotangent": cotangent, "adjacency": adjacency, "taps": taps, "gain": gain, "w_up": w_up, "b_up": b_up, "w_down": w_down, "b_down": b_down, "w_gates": w_gates, "b_gates": b_gates, "w_cand": w_cand, "b_cand": b_cand}


EPSILON = 1e-06

def border_lines(grid_field):
    return jnp.stack([grid_field[:, 0], grid_field[:, :, -1], grid_field[:, -1], grid_field[:, :, 0]], axis=1)

def beside(grid_field, adjacency, edge_number):
    edge_lines = border_lines(grid_field)
    return edge_lines[adjacency[:, edge_number, 0], adjacency[:, edge_number, 1]]

def along_columns(grid_field, taps_row, adjacency):
    padded = jnp.concatenate([beside(grid_field, adjacency, 3)[:, :, None], grid_field, beside(grid_field, adjacency, 1)[:, :, None]], axis=2)
    extent = grid_field.shape[2]
    return taps_row[0] * padded[:, :, 0:extent] + taps_row[1] * padded[:, :, 1:extent + 1] + taps_row[2] * padded[:, :, 2:extent + 2]

def along_rows(grid_field, taps_row, adjacency):
    padded = jnp.concatenate([beside(grid_field, adjacency, 0)[:, None], grid_field, beside(grid_field, adjacency, 2)[:, None]], axis=1)
    extent = grid_field.shape[1]
    return taps_row[0] * padded[:, 0:extent] + taps_row[1] * padded[:, 1:extent + 1] + taps_row[2] * padded[:, 2:extent + 2]

def normalize(values):
    average = lax.optimization_barrier(jnp.mean(values, axis=-1, keepdims=True))
    centred = values - average
    inv_scale = lax.rsqrt(lax.optimization_barrier(jnp.mean(centred * centred, axis=-1, keepdims=True)) + EPSILON)
    return (centred * inv_scale, inv_scale)

def normalize_back(d_standard, standard, inv_scale):
    first_mean = lax.optimization_barrier(jnp.mean(d_standard, axis=-1, keepdims=True))
    second_mean = lax.optimization_barrier(jnp.mean(d_standard * standard, axis=-1, keepdims=True))
    return inv_scale * (d_standard - first_mean - standard * second_mean)

def cell_step(inputs_rows, state_rows, cot_rows, second, gain, w_up, b_up, w_down, b_down, w_gates, b_gates, w_cand, b_cand):
    channels = inputs_rows.shape[1]
    standard, inv_scale = normalize(second)
    normed = (standard * gain.astype(jnp.float32)).astype(jnp.bfloat16)
    pre_up = jnp.dot(normed, w_up, preferred_element_type=jnp.float32) + b_up.astype(jnp.float32)
    hidden = jax.nn.gelu(pre_up).astype(jnp.bfloat16)
    mixed_out = (inputs_rows.astype(jnp.float32) + jnp.dot(hidden, w_down, preferred_element_type=jnp.float32) + b_down.astype(jnp.float32)).astype(jnp.bfloat16)
    joined = jnp.concatenate([mixed_out, state_rows], axis=1)
    gate_pre = jnp.dot(joined, w_gates, preferred_element_type=jnp.float32) + b_gates.astype(jnp.float32)
    update = jax.nn.sigmoid(gate_pre[:, :channels])
    reset_gate = jax.nn.sigmoid(gate_pre[:, channels:])
    prior_state = state_rows.astype(jnp.float32)
    reset_state = (reset_gate * prior_state).astype(jnp.bfloat16)
    joined_reset = jnp.concatenate([mixed_out, reset_state], axis=1)
    candidate = jnp.tanh(jnp.dot(joined_reset, w_cand, preferred_element_type=jnp.float32) + b_cand.astype(jnp.float32))
    new_state = lax.optimization_barrier(((1.0 - update) * candidate + update * prior_state).astype(jnp.bfloat16))
    upstream = cot_rows.astype(jnp.float32)
    d_cand = (upstream * (1.0 - update) * (1.0 - candidate * candidate)).astype(jnp.bfloat16)
    d_joined_reset = jnp.dot(d_cand, w_cand.T, preferred_element_type=jnp.float32)
    d_update = upstream * (prior_state - candidate) * update * (1.0 - update)
    d_reset = d_joined_reset[:, channels:] * prior_state * reset_gate * (1.0 - reset_gate)
    d_gate = jnp.concatenate([d_update, d_reset], axis=1).astype(jnp.bfloat16)
    d_joined = jnp.dot(d_gate, w_gates.T, preferred_element_type=jnp.float32)
    d_mixed = lax.optimization_barrier((d_joined_reset[:, :channels] + d_joined[:, :channels]).astype(jnp.bfloat16))
    d_hidden = jnp.dot(d_mixed, w_down.T, preferred_element_type=jnp.float32)
    gelu_back = jax.vjp(jax.nn.gelu, pre_up)[1]
    d_pre_up = gelu_back(d_hidden)[0].astype(jnp.bfloat16)
    d_normed = jnp.dot(d_pre_up, w_up.T, preferred_element_type=jnp.float32)
    d_second = lax.optimization_barrier(normalize_back(d_normed * gain.astype(jnp.float32), standard, inv_scale).astype(jnp.bfloat16))
    grad_sums = (lax.optimization_barrier(jnp.sum(d_normed * standard, axis=0)), jnp.dot(normed.T, d_pre_up, preferred_element_type=jnp.float32), lax.optimization_barrier(jnp.sum(d_pre_up.astype(jnp.float32), axis=0)), jnp.dot(hidden.T, d_mixed, preferred_element_type=jnp.float32), lax.optimization_barrier(jnp.sum(d_mixed.astype(jnp.float32), axis=0)), jnp.dot(joined.T, d_gate, preferred_element_type=jnp.float32), lax.optimization_barrier(jnp.sum(d_gate.astype(jnp.float32), axis=0)), jnp.dot(joined_reset.T, d_cand, preferred_element_type=jnp.float32), lax.optimization_barrier(jnp.sum(d_cand.astype(jnp.float32), axis=0)))
    return (new_state, d_mixed, d_second, grad_sums)

def assemble(block):
    grid = block.reshape(Q, Q, 2, N_DATE, FACES, P_SIZE, P_SIZE, C)
    grid = jnp.transpose(grid, (3, 2, 4, 0, 5, 1, 6, 7))
    return grid.reshape(2 * N_DATE, FACES, F, F, C)

def disassemble(whole_field):
    grid = whole_field.reshape(N_DATE, 2, FACES, Q, P_SIZE, Q, P_SIZE, C)
    grid = jnp.transpose(grid, (3, 5, 1, 0, 2, 4, 6, 7))
    return grid.reshape(N_TILE, N_DATE, FACES, P_SIZE, P_SIZE, C)

def reference(inputs, state, cotangent, adjacency, taps, gain, w_up, b_up, w_down, b_down, w_gates, b_gates, w_cand, b_cand):
    taps_f = taps.astype(jnp.float32)

    def one_date(carry, sample):
        sample_in, sample_state, sample_cot = sample
        input_f = sample_in.astype(jnp.float32)
        first_pass = lax.optimization_barrier(along_columns(input_f, taps_f[0], adjacency).astype(jnp.bfloat16))
        second_pass, rows_back = jax.vjp(lambda grid_field, taps_row: along_rows(grid_field, taps_row, adjacency), first_pass.astype(jnp.float32), taps_f[1])
        new_rows, d_mixed, d_second, grad_sums = cell_step(sample_in.reshape(-1, C), sample_state.reshape(-1, C), sample_cot.reshape(-1, C), second_pass.reshape(-1, C), gain, w_up, b_up, w_down, b_down, w_gates, b_gates, w_cand, b_cand)
        d_first, grad_rows = rows_back(d_second.reshape(second_pass.shape).astype(jnp.float32))
        d_first_round = lax.optimization_barrier(d_first.astype(jnp.bfloat16))
        columns_back = jax.vjp(lambda grid_field, taps_row: along_columns(grid_field, taps_row, adjacency), input_f, taps_f[0])[1]
        d_input, grad_cols = columns_back(d_first_round.astype(jnp.float32))
        grad_input = (d_input + d_mixed.reshape(d_input.shape).astype(jnp.float32)).astype(jnp.bfloat16)
        totals = (jnp.stack([grad_cols, grad_rows]),) + grad_sums
        carry = tuple((running + extra for running, extra in zip(carry, totals)))
        return (carry, (new_rows.reshape(sample_in.shape), grad_input))
    start = (jnp.zeros((2, 3, C), jnp.float32), jnp.zeros((C,), jnp.float32), jnp.zeros((C, FF), jnp.float32), jnp.zeros((FF,), jnp.float32), jnp.zeros((FF, C), jnp.float32), jnp.zeros((C,), jnp.float32), jnp.zeros((2 * C, 2 * C), jnp.float32), jnp.zeros((2 * C,), jnp.float32), jnp.zeros((2 * C, C), jnp.float32), jnp.zeros((C,), jnp.float32))
    summed, outputs = lax.scan(one_date, start, (assemble(inputs), assemble(state), assemble(cotangent)))
    norm_factor = PIXELS ** (-0.5)
    finished = tuple(((grad_piece * norm_factor).astype(jnp.bfloat16) for grad_piece in summed))
    return (disassemble(outputs[0]), disassemble(outputs[1]), finished[0], finished[1], finished[2], finished[3], finished[4], finished[5], finished[6], finished[7], finished[8], finished[9])
```

```python
import functools
import math

import jax
import jax.numpy as jnp
from jax import lax
from jax.experimental import pallas as pl
from jax.experimental.pallas import tpu as pltpu
from jax.sharding import PartitionSpec as P

EPSILON = 1e-06
MESH = pl.DeviceIdType.MESH
F32 = jnp.float32
BF16 = jnp.bfloat16
FACES = 12
SIDE = 8
HALF = 128
X_PART, Y_PART, Z_PART = 64, 32, 32
FIRST_ROW, LAST_ROW, FIRST_COL, LAST_COL = range(4)
GELU_A = math.sqrt(2.0 / math.pi)
GELU_B = 0.044715
ROW_BUP, ROW_BGATES, ROW_TAPS, ROW_GAIN, ROW_BDOWN, ROW_BCAND = 0, 1, 2, 8, 9, 10
SMALL_ROWS = ((0, 6), (1, 3)) + tuple((row, 2) for row in range(2, 11))
CAND_AT, GATES_AT, DOWN_AT, UP_AT, SMALL_AT = 0, 36, 108, 180, 252


def nn(left, right):
    return jnp.dot(left, right, preferred_element_type=F32)


def nt(left, right):
    return lax.dot_general(left, right, (((1,), (1,)), ((), ())), preferred_element_type=F32)


def tn(left, right):
    return lax.dot_general(left, right, (((0,), (0,)), ((), ())), preferred_element_type=F32)


def sigmoid(value):
    return 0.5 + 0.5 * jnp.tanh(0.5 * value)


def store_tiles(slab, at, matrix):
    rows, columns = matrix.shape
    packed = matrix.astype(BF16)
    across = columns // 128
    for row in range(rows // 16):
        for column in range(across):
            slab[at + row * across + column] = packed[
                row * 16 : row * 16 + 16, column * 128 : column * 128 + 128
            ]


def level_kernel(
    side,
    x_low,
    norm_factor,
    adj,
    x_ref,
    h_ref,
    g_ref,
    par,
    w_up,
    w_down_t,
    w_gates,
    w_cand_t,
    ns_out,
    gi_out,
    slab_out,
    snd,
    rcv,
    pool,
    halo,
    field,
    second,
    wg_u,
    wg_r,
    wc_m,
    wc_r,
    normed_s,
    hid_s,
    d_pre_s,
    d_mix_s,
    d_gate_s,
    joined_s,
    d_cand_s,
    d_sec_s,
    small,
    tile32,
    slab,
    core_rcv,
    t1,
    x_rcv,
    y_rcv,
    z_rcv,
    t2,
    b0_rcv,
    b1_rcv,
    b2_rcv,
    b3_rcv,
    cz,
    cy,
    gathered,
    halo_send,
    halo_recv,
    red_send,
    red_recv,
):
    channels = x_ref.shape[1]
    nx = 2 * x_low
    unit = 32 // (nx * side)
    tile = lax.axis_index("tile")
    date = lax.axis_index("date")
    ty, tx = tile // 2 // side, tile // 2 % side
    core = date % 2
    mx = (tile % 2) * x_low + date // 2

    def device(x, y, z, c):
        return ((y * side + z) * 2 + x // x_low, (x % x_low) * 2 + c)

    def along(axis, steps):
        if axis == "x":
            return device((mx + steps) % nx, ty, tx, core)
        if axis == "y":
            return device(mx, (ty + steps) % side, tx, core)
        return device(mx, ty, (tx + steps) % side, core)

    sibling = device(mx, ty, tx, 1 - core)
    across = device(mx, tx, ty, core)
    top, bottom = ty == 0, ty == side - 1
    west, east = tx == 0, tx == side - 1
    has_across = jnp.logical_and(
        ty != tx,
        jnp.logical_or(jnp.logical_or(top, bottom), jnp.logical_or(west, east)),
    )

    barrier = pltpu.get_barrier_semaphore()
    peers = [sibling]
    peers += [along("x", step) for step in range(1, nx)]
    peers += [along("y", step) for step in range(1, side)]
    peers += [along("z", step) for step in range(1, side)]
    for peer in peers:
        pl.semaphore_signal(barrier, inc=1, device_id=peer, device_id_type=MESH)

    @pl.when(has_across)
    def _():
        pl.semaphore_signal(barrier, inc=1, device_id=across, device_id_type=MESH)

    pool[...] = jnp.zeros_like(pool)
    small[...] = jnp.zeros_like(small)
    slab[SMALL_AT + 2] = jnp.zeros((16, 128), BF16)
    slab[SMALL_AT + 3] = jnp.zeros((16, 128), BF16)
    wg_u[...] = w_gates[:, :channels]
    wg_r[...] = w_gates[:, channels:]
    wc_m[...] = w_cand_t[:, :channels]
    wc_r[...] = w_cand_t[:, channels:]

    def tap(axis, number):
        row = ROW_TAPS + 3 * axis + number
        return par[row : row + 1, :channels].reshape(1, 1, channels)

    def block(ref, b):
        rows = pl.ds(pl.multiple_of(b * 128, 128), 128)
        return ref[rows, :].astype(F32).reshape(16, 8, channels)

    def put_lines(exchange, b, value, kinds):
        rows = pl.ds(pl.multiple_of(b * 16, 16), 16)
        faces = value.reshape(2, 8, 8, channels)
        for kind in kinds:
            if kind == FIRST_ROW:
                line = faces[:, 0].reshape(16, channels)
            elif kind == LAST_ROW:
                line = faces[:, 7].reshape(16, channels)
            elif kind == FIRST_COL:
                line = value[:, 0, :]
            else:
                line = value[:, 7, :]
            snd[exchange, kind, rows, :] = line.astype(BF16)

    def x_lines(b, carry):
        put_lines(0, b, block(x_ref, b), range(4))
        return carry

    lax.fori_loop(0, 6, x_lines, 0)

    @pl.when(has_across)
    def _():
        pl.semaphore_wait(barrier, len(peers) + 1)

    @pl.when(jnp.logical_not(has_across))
    def _():
        pl.semaphore_wait(barrier, len(peers))

    def halo_copies(exchange):
        on_columns = exchange in (0, 3)
        rows_turn = exchange in (0, 2)
        axis = "z" if on_columns else "y"
        last, first = (LAST_COL, FIRST_COL) if on_columns else (LAST_ROW, FIRST_ROW)
        t_first, t_last = (FIRST_ROW, LAST_ROW) if rows_turn else (FIRST_COL, LAST_COL)
        row_first = jnp.logical_and(top, jnp.logical_not(west))
        row_last = jnp.logical_and(bottom, jnp.logical_not(east))
        col_first = jnp.logical_and(west, jnp.logical_not(top))
        col_last = jnp.logical_and(east, jnp.logical_not(bottom))
        if rows_turn:
            sends, receives = (row_first, row_last), (col_first, col_last)
        else:
            sends, receives = (col_first, col_last), (row_first, row_last)
        targets = (along(axis, 1), along(axis, -1), across, across)
        return [
            (
                pltpu.make_async_remote_copy(
                    src_ref=snd.at[exchange, line],
                    dst_ref=rcv.at[exchange, kind],
                    send_sem=halo_send.at[exchange, kind],
                    recv_sem=halo_recv.at[exchange, kind],
                    device_id=target,
                    device_id_type=MESH,
                ),
                None if kind < 2 else sends[kind - 2],
                None if kind < 2 else receives[kind - 2],
                line,
            )
            for kind, (line, target) in enumerate(zip((last, first, t_first, t_last), targets))
        ]

    def start_halos(exchange):
        for copy, sends, _, _ in halo_copies(exchange):
            if sends is None:
                copy.start()
            else:
                pl.when(sends)(copy.start)

    def finish_halo_sends(exchange):
        for copy, sends, _, _ in halo_copies(exchange):
            if sends is None:
                copy.wait_send()
            else:
                pl.when(sends)(copy.wait_send)

    def receive_halos(exchange):
        copies = halo_copies(exchange)
        corners = (jnp.logical_and(top, west), jnp.logical_and(bottom, east))

        def spread(ref, at):
            pool[at[0], at[1] : at[1] + 12] = (
                ref[...].astype(F32).reshape(FACES, SIDE, channels)
            )

        for kind, (copy, _, receives, line) in enumerate(copies):
            if kind < 2:
                copy.wait_recv()
                spread(rcv.at[exchange, kind], (kind, 0))
            else:

                @pl.when(receives)
                def _():
                    copy.wait_recv()
                    spread(rcv.at[exchange, kind], (kind - 2, 12))

                @pl.when(corners[kind - 2])
                def _():
                    spread(snd.at[exchange, line], (kind - 2, 12))

    def beside(face, edge):
        return adj[(face * 4 + edge) * 2], adj[(face * 4 + edge) * 2 + 1] != (edge + 2) % 4

    def gather(to, which, edge, on_border, mode):
        def one(face, carry):
            neighbour, turned = beside(face, edge)
            if mode == "both":
                there = jnp.where(turned, 12 + neighbour, neighbour)
                index = jnp.where(on_border, there, face)
            elif mode == "straight":
                index = jnp.where(on_border, jnp.where(turned, 24, neighbour), face)
            else:
                index = jnp.where(jnp.logical_and(on_border, turned), 12 + neighbour, 24)
            halo[to, face] = pool[which, index]
            return carry

        lax.fori_loop(0, FACES, one, 0)

    def halo_lines(which, b):
        return halo[which, pl.ds(2 * b, 2)]

    place = lax.broadcasted_iota(jnp.int32, (16, 8, channels), 1)

    def upright(lines):
        return jnp.broadcast_to(lines.reshape(16, 1, channels), (16, 8, channels))

    def column_shifts(value, lines_west, lines_east):
        left = jnp.where(place == 0, upright(lines_west), pltpu.roll(value, 1, 1))
        right = jnp.where(place == 7, upright(lines_east), pltpu.roll(value, 7, 1))
        return left, right

    def row_shifts(value, lines_north, lines_south):
        faces = value.reshape(2, 8, 8, channels)
        up = jnp.concatenate([lines_north[:, None], faces[:, :7]], axis=1)
        down = jnp.concatenate([faces[:, 1:], lines_south[:, None]], axis=1)
        return up.reshape(16, 8, channels), down.reshape(16, 8, channels)

    def rounded(value):
        return value.astype(BF16).astype(F32)

    def put_block(ref, b, value):
        rows = pl.ds(pl.multiple_of(b * 128, 128), 128)
        ref[rows, :] = value.reshape(128, channels).astype(ref.dtype)

    start_halos(0)
    receive_halos(0)
    gather(0, 0, 3, west, "both")
    gather(1, 1, 1, east, "both")

    def first_pass(b, carry):
        value = block(x_ref, b)
        left, right = column_shifts(value, halo_lines(0, b), halo_lines(1, b))
        first = rounded(tap(0, 0) * left + tap(0, 1) * value + tap(0, 2) * right)
        put_block(field, b, first)
        put_lines(1, b, first, range(4))
        return carry

    lax.fori_loop(0, 6, first_pass, 0)

    start_halos(1)
    receive_halos(1)
    gather(2, 0, 0, top, "both")
    gather(3, 1, 2, bottom, "both")

    def second_pass(b, carry):
        value = block(field, b)
        up, down = row_shifts(value, halo_lines(2, b), halo_lines(3, b))
        put_block(second, b, tap(1, 0) * up + tap(1, 1) * value + tap(1, 2) * down)
        return carry

    lax.fori_loop(0, 6, second_pass, 0)

    def vector(row, start, size):
        return par[row : row + 1, start : start + size]

    def cell(b, sums):
        rows = pl.ds(pl.multiple_of(b * 256, 256), 256)
        gain = vector(ROW_GAIN, 0, channels)
        centred = second[rows, :]
        centred = centred - jnp.mean(centred, axis=-1, keepdims=True)
        inv_scale = lax.rsqrt(jnp.mean(centred * centred, axis=-1, keepdims=True) + EPSILON)
        standard = centred * inv_scale
        normed = (standard * gain).astype(BF16)
        normed_s[rows, :] = normed
        pre = nn(normed, w_up[...]) + vector(ROW_BUP, 0, w_up.shape[1])
        square = pre * pre
        curve = jnp.tanh(GELU_A * pre * (1.0 + GELU_B * square))
        hid = (0.5 * pre * (1.0 + curve)).astype(BF16)
        hid_s[rows, :] = hid
        slope = 0.5 * (1.0 + curve) + (0.5 * GELU_A) * pre * (1.0 - curve * curve) * (
            1.0 + 3.0 * GELU_B * square
        )
        mixed = (
            x_ref[rows, :].astype(F32)
            + nt(hid, w_down_t[...])
            + vector(ROW_BDOWN, 0, channels)
        ).astype(BF16)
        joined_s[rows, :channels] = mixed
        prior_b = h_ref[rows, :]
        prior = prior_b.astype(F32)
        update = sigmoid(
            nn(mixed, wg_u[:channels])
            + nn(prior_b, wg_u[channels:])
            + vector(ROW_BGATES, 0, channels)
        )
        reset = sigmoid(
            nn(mixed, wg_r[:channels])
            + nn(prior_b, wg_r[channels:])
            + vector(ROW_BGATES, channels, channels)
        )
        reset_state = (reset * prior).astype(BF16)
        joined_s[rows, channels:] = reset_state
        candidate = jnp.tanh(
            nt(mixed, wc_m[...])
            + nt(reset_state, wc_r[...])
            + vector(ROW_BCAND, 0, channels)
        )
        ns_out[rows, :] = ((1.0 - update) * candidate + update * prior).astype(BF16)
        upstream = g_ref[rows, :].astype(F32)
        kept = upstream * (1.0 - update)
        d_cand = (kept * (1.0 - candidate * candidate)).astype(BF16)
        d_cand_s[rows, :] = d_cand
        d_update = (kept * (prior - candidate) * update).astype(BF16)
        d_reset = (nn(d_cand, wc_r[...]) * prior * reset * (1.0 - reset)).astype(BF16)
        d_gate_s[rows, :channels] = d_update
        d_gate_s[rows, channels:] = d_reset
        d_mixed = (
            nn(d_cand, wc_m[...])
            + nt(d_update, wg_u[:channels])
            + nt(d_reset, wg_r[:channels])
        ).astype(BF16)
        d_mix_s[rows, :] = d_mixed
        d_pre = (nn(d_mixed, w_down_t[...]) * slope).astype(BF16)
        d_pre_s[rows, :] = d_pre
        d_normed = nt(d_pre, w_up[...])
        d_standard = d_normed * gain
        d_second = inv_scale * (
            d_standard
            - jnp.mean(d_standard, axis=-1, keepdims=True)
            - standard * jnp.mean(d_standard * standard, axis=-1, keepdims=True)
        )
        d_sec_s[rows, :] = d_second.astype(BF16)

        def total(value):
            return jnp.sum(value.astype(F32), axis=0, keepdims=True)

        extras = (
            total(d_pre),
            total(d_update),
            total(d_reset),
            total(d_normed * standard),
            total(d_mixed),
            total(d_cand),
        )
        return tuple(old + new for old, new in zip(sums, extras))

    zeros = jnp.zeros((1, channels), F32)
    sums = lax.fori_loop(
        0,
        3,
        cell,
        (jnp.zeros((1, w_up.shape[1]), F32), zeros, zeros, zeros, zeros, zeros),
    )
    small[ROW_BUP : ROW_BUP + 1, :] = sums[0]
    small[ROW_BGATES : ROW_BGATES + 1, :channels] = sums[1]
    small[ROW_BGATES : ROW_BGATES + 1, channels : 2 * channels] = sums[2]
    small[ROW_GAIN : ROW_GAIN + 1, :channels] = sums[3]
    small[ROW_BDOWN : ROW_BDOWN + 1, :channels] = sums[4]
    small[ROW_BCAND : ROW_BCAND + 1, :channels] = sums[5]

    def second_lines(b, carry):
        put_lines(2, b, block(d_sec_s, b), (FIRST_ROW, LAST_ROW))
        return carry

    lax.fori_loop(0, 6, second_lines, 0)
    start_halos(2)

    store_tiles(slab, CAND_AT, tn(d_cand_s[...], joined_s[...]))
    store_tiles(slab, GATES_AT, tn(joined_s[:, :channels], d_gate_s[...]))
    store_tiles(slab, GATES_AT + 36, tn(h_ref[...], d_gate_s[...]))
    store_tiles(slab, DOWN_AT, tn(d_mix_s[...], hid_s[...]))
    store_tiles(slab, UP_AT, tn(normed_s[...], d_pre_s[...]))

    regions = ((0, X_PART), (X_PART, Y_PART), (X_PART + Y_PART, Z_PART))

    def remote(src, dst, stage, target):
        return pltpu.make_async_remote_copy(
            src_ref=src,
            dst_ref=dst,
            send_sem=red_send.at[stage],
            recv_sem=red_recv.at[stage],
            device_id=target,
            device_id_type=MESH,
        )

    def core_copy(number):
        at, size = regions[number]
        return remote(
            slab.at[pl.ds((1 - core) * HALF + at, size)],
            core_rcv.at[pl.ds(at, size)],
            number,
            sibling,
        )

    core_copy(0).start()
    core_copy(1).start()

    receive_halos(2)
    gather(4, 0, 0, top, "straight")
    gather(5, 1, 2, bottom, "straight")
    gather(6, 0, 3, west, "turned")
    gather(7, 1, 1, east, "turned")

    def first_back(b, sums):
        value = block(d_sec_s, b)
        up, down = row_shifts(value, halo_lines(4, b), halo_lines(5, b))
        d_first = tap(1, 0) * down + tap(1, 1) * value + tap(1, 2) * up
        d_first += jnp.where(place == 0, tap(1, 0) * upright(halo_lines(6, b)), 0.0)
        d_first += jnp.where(place == 7, tap(1, 2) * upright(halo_lines(7, b)), 0.0)
        first = block(field, b)
        above, below = row_shifts(first, halo_lines(2, b), halo_lines(3, b))
        d_first = rounded(d_first)
        put_lines(3, b, d_first, (FIRST_COL, LAST_COL))
        put_block(second, b, d_first)
        x_value = block(x_ref, b)
        left, right = column_shifts(x_value, halo_lines(0, b), halo_lines(1, b))
        pairs = (
            (d_first, left),
            (d_first, x_value),
            (d_first, right),
            (value, above),
            (value, first),
            (value, below),
        )
        return tuple(old + jnp.sum(a * c, axis=0) for old, (a, c) in zip(sums, pairs))

    tap_sums = lax.fori_loop(0, 6, first_back, tuple(jnp.zeros((8, channels), F32) for _ in range(6)))
    start_halos(3)
    for number, tap_sum in enumerate(tap_sums):
        row = ROW_TAPS + number
        small[row : row + 1, :channels] = jnp.sum(tap_sum, axis=0, keepdims=True)
    tile32[...] = jnp.zeros_like(tile32)
    line = 0
    for row, count in SMALL_ROWS:
        for number in range(count):
            tile32[line : line + 1, :] = small[row : row + 1, number * 128 : number * 128 + 128]
            line += 1
    slab[SMALL_AT] = tile32[:16].astype(BF16)
    slab[SMALL_AT + 1] = tile32[16:].astype(BF16)
    core_copy(2).start()

    def add_cores(number):
        at, size = regions[number]
        core_copy(number).wait_recv()

        def some(step, carry):
            here = at + step * 8
            total = slab[pl.ds(core * HALF + here, 8)].astype(F32)
            t1[pl.ds(here, 8)] = (total + core_rcv[pl.ds(here, 8)].astype(F32)).astype(BF16)
            return carry

        lax.fori_loop(0, size // 8, some, 0)

    def scatter(source, base, chunk, received, axis, count, me, stage):
        for step in range(1, count):
            to = (me + step) % count
            remote(
                source.at[pl.ds(base + to * chunk, chunk)],
                received.at[step - 1],
                stage,
                along(axis, step),
            ).start()

    def whole_wait(ref, sem):
        pltpu.make_async_copy(ref, ref, sem).wait()

    def add_all(source, at, received, target, to, stage):
        whole_wait(received, red_recv.at[stage])
        chunk = received.shape[1]
        total = source[pl.ds(at, chunk)].astype(F32)
        for number in range(received.shape[0]):
            total += received[number].astype(F32)
        target[pl.ds(to, chunk)] = total.astype(BF16)

    x_chunk, y_chunk, z_chunk = X_PART // nx, Y_PART // side, Z_PART // side
    add_cores(0)
    scatter(t1, 0, x_chunk, x_rcv, "x", nx, mx, 3)
    add_cores(1)
    scatter(t1, X_PART, y_chunk, y_rcv, "y", side, ty, 4)
    add_cores(2)
    scatter(t1, X_PART + Y_PART, z_chunk, z_rcv, "z", side, tx, 5)

    receive_halos(3)
    gather(4, 0, 3, west, "straight")
    gather(5, 1, 1, east, "straight")
    gather(6, 0, 0, top, "turned")
    gather(7, 1, 2, bottom, "turned")

    def input_back(b, carry):
        value = block(second, b)
        left, right = column_shifts(value, halo_lines(4, b), halo_lines(5, b))
        d_input = tap(0, 0) * right + tap(0, 1) * value + tap(0, 2) * left
        faces = d_input.reshape(2, 8, 8, channels)
        inner = faces[:, 1:7]
        north = faces[:, :1] + (tap(0, 0) * halo_lines(6, b))[:, None]
        south = faces[:, 7:] + (tap(0, 2) * halo_lines(7, b))[:, None]
        d_input = jnp.concatenate([north, inner, south], axis=1).reshape(16, 8, channels)
        put_block(gi_out, b, d_input + block(d_mix_s, b))
        return carry

    lax.fori_loop(0, 6, input_back, 0)

    y_at = x_chunk
    z_at = x_chunk + y_chunk
    half = x_chunk // 2
    add_all(t1, X_PART + ty * y_chunk, y_rcv, t2, y_at, 4)
    scatter(t2, y_at, unit, b2_rcv, "x", nx, mx, 8)
    add_all(t1, X_PART + Y_PART + tx * z_chunk, z_rcv, t2, z_at, 5)
    scatter(t2, z_at, unit, b3_rcv, "x", nx, mx, 9)
    add_all(t1, mx * x_chunk, x_rcv, t2, 0, 3)
    scatter(t2, 0, unit, b0_rcv, "y", side, ty, 6)
    scatter(t2, half, unit, b1_rcv, "z", side, tx, 7)

    def to_slot(source, at, received, slots, slot, piece, stage):
        whole_wait(received, red_recv.at[stage])
        total = source[pl.ds(at, unit)].astype(F32)
        for number in range(received.shape[0]):
            total += received[number].astype(F32)
        slots[slot, pl.ds(piece * unit, unit)] = total.astype(BF16)

    def spread_slot(slots, me, axis, stage):
        for step in range(1, side):
            remote(slots.at[me], slots.at[me], stage, along(axis, step)).start()

    to_slot(t2, y_at + mx * unit, b2_rcv, cz, tx, 1, 8)
    to_slot(t2, z_at + mx * unit, b3_rcv, cy, ty, 1, 9)
    to_slot(t2, ty * unit, b0_rcv, cz, tx, 0, 6)
    spread_slot(cz, tx, "z", 10)
    to_slot(t2, half + tx * unit, b1_rcv, cy, ty, 0, 7)
    spread_slot(cy, ty, "y", 11)

    base = core * HALF

    def sum_slots(slots, stage):
        whole_wait(slots.at[pl.ds(0, side - 1)], red_recv.at[stage])
        total = slots[0].astype(F32)
        for number in range(1, side):
            total += slots[number].astype(F32)
        return (total * norm_factor).astype(BF16)

    def share(at, size, axis, count, stage):
        piece = gathered.at[pl.ds(at, size)]
        for step in range(1, count):
            remote(piece, piece, stage, along(axis, step)).start()

    def await_shares(size, count, stage):
        whole_wait(gathered.at[pl.ds(0, size * (count - 1))], red_recv.at[stage])

    at0 = base + mx * x_chunk + ty * unit
    at1 = base + mx * x_chunk + half + tx * unit
    at2 = base + X_PART + ty * y_chunk + mx * unit
    at3 = base + X_PART + Y_PART + tx * z_chunk + mx * unit
    done = sum_slots(cz, 10)
    gathered[pl.ds(at0, unit)] = done[:unit]
    gathered[pl.ds(at2, unit)] = done[unit:]
    share(at0, unit, "y", side, 12)
    share(at2, unit, "x", nx, 14)
    done = sum_slots(cy, 11)
    gathered[pl.ds(at1, unit)] = done[:unit]
    gathered[pl.ds(at3, unit)] = done[unit:]
    share(at1, unit, "z", side, 13)
    share(at3, unit, "x", nx, 15)
    await_shares(unit, nx, 14)
    share(base + X_PART + ty * y_chunk, y_chunk, "y", side, 17)
    await_shares(unit, side, 12)
    await_shares(unit, side, 13)
    share(base + mx * x_chunk, x_chunk, "x", nx, 16)
    await_shares(unit, nx, 15)
    share(base + X_PART + Y_PART + tx * z_chunk, z_chunk, "z", side, 18)

    def core_back(number):
        at, size = regions[number]
        piece = gathered.at[pl.ds(base + at, size)]
        return remote(piece, piece, 19 + number, sibling)

    await_shares(x_chunk, nx, 16)
    core_back(0).start()
    await_shares(y_chunk, side, 17)
    core_back(1).start()
    await_shares(z_chunk, side, 18)
    core_back(2).start()
    for number in range(3):
        core_back(number).wait_recv()

    slab_out[...] = gathered[...]

    for exchange in range(4):
        finish_halo_sends(exchange)
    for number in range(3):
        core_copy(number).wait_send()
        core_back(number).wait_send()
    for ref, stage in (
        (x_rcv, 3),
        (y_rcv, 4),
        (z_rcv, 5),
        (b0_rcv, 6),
        (b1_rcv, 7),
        (b2_rcv, 8),
        (b3_rcv, 9),
        (cz.at[pl.ds(0, side - 1)], 10),
        (cy.at[pl.ds(0, side - 1)], 11),
        (gathered.at[pl.ds(0, unit * (side - 1))], 12),
        (gathered.at[pl.ds(0, unit * (side - 1))], 13),
        (gathered.at[pl.ds(0, unit * (nx - 1))], 14),
        (gathered.at[pl.ds(0, unit * (nx - 1))], 15),
        (gathered.at[pl.ds(0, x_chunk * (nx - 1))], 16),
        (gathered.at[pl.ds(0, y_chunk * (side - 1))], 17),
        (gathered.at[pl.ds(0, z_chunk * (side - 1))], 18),
    ):
        whole_wait(ref, red_send.at[stage])


def unpack_kernel(ns, gi, slab, ns_out, gi_out, up_out, down_out, gates_out, cand_out, small_out):
    ns_out[...] = ns[...]
    gi_out[...] = gi[...]

    def unpack(at, out, row_at, rows):
        across = out.shape[1] // 128
        for row in range(rows // 16):
            for column in range(across):
                out[
                    row_at + row * 16 : row_at + row * 16 + 16, column * 128 : column * 128 + 128
                ] = slab[at + row * across + column]

    unpack(CAND_AT, cand_out, 0, cand_out.shape[0])
    unpack(GATES_AT, gates_out, 0, gates_out.shape[0])
    unpack(DOWN_AT, down_out, 0, down_out.shape[0])
    unpack(UP_AT, up_out, 0, up_out.shape[0])
    small_out[:16, :] = slab[SMALL_AT]
    small_out[16:, :] = slab[SMALL_AT + 1]


def on_device(
    inputs,
    state,
    cotangent,
    adjacency,
    taps,
    gain,
    w_up,
    b_up,
    w_down,
    b_down,
    w_gates,
    b_gates,
    w_cand,
    b_cand,
):
    channels = inputs.shape[-1]
    wide = w_up.shape[1]
    tokens = FACES * SIDE * SIDE
    tile_count, date_count = lax.axis_size("tile"), lax.axis_size("date")
    side = 2 ** ((tile_count.bit_length() - 2) // 2)
    x_low = date_count // 2
    nx = 2 * x_low
    unit = 32 // (nx * side)
    norm_factor = float(tokens * tile_count * date_count) ** (-0.5)

    def row(value):
        return jnp.pad(value.astype(F32), (0, wide - value.shape[0]))

    par = jnp.stack(
        [row(b_up), row(b_gates)]
        + [row(taps[axis, number]) for axis in range(2) for number in range(3)]
        + [row(gain), row(b_down), row(b_cand)]
        + [jnp.zeros((wide,), F32)] * 5
    )
    vmem = pl.BlockSpec(memory_space=pltpu.VMEM)

    def buf(*shape):
        return pltpu.VMEM(shape, BF16)

    new_rows, grad_rows, slab = pl.pallas_call(
        functools.partial(level_kernel, side, x_low, norm_factor),
        name="level",
        out_shape=(
            jax.ShapeDtypeStruct((tokens, channels), BF16),
            jax.ShapeDtypeStruct((tokens, channels), BF16),
            jax.ShapeDtypeStruct((2 * HALF, 16, 128), BF16),
        ),
        in_specs=[pl.BlockSpec(memory_space=pltpu.SMEM)] + [vmem] * 8,
        out_specs=[vmem] * 3,
        scratch_shapes=[
            buf(4, 4, FACES * SIDE, channels),
            buf(4, 4, FACES * SIDE, channels),
            pltpu.VMEM((2, 25, SIDE, channels), F32),
            pltpu.VMEM((8, FACES, SIDE, channels), F32),
            pltpu.VMEM((tokens, channels), F32),
            pltpu.VMEM((tokens, channels), F32),
            buf(2 * channels, channels),
            buf(2 * channels, channels),
            buf(channels, channels),
            buf(channels, channels),
            buf(tokens, channels),
            buf(tokens, wide),
            buf(tokens, wide),
            buf(tokens, channels),
            buf(tokens, 2 * channels),
            buf(tokens, 2 * channels),
            buf(tokens, channels),
            buf(tokens, channels),
            pltpu.VMEM((16, wide), F32),
            pltpu.VMEM((32, 128), F32),
            buf(2 * HALF, 16, 128),
            buf(HALF, 16, 128),
            buf(HALF, 16, 128),
            buf(nx - 1, X_PART // nx, 16, 128),
            buf(side - 1, Y_PART // side, 16, 128),
            buf(side - 1, Z_PART // side, 16, 128),
            buf(X_PART // nx + Y_PART // side + Z_PART // side, 16, 128),
            buf(side - 1, unit, 16, 128),
            buf(side - 1, unit, 16, 128),
            buf(nx - 1, unit, 16, 128),
            buf(nx - 1, unit, 16, 128),
            buf(side, 2 * unit, 16, 128),
            buf(side, 2 * unit, 16, 128),
            buf(2 * HALF, 16, 128),
            pltpu.SemaphoreType.DMA((4, 4)),
            pltpu.SemaphoreType.DMA((4, 4)),
            pltpu.SemaphoreType.DMA((22,)),
            pltpu.SemaphoreType.DMA((22,)),
        ],
        compiler_params=pltpu.CompilerParams(
            collective_id=0, has_side_effects=True, vmem_limit_bytes=48 * 2**20
        ),
    )(
        adjacency.reshape(-1),
        inputs.reshape(tokens, channels),
        state.reshape(tokens, channels),
        cotangent.reshape(tokens, channels),
        par,
        w_up,
        w_down.T,
        w_gates,
        w_cand.T,
    )
    new_rows, grad_rows, g_up, g_down, g_gates, g_cand, g_small = pl.pallas_call(
        unpack_kernel,
        name="unpack",
        out_shape=(
            jax.ShapeDtypeStruct((tokens, channels), BF16),
            jax.ShapeDtypeStruct((tokens, channels), BF16),
            jax.ShapeDtypeStruct((channels, wide), BF16),
            jax.ShapeDtypeStruct((channels, wide), BF16),
            jax.ShapeDtypeStruct((2 * channels, 2 * channels), BF16),
            jax.ShapeDtypeStruct((channels, 2 * channels), BF16),
            jax.ShapeDtypeStruct((32, 128), BF16),
        ),
        in_specs=[vmem] * 3,
        out_specs=[vmem] * 7,
        compiler_params=pltpu.CompilerParams(vmem_limit_bytes=32 * 2**20),
    )(new_rows, grad_rows, slab)

    flat = g_small.reshape(-1)

    def piece(line, size):
        return flat[line * 128 : line * 128 + size]

    g_taps = g_small[9:21].reshape(2, 3, 256)[:, :, :channels]
    return (
        new_rows.reshape(inputs.shape),
        grad_rows.reshape(inputs.shape),
        g_taps,
        piece(21, channels),
        g_up,
        piece(0, wide),
        g_down.T,
        piece(23, channels),
        g_gates,
        piece(6, 2 * channels),
        g_cand.T,
        piece(25, channels),
    )


def solution(mesh):
    field = P("tile", "date", None, None, None, None)
    return jax.shard_map(
        on_device,
        mesh=mesh,
        in_specs=(field,) * 3 + (P(),) * 11,
        out_specs=(field,) * 2 + (P(),) * 10,
        check_vma=False,
    )
```

```python
import functools
import math

import jax
import jax.numpy as jnp
from jax import lax
from jax.experimental import pallas as pl
from jax.experimental.pallas import tpu as pltpu
from jax.sharding import PartitionSpec as P

EPSILON = 1e-06
MESH = pl.DeviceIdType.MESH
F32 = jnp.float32
BF16 = jnp.bfloat16
FACES = 12
SIDE = 8
HALF = 128
REGION = 64
FIRST_ROW, LAST_ROW, FIRST_COL, LAST_COL = range(4)
GELU_A = math.sqrt(2.0 / math.pi)
GELU_B = 0.044715
ROW_BUP, ROW_BGATES, ROW_TAPS, ROW_GAIN, ROW_BDOWN, ROW_BCAND = 0, 1, 2, 8, 9, 10
SMALL_ROWS = ((0, 6), (1, 3)) + tuple((row, 2) for row in range(2, 11))
CAND_AT, GATES_AT, DOWN_AT, UP_AT, SMALL_AT = 0, 36, 108, 180, 252


def nn(left, right):
    return jnp.dot(left, right, preferred_element_type=F32)


def nt(left, right):
    return lax.dot_general(left, right, (((1,), (1,)), ((), ())), preferred_element_type=F32)


def tn(left, right):
    return lax.dot_general(left, right, (((0,), (0,)), ((), ())), preferred_element_type=F32)


def sigmoid(value):
    return 0.5 + 0.5 * jnp.tanh(0.5 * value)


def tile_place(number):
    if 64 <= number < 128:
        return number + 64
    if 128 <= number < 192:
        return number - 64
    return number


def store_tiles(slab, at, matrix):
    rows, columns = matrix.shape
    packed = matrix.astype(BF16)
    across = columns // 128
    for row in range(rows // 16):
        for column in range(across):
            slab[tile_place(at + row * across + column)] = packed[
                row * 16 : row * 16 + 16, column * 128 : column * 128 + 128
            ]


def level_kernel(
    side,
    x_low,
    norm_factor,
    adj_in,
    x_in,
    h_in,
    g_in,
    taps_in,
    gain_in,
    b_up_in,
    b_down_in,
    b_gates_in,
    b_cand_in,
    w_up_in,
    w_down_in,
    w_gates_in,
    w_cand_in,
    ns_out,
    gi_out,
    slab_out,
    small_out,
    adj,
    x_ref,
    h_ref,
    g_ref,
    taps_ref,
    gain_ref,
    b_up_ref,
    b_down_ref,
    b_gates_ref,
    b_cand_ref,
    w_up,
    w_down_t,
    w_gates,
    w_cand_t,
    par,
    snd,
    rcv,
    pool,
    halo,
    columns,
    field,
    d_sec,
    d_first_s,
    wg_u,
    wg_r,
    wc_m,
    wc_r,
    prior_s,
    normed_s,
    hid_s,
    d_pre_s,
    d_mix_s,
    d_gate_s,
    joined_s,
    d_cand_s,
    small,
    tile32,
    small_c,
    small_x,
    small_y,
    small_z,
    slab,
    core_rcv,
    t1,
    xy_rcv,
    xz_rcv,
    cz,
    cy,
    gathered,
    load_sem,
    halo_send,
    halo_recv,
    red_send,
    red_recv,
):
    channels = x_ref.shape[3]
    nx = 2 * x_low
    unit = REGION // (nx * side)
    tile = lax.axis_index("tile")
    date = lax.axis_index("date")
    place_of_tile = lax.div(tile, 2)
    ty, tx = lax.div(place_of_tile, side), lax.rem(place_of_tile, side)
    core = lax.rem(date, 2)
    mx = lax.rem(tile, 2) * x_low + lax.div(date, 2)

    def device(x, y, z, c):
        return ((y * side + z) * 2 + lax.div(x, x_low), lax.rem(x, x_low) * 2 + c)

    def moved(dx, dy, dz):
        x = lax.rem(mx + dx, nx) if dx else mx
        y = lax.rem(ty + dy, side) if dy else ty
        z = lax.rem(tx + dz, side) if dz else tx
        return x, y, z

    def offset(dx, dy, dz):
        return device(*moved(dx, dy, dz), core)

    sibling = device(mx, ty, tx, 1 - core)
    across = device(mx, tx, ty, core)
    top, bottom = ty == 0, ty == side - 1
    west, east = tx == 0, tx == side - 1
    has_across = jnp.logical_and(
        ty != tx,
        jnp.logical_or(jnp.logical_or(top, bottom), jnp.logical_or(west, east)),
    )

    def far(step):
        dx, dy, dz = step
        return min(dx, nx - dx) + min(dy, side - dy) + min(dz, side - dz)

    xy_steps = [(dx, dy, 0) for dx in range(nx) for dy in range(side) if dx or dy]
    xz_steps = [(dx, 0, dz) for dx in range(nx) for dz in range(side) if dx or dz]
    xy_steps.sort(key=far, reverse=True)
    xz_steps.sort(key=far, reverse=True)
    x_steps = [(dx, 0, 0) for dx in range(1, nx)]
    y_steps = [(0, dy, 0) for dy in range(1, side)]
    z_steps = [(0, 0, dz) for dz in range(1, side)]

    barrier = pltpu.get_barrier_semaphore()

    @pl.when(has_across)
    def _():
        pl.semaphore_signal(barrier, inc=1, device_id=across, device_id_type=MESH)

    peers = [offset(*step) for step in xy_steps]
    peers += [offset(*step) for step in xz_steps if step[2]]
    peers.append(sibling)
    for peer in peers:
        pl.semaphore_signal(barrier, inc=1, device_id=peer, device_id_type=MESH)

    loads = [
        pltpu.make_async_copy(src, dst, load_sem.at[number])
        for number, (src, dst) in enumerate(
            (
                (x_in, x_ref),
                (taps_in, taps_ref),
                (adj_in, adj),
                (w_gates_in, w_gates),
                (w_cand_in, w_cand_t),
                (gain_in, gain_ref),
                (b_up_in, b_up_ref),
                (b_down_in, b_down_ref),
                (b_gates_in, b_gates_ref),
                (b_cand_in, b_cand_ref),
                (w_up_in, w_up),
                (w_down_in, w_down_t),
                (h_in, h_ref),
                (g_in, g_ref),
            )
        )
    ]
    for load in loads:
        load.start()

    def tap(axis, number):
        row = ROW_TAPS + 3 * axis + number
        return par[row : row + 1, :channels].reshape(1, 1, channels)

    def set_columns(value, i):
        columns[0, :, pl.ds(i, 1), :] = value[:, 0:1, :]
        columns[1, :, pl.ds(i, 1), :] = value[:, 7:8, :]

    def put_line(exchange, kind, value):
        snd[exchange, kind] = value.reshape(FACES * SIDE, channels).astype(BF16)

    def put_columns(exchange):
        put_line(exchange, FIRST_COL, columns[0])
        put_line(exchange, LAST_COL, columns[1])

    loads[0].wait()

    def x_row(i):
        return x_ref[:, pl.ds(i, 1)].astype(F32).reshape(FACES, SIDE, channels)

    def x_lines(i, carry):
        set_columns(x_row(i), i)
        return carry

    lax.fori_loop(0, 8, x_lines, 0)
    put_columns(0)
    put_line(0, FIRST_ROW, x_row(0))
    put_line(0, LAST_ROW, x_row(7))

    @pl.when(has_across)
    def _():
        pl.semaphore_wait(barrier, len(peers) + 1)

    @pl.when(jnp.logical_not(has_across))
    def _():
        pl.semaphore_wait(barrier, len(peers))

    def halo_copies(exchange):
        on_columns = exchange in (0, 3)
        rows_turn = exchange in (0, 2)
        last, first = (LAST_COL, FIRST_COL) if on_columns else (LAST_ROW, FIRST_ROW)
        t_first, t_last = (FIRST_ROW, LAST_ROW) if rows_turn else (FIRST_COL, LAST_COL)
        row_first = jnp.logical_and(top, jnp.logical_not(west))
        row_last = jnp.logical_and(bottom, jnp.logical_not(east))
        col_first = jnp.logical_and(west, jnp.logical_not(top))
        col_last = jnp.logical_and(east, jnp.logical_not(bottom))
        if rows_turn:
            sends, receives = (row_first, row_last), (col_first, col_last)
        else:
            sends, receives = (col_first, col_last), (row_first, row_last)
        if on_columns:
            ahead, behind = offset(0, 0, 1), offset(0, 0, side - 1)
        else:
            ahead, behind = offset(0, 1, 0), offset(0, side - 1, 0)
        targets = (ahead, behind, across, across)
        return [
            (
                pltpu.make_async_remote_copy(
                    src_ref=snd.at[exchange, line],
                    dst_ref=rcv.at[exchange, kind],
                    send_sem=halo_send.at[exchange, kind],
                    recv_sem=halo_recv.at[exchange, kind],
                    device_id=target,
                    device_id_type=MESH,
                ),
                None if kind < 2 else sends[kind - 2],
                None if kind < 2 else receives[kind - 2],
                line,
            )
            for kind, (line, target) in enumerate(zip((last, first, t_first, t_last), targets))
        ]

    def start_halos(exchange):
        for copy, sends, _, _ in reversed(halo_copies(exchange)):
            if sends is None:
                copy.start()
            else:
                pl.when(sends)(copy.start)

    def finish_halo_sends(exchange):
        for copy, sends, _, _ in halo_copies(exchange):
            if sends is None:
                copy.wait_send()
            else:
                pl.when(sends)(copy.wait_send)

    def receive_halos(exchange):
        copies = halo_copies(exchange)
        corners = (jnp.logical_and(top, west), jnp.logical_and(bottom, east))

        def spread(ref, at):
            pool[at[0], at[1] : at[1] + 12] = (
                ref[...].astype(F32).reshape(FACES, SIDE, channels)
            )

        for kind, (copy, _, receives, line) in enumerate(copies):
            if kind < 2:
                copy.wait_recv()
                spread(rcv.at[exchange, kind], (kind, 0))
            else:

                @pl.when(receives)
                def _():
                    copy.wait_recv()
                    spread(rcv.at[exchange, kind], (kind - 2, 12))

                @pl.when(corners[kind - 2])
                def _():
                    spread(snd.at[exchange, line], (kind - 2, 12))

    def gather(to, which, edge, on_border, mode):
        for face in range(FACES):
            neighbour = adj[edge, 0, face]
            turned = adj[edge, 1, face] != (edge + 2) % 4
            if mode == "both":
                there = jnp.where(turned, 12 + neighbour, neighbour)
                index = jnp.where(on_border, there, face)
            elif mode == "straight":
                index = jnp.where(on_border, jnp.where(turned, 24, neighbour), face)
            else:
                index = jnp.where(jnp.logical_and(on_border, turned), 12 + neighbour, 24)
            to[face] = pool[which, index]

    place = lax.broadcasted_iota(jnp.int32, (FACES, SIDE, channels), 1)

    def upright(which, i):
        return jnp.broadcast_to(halo[which, :, pl.ds(i, 1), :], (FACES, SIDE, channels))

    def column_shifts(value, west_lines, east_lines, i):
        left = jnp.where(place == 0, upright(west_lines, i), pltpu.roll(value, 1, 1))
        right = jnp.where(place == 7, upright(east_lines, i), pltpu.roll(value, 7, 1))
        return left, right

    def rounded(value):
        return value.astype(BF16).astype(F32)

    start_halos(0)
    pool[...] = jnp.zeros_like(pool)
    small[...] = jnp.zeros_like(small)
    slab[SMALL_AT : 2 * HALF] = jnp.zeros((2 * HALF - SMALL_AT, 16, 128), BF16)
    for load in loads[1:10]:
        load.wait()
    for axis in range(2):
        for number in range(3):
            row = ROW_TAPS + 3 * axis + number
            par[row : row + 1, :channels] = taps_ref[number, axis : axis + 1, :].astype(F32)
    for row, ref in (
        (ROW_GAIN, gain_ref),
        (ROW_BUP, b_up_ref),
        (ROW_BDOWN, b_down_ref),
        (ROW_BGATES, b_gates_ref),
        (ROW_BCAND, b_cand_ref),
    ):
        size = ref.shape[0]
        par[row : row + 1, :size] = ref[...].astype(F32).reshape(1, size)
    wg_u[...] = w_gates[:, :channels]
    wg_r[...] = w_gates[:, channels:]
    wc_m[...] = w_cand_t[:, :channels]
    wc_r[...] = w_cand_t[:, channels:]
    for load in loads[10:]:
        load.wait()

    receive_halos(0)
    gather(halo.at[0], 0, 3, west, "both")
    gather(halo.at[1], 1, 1, east, "both")

    def first_pass(i, carry):
        value = x_row(i)
        left, right = column_shifts(value, 0, 1, i)
        first = rounded(tap(0, 0) * left + tap(0, 1) * value + tap(0, 2) * right)
        field[i + 1] = first
        set_columns(first, i)
        return carry

    lax.fori_loop(0, 8, first_pass, 0)
    put_columns(1)
    put_line(1, FIRST_ROW, field[1])
    put_line(1, LAST_ROW, field[8])
    start_halos(1)

    def vector(row, start, size):
        return par[row : row + 1, start : start + size]

    def cell(b, sums):
        rows = pl.ds(pl.multiple_of(b * 192, 192), 192)
        pair = (2 * b + 1, lax.rem(2 * b + 2, 8))

        @pl.when(b == 3)
        def _():
            receive_halos(1)
            gather(field.at[0], 0, 0, top, "both")
            gather(field.at[9], 1, 2, bottom, "both")

        def both(read):
            return jnp.concatenate(
                [read(i).reshape(FACES * SIDE, channels) for i in pair], axis=0
            )

        def second_row(i):
            return tap(1, 0) * field[i] + tap(1, 1) * field[i + 1] + tap(1, 2) * field[i + 2]

        def row_of(ref):
            return lambda i: ref[:, pl.ds(i, 1)].astype(F32)

        gain = vector(ROW_GAIN, 0, channels)
        centred = both(second_row)
        centred = centred - jnp.mean(centred, axis=-1, keepdims=True)
        inv_scale = lax.rsqrt(jnp.mean(centred * centred, axis=-1, keepdims=True) + EPSILON)
        standard = centred * inv_scale
        normed = (standard * gain).astype(BF16)
        normed_s[rows, :] = normed
        pre = nn(normed, w_up[...]) + vector(ROW_BUP, 0, w_up.shape[1])
        square = pre * pre
        curve = jnp.tanh(GELU_A * pre * (1.0 + GELU_B * square))
        hid = (0.5 * pre * (1.0 + curve)).astype(BF16)
        hid_s[rows, :] = hid
        slope = 0.5 * (1.0 + curve) + (0.5 * GELU_A) * pre * (1.0 - curve * curve) * (
            1.0 + 3.0 * GELU_B * square
        )
        mixed = (
            both(row_of(x_ref)) + nt(hid, w_down_t[...]) + vector(ROW_BDOWN, 0, channels)
        ).astype(BF16)
        joined_s[rows, :channels] = mixed
        prior = both(row_of(h_ref))
        prior_b = prior.astype(BF16)
        prior_s[rows, :] = prior_b
        update = sigmoid(
            nn(mixed, wg_u[:channels])
            + nn(prior_b, wg_u[channels:])
            + vector(ROW_BGATES, 0, channels)
        )
        reset = sigmoid(
            nn(mixed, wg_r[:channels])
            + nn(prior_b, wg_r[channels:])
            + vector(ROW_BGATES, channels, channels)
        )
        reset_state = (reset * prior).astype(BF16)
        joined_s[rows, channels:] = reset_state
        candidate = jnp.tanh(
            nt(mixed, wc_m[...]) + nt(reset_state, wc_r[...]) + vector(ROW_BCAND, 0, channels)
        )
        new = ((1.0 - update) * candidate + update * prior).astype(BF16)
        upstream = both(row_of(g_ref))
        kept = upstream * (1.0 - update)
        d_cand = (kept * (1.0 - candidate * candidate)).astype(BF16)
        d_cand_s[rows, :] = d_cand
        d_update = (kept * (prior - candidate) * update).astype(BF16)
        d_reset = (nn(d_cand, wc_r[...]) * prior * reset * (1.0 - reset)).astype(BF16)
        d_gate_s[rows, :channels] = d_update
        d_gate_s[rows, channels:] = d_reset
        d_mixed = (
            nn(d_cand, wc_m[...])
            + nt(d_update, wg_u[:channels])
            + nt(d_reset, wg_r[:channels])
        ).astype(BF16)
        d_mix_s[rows, :] = d_mixed
        d_pre = (nn(d_mixed, w_down_t[...]) * slope).astype(BF16)
        d_pre_s[rows, :] = d_pre
        d_normed = nt(d_pre, w_up[...])
        d_standard = d_normed * gain
        d_second = rounded(
            inv_scale
            * (
                d_standard
                - jnp.mean(d_standard, axis=-1, keepdims=True)
                - standard * jnp.mean(d_standard * standard, axis=-1, keepdims=True)
            )
        )
        new = new.astype(F32)
        for number, i in enumerate(pair):
            part = slice(number * 96, number * 96 + 96)
            d_sec[i + 1] = d_second[part].reshape(FACES, SIDE, channels)
            ns_out[:, pl.ds(i, 1)] = (
                new[part].reshape(FACES, 1, SIDE, channels).astype(BF16)
            )

        def total(value):
            return jnp.sum(value.astype(F32), axis=0, keepdims=True)

        extras = (
            total(d_pre),
            total(d_update),
            total(d_reset),
            total(d_normed * standard),
            total(d_mixed),
            total(d_cand),
        )
        return tuple(old + new_sum for old, new_sum in zip(sums, extras))

    zeros = jnp.zeros((1, channels), F32)
    sums = lax.fori_loop(
        0,
        4,
        cell,
        (jnp.zeros((1, w_up.shape[1]), F32), zeros, zeros, zeros, zeros, zeros),
    )
    put_line(2, FIRST_ROW, d_sec[1])
    put_line(2, LAST_ROW, d_sec[8])
    start_halos(2)
    small[ROW_BUP : ROW_BUP + 1, :] = sums[0]
    small[ROW_BGATES : ROW_BGATES + 1, :channels] = sums[1]
    small[ROW_BGATES : ROW_BGATES + 1, channels : 2 * channels] = sums[2]
    small[ROW_GAIN : ROW_GAIN + 1, :channels] = sums[3]
    small[ROW_BDOWN : ROW_BDOWN + 1, :channels] = sums[4]
    small[ROW_BCAND : ROW_BCAND + 1, :channels] = sums[5]

    def remote(src, dst, stage, target):
        return pltpu.make_async_remote_copy(
            src_ref=src,
            dst_ref=dst,
            send_sem=red_send.at[stage],
            recv_sem=red_recv.at[stage],
            device_id=target,
            device_id_type=MESH,
        )

    def whole_wait(ref, sem):
        pltpu.make_async_copy(ref, ref, sem).wait()

    def core_copy(region):
        return remote(
            slab.at[pl.ds((1 - core) * HALF + region * REGION, REGION)],
            core_rcv.at[pl.ds(region * REGION, REGION)],
            region,
            sibling,
        )

    store_tiles(slab, CAND_AT, tn(d_cand_s[...], joined_s[...]))
    store_tiles(slab, GATES_AT, tn(joined_s[:, :channels], d_gate_s[...]))
    store_tiles(slab, GATES_AT + 36, tn(prior_s[...], d_gate_s[...]))
    store_tiles(slab, DOWN_AT, tn(d_mix_s[...], hid_s[...]))
    core_copy(0).start()
    store_tiles(slab, UP_AT, tn(normed_s[...], d_pre_s[...]))
    core_copy(1).start()

    def add_cores(region):
        core_copy(region).wait_recv()

        def some(step, carry):
            here = region * REGION + step * 8
            total = slab[pl.ds(core * HALF + here, 8)].astype(F32)
            t1[pl.ds(here, 8)] = (total + core_rcv[pl.ds(here, 8)].astype(F32)).astype(BF16)
            return carry

        lax.fori_loop(0, REGION // 8, some, 0)

    def scatter(region, steps, received, stage):
        for number, step in enumerate(steps):
            x, y, z = moved(*step)
            other = z if region else y
            remote(
                t1.at[pl.ds(region * REGION + (x * side + other) * unit, unit)],
                received.at[number],
                stage,
                device(x, y, z, core),
            ).start()

    add_cores(0)
    scatter(0, xy_steps, xy_rcv, 2)
    add_cores(1)
    scatter(1, xz_steps, xz_rcv, 3)

    receive_halos(2)
    gather(d_sec.at[0], 0, 0, top, "straight")
    gather(d_sec.at[9], 1, 2, bottom, "straight")
    gather(halo.at[2], 0, 3, west, "turned")
    gather(halo.at[3], 1, 1, east, "turned")

    def first_back(i, sums):
        value = d_sec[i + 1]
        d_first = tap(1, 0) * d_sec[i + 2] + tap(1, 1) * value + tap(1, 2) * d_sec[i]
        d_first += jnp.where(place == 0, tap(1, 0) * upright(2, i), 0.0)
        d_first += jnp.where(place == 7, tap(1, 2) * upright(3, i), 0.0)
        d_first = rounded(d_first)
        d_first_s[i] = d_first
        set_columns(d_first, i)
        x_value = x_row(i)
        left, right = column_shifts(x_value, 0, 1, i)
        pairs = (
            (d_first, left),
            (d_first, x_value),
            (d_first, right),
            (value, field[i]),
            (value, field[i + 1]),
            (value, field[i + 2]),
        )
        return tuple(old + jnp.sum(a * c, axis=0) for old, (a, c) in zip(sums, pairs))

    tap_sums = lax.fori_loop(
        0, 8, first_back, tuple(jnp.zeros((SIDE, channels), F32) for _ in range(6))
    )
    put_columns(3)
    start_halos(3)

    for number, tap_sum in enumerate(tap_sums):
        row = ROW_TAPS + number
        small[row : row + 1, :channels] = jnp.sum(tap_sum, axis=0, keepdims=True)
    tile32[...] = jnp.zeros_like(tile32)
    line = 0
    for row, count in SMALL_ROWS:
        for number in range(count):
            tile32[line : line + 1, :] = small[row : row + 1, number * 128 : number * 128 + 128]
            line += 1
    small_c[0] = tile32[...].astype(BF16)
    small_core = remote(small_c.at[0], small_c.at[1], 4, sibling)
    small_core.start()

    def spread_slot(slots, me, steps, stage):
        for step in steps:
            remote(slots.at[me], slots.at[me], stage, offset(*step)).start()

    def sum_slots(slots, stage):
        count = slots.shape[0]
        whole_wait(slots.at[pl.ds(0, count - 1)], red_recv.at[stage])
        total = slots[0].astype(F32)
        for number in range(1, count):
            total += slots[number].astype(F32)
        return total

    def add_scattered(region, at, received, slots, slot, stage):
        whole_wait(received, red_recv.at[stage])
        total = t1[pl.ds(region * REGION + at * unit, unit)].astype(F32)
        for number in range(received.shape[0]):
            total += received[number].astype(F32)
        slots[slot] = total.astype(BF16)

    add_scattered(0, mx * side + ty, xy_rcv, cz, tx, 2)
    spread_slot(cz, tx, z_steps, 5)
    add_scattered(1, mx * side + tx, xz_rcv, cy, ty, 3)
    spread_slot(cy, ty, y_steps, 6)
    small_core.wait_recv()
    small_x[mx] = (small_c[0].astype(F32) + small_c[1].astype(F32)).astype(BF16)
    spread_slot(small_x, mx, x_steps, 7)
    small_y[ty] = sum_slots(small_x, 7).astype(BF16)
    spread_slot(small_y, ty, y_steps, 8)

    base = core * HALF

    def share(region, at, slots, stage, steps, out_stage):
        at = base + region * REGION + at * unit
        gathered[pl.ds(at, unit)] = (sum_slots(slots, stage) * norm_factor).astype(BF16)
        piece = gathered.at[pl.ds(at, unit)]
        for step in steps:
            remote(piece, piece, out_stage, offset(*step)).start()

    share(0, mx * side + ty, cz, 5, xy_steps, 10)
    share(1, mx * side + tx, cy, 6, xz_steps, 11)

    receive_halos(3)
    gather(halo.at[2], 0, 3, west, "straight")
    gather(halo.at[3], 1, 1, east, "straight")
    gather(halo.at[4], 0, 0, top, "turned")
    gather(halo.at[5], 1, 2, bottom, "turned")

    def input_back(i, carry):
        value = d_first_s[i]
        left, right = column_shifts(value, 2, 3, i)
        d_input = tap(0, 0) * right + tap(0, 1) * value + tap(0, 2) * left
        on_top = jnp.where(i == 0, 1.0, 0.0)
        on_bottom = jnp.where(i == 7, 1.0, 0.0)
        d_input += on_top * (tap(0, 0) * halo[4]) + on_bottom * (tap(0, 2) * halo[5])
        at = pl.multiple_of(lax.rem(i + 7, 8) * 96, 96)
        d_mixed = d_mix_s[pl.ds(at, 96), :].astype(F32).reshape(FACES, SIDE, channels)
        gi_out[:, pl.ds(i, 1)] = (
            (d_input + d_mixed).reshape(FACES, 1, SIDE, channels).astype(BF16)
        )
        return carry

    lax.fori_loop(0, 8, input_back, 0)

    small_z[tx] = sum_slots(small_y, 8).astype(BF16)
    spread_slot(small_z, tx, z_steps, 9)
    small_out[...] = sum_slots(small_z, 9) * norm_factor

    def core_back(region):
        piece = gathered.at[pl.ds(base + region * REGION, REGION)]
        return remote(piece, piece, 12 + region, sibling)

    shares = nx * side - 1
    for region in range(2):
        whole_wait(gathered.at[pl.ds(0, unit * shares)], red_recv.at[10 + region])
        core_back(region).start()
    for region in range(2):
        core_back(region).wait_recv()
    slab_out[...] = gathered[...]

    for exchange in range(4):
        finish_halo_sends(exchange)
    small_core.wait_send()
    for region in range(2):
        core_copy(region).wait_send()
        core_back(region).wait_send()
    for ref, stage in (
        (xy_rcv, 2),
        (xz_rcv, 3),
        (cz.at[pl.ds(0, side - 1)], 5),
        (cy.at[pl.ds(0, side - 1)], 6),
        (small_x.at[pl.ds(0, nx - 1)], 7),
        (small_y.at[pl.ds(0, side - 1)], 8),
        (small_z.at[pl.ds(0, side - 1)], 9),
        (gathered.at[pl.ds(0, unit * shares)], 10),
        (gathered.at[pl.ds(0, unit * shares)], 11),
    ):
        whole_wait(ref, red_send.at[stage])


def unpack_kernel(
    ns,
    gi,
    slab,
    small,
    ns_out,
    gi_out,
    taps_out,
    gain_out,
    up_out,
    b_up_out,
    down_out,
    b_down_out,
    gates_out,
    b_gates_out,
    cand_out,
    b_cand_out,
):
    ns_out[...] = ns[...]
    gi_out[...] = gi[...]

    def unpack(at, out):
        across = out.shape[1] // 128
        for row in range(out.shape[0] // 16):
            for column in range(across):
                out[row * 16 : row * 16 + 16, column * 128 : column * 128 + 128] = slab[
                    tile_place(at + row * across + column)
                ]

    unpack(CAND_AT, cand_out)
    unpack(GATES_AT, gates_out)
    unpack(DOWN_AT, down_out)
    unpack(UP_AT, up_out)

    def row_at(line, size):
        pieces = [small[line + number : line + number + 1, :] for number in range(-(-size // 128))]
        return jnp.concatenate(pieces, axis=1)[:, :size].astype(BF16)

    channels = gain_out.shape[0]
    for axis in range(2):
        for number in range(3):
            taps_out[number, axis : axis + 1, :] = row_at(9 + 2 * (3 * axis + number), channels)
    for out, line in (
        (b_up_out, 0),
        (b_gates_out, 6),
        (gain_out, 21),
        (b_down_out, 23),
        (b_cand_out, 25),
    ):
        out[...] = row_at(line, out.shape[0]).reshape(out.shape)


def on_device(
    inputs,
    state,
    cotangent,
    adjacency,
    taps,
    gain,
    w_up,
    b_up,
    w_down,
    b_down,
    w_gates,
    b_gates,
    w_cand,
    b_cand,
):
    channels = inputs.shape[-1]
    wide = w_up.shape[1]
    tokens = FACES * SIDE * SIDE
    lines = FACES * SIDE
    tile_count, date_count = lax.axis_size("tile"), lax.axis_size("date")
    side = 2 ** ((tile_count.bit_length() - 2) // 2)
    x_low = date_count // 2
    nx = 2 * x_low
    unit = REGION // (nx * side)
    norm_factor = float(tokens * tile_count * date_count) ** (-0.5)
    vmem = pl.BlockSpec(memory_space=pltpu.VMEM)
    hbm = pl.BlockSpec(memory_space=pltpu.HBM)
    grid_shape = (FACES, SIDE, SIDE, channels)

    def buf(*shape):
        return pltpu.VMEM(shape, BF16)

    def wide_buf(*shape):
        return pltpu.VMEM(shape, F32)

    def arr(*shape):
        return jax.ShapeDtypeStruct(shape, BF16)

    shares = nx * side - 1
    new_rows, grad_rows, slab, small = pl.pallas_call(
        functools.partial(level_kernel, side, x_low, norm_factor),
        name="level",
        out_shape=(
            arr(*grid_shape),
            arr(*grid_shape),
            arr(2 * HALF, 16, 128),
            jax.ShapeDtypeStruct((32, 128), F32),
        ),
        in_specs=[hbm] * 14,
        out_specs=[vmem] * 4,
        scratch_shapes=[
            pltpu.SMEM((4, 2, FACES), jnp.int32),
            buf(*grid_shape),
            buf(*grid_shape),
            buf(*grid_shape),
            buf(3, 2, channels),
            buf(channels),
            buf(wide),
            buf(channels),
            buf(2 * channels),
            buf(channels),
            buf(channels, wide),
            buf(channels, wide),
            buf(2 * channels, 2 * channels),
            buf(channels, 2 * channels),
            wide_buf(16, wide),
            buf(4, 4, lines, channels),
            buf(4, 4, lines, channels),
            wide_buf(2, 25, SIDE, channels),
            wide_buf(6, FACES, SIDE, channels),
            wide_buf(2, FACES, SIDE, channels),
            wide_buf(10, FACES, SIDE, channels),
            wide_buf(10, FACES, SIDE, channels),
            wide_buf(8, FACES, SIDE, channels),
            buf(2 * channels, channels),
            buf(2 * channels, channels),
            buf(channels, channels),
            buf(channels, channels),
            buf(tokens, channels),
            buf(tokens, channels),
            buf(tokens, wide),
            buf(tokens, wide),
            buf(tokens, channels),
            buf(tokens, 2 * channels),
            buf(tokens, 2 * channels),
            buf(tokens, channels),
            wide_buf(16, wide),
            wide_buf(32, 128),
            buf(2, 32, 128),
            buf(nx, 32, 128),
            buf(side, 32, 128),
            buf(side, 32, 128),
            buf(2 * HALF, 16, 128),
            buf(HALF, 16, 128),
            buf(HALF, 16, 128),
            buf(shares, unit, 16, 128),
            buf(shares, unit, 16, 128),
            buf(side, unit, 16, 128),
            buf(side, unit, 16, 128),
            buf(2 * HALF, 16, 128),
            pltpu.SemaphoreType.DMA((14,)),
            pltpu.SemaphoreType.DMA((4, 4)),
            pltpu.SemaphoreType.DMA((4, 4)),
            pltpu.SemaphoreType.DMA((14,)),
            pltpu.SemaphoreType.DMA((14,)),
        ],
        compiler_params=pltpu.CompilerParams(
            collective_id=0, has_side_effects=True, vmem_limit_bytes=60 * 2**20
        ),
    )(
        adjacency.transpose(1, 2, 0),
        inputs.reshape(grid_shape),
        state.reshape(grid_shape),
        cotangent.reshape(grid_shape),
        taps.transpose(1, 0, 2),
        gain,
        b_up,
        b_down,
        b_gates,
        b_cand,
        w_up,
        w_down.T,
        w_gates,
        w_cand.T,
    )
    new_rows, grad_rows, g_taps, g_gain, g_up, g_bup, g_down, g_bdown, g_gates, g_bgates, g_cand, g_bcand = (
        pl.pallas_call(
            unpack_kernel,
            name="unpack",
            out_shape=(
                arr(*grid_shape),
                arr(*grid_shape),
                arr(3, 2, channels),
                arr(channels),
                arr(channels, wide),
                arr(wide),
                arr(channels, wide),
                arr(channels),
                arr(2 * channels, 2 * channels),
                arr(2 * channels),
                arr(channels, 2 * channels),
                arr(channels),
            ),
            in_specs=[vmem] * 4,
            out_specs=[vmem] * 12,
            compiler_params=pltpu.CompilerParams(vmem_limit_bytes=32 * 2**20),
        )(new_rows, grad_rows, slab, small)
    )
    return (
        new_rows.reshape(inputs.shape),
        grad_rows.reshape(inputs.shape),
        g_taps.transpose(1, 0, 2),
        g_gain,
        g_up,
        g_bup,
        g_down.T,
        g_bdown,
        g_gates,
        g_bgates,
        g_cand.T,
        g_bcand,
    )


def solution(mesh):
    field = P("tile", "date", None, None, None, None)
    return jax.shard_map(
        on_device,
        mesh=mesh,
        in_specs=(field,) * 3 + (P(),) * 11,
        out_specs=(field,) * 2 + (P(),) * 10,
        check_vma=False,
    )
```

```python
import functools
import math

import jax
import jax.numpy as jnp
from jax import lax
from jax.experimental import pallas as pl
from jax.experimental.pallas import tpu as pltpu
from jax.sharding import PartitionSpec as P

EPSILON = 1e-06
MESH = pl.DeviceIdType.MESH
F32 = jnp.float32
BF16 = jnp.bfloat16
FACES = 12
SIDE = 8
HALF = 128
REGION = 64
FIRST_ROW, LAST_ROW, FIRST_COL, LAST_COL = range(4)
GELU_A = math.sqrt(2.0 / math.pi)
GELU_B = 0.044715
ROW_BUP, ROW_BGATES, ROW_TAPS, ROW_GAIN, ROW_BDOWN, ROW_BCAND = 0, 1, 2, 8, 9, 10
SMALL_ROWS = ((0, 6), (1, 3)) + tuple((row, 2) for row in range(2, 11))
CAND_AT, GATES_AT, DOWN_AT, UP_AT, SMALL_AT = 0, 36, 108, 180, 252


def nn(left, right):
    return jnp.dot(left, right, preferred_element_type=F32)


def nt(left, right):
    return lax.dot_general(left, right, (((1,), (1,)), ((), ())), preferred_element_type=F32)


def tn(left, right):
    return lax.dot_general(left, right, (((0,), (0,)), ((), ())), preferred_element_type=F32)


def sigmoid(value):
    return 0.5 + 0.5 * jnp.tanh(0.5 * value)


def tile_place(number):
    if 64 <= number < 128:
        return number + 64
    if 128 <= number < 192:
        return number - 64
    return number


def store_tiles(slab, at, matrix):
    rows, columns = matrix.shape
    packed = matrix.astype(BF16)
    across = columns // 128
    for row in range(rows // 16):
        for column in range(across):
            slab[tile_place(at + row * across + column)] = packed[
                row * 16 : row * 16 + 16, column * 128 : column * 128 + 128
            ]


def level_kernel(
    side,
    x_low,
    norm_factor,
    adj_in,
    x_in,
    h_in,
    g_in,
    taps_in,
    gain_in,
    b_up_in,
    b_down_in,
    b_gates_in,
    b_cand_in,
    w_up_in,
    w_down_in,
    w_gates_in,
    w_cand_in,
    ns_out,
    gi_out,
    taps_out,
    gain_out,
    up_out,
    b_up_out,
    down_out,
    b_down_out,
    gates_out,
    b_gates_out,
    cand_out,
    b_cand_out,
    adj,
    x_ref,
    h_ref,
    g_ref,
    taps_ref,
    gain_ref,
    b_up_ref,
    b_down_ref,
    b_gates_ref,
    b_cand_ref,
    w_up,
    w_down_t,
    w_gates,
    w_cand_t,
    par,
    snd,
    rcv,
    far_snd,
    far_rcv,
    far_pool,
    pool,
    halo,
    columns,
    field,
    d_sec,
    d_first_s,
    wg_u,
    wg_r,
    wc_m,
    wc_r,
    prior_s,
    normed_s,
    hid_s,
    d_pre_s,
    d_mix_s,
    d_gate_s,
    joined_s,
    d_cand_s,
    small,
    tile32,
    small_c,
    small_x,
    small_y,
    small_z,
    slab,
    core_rcv,
    t1,
    xy_rcv,
    xz_rcv,
    cz,
    cy,
    gathered,
    load_sem,
    halo_send,
    halo_recv,
    far_send,
    far_recv,
    red_send,
    red_recv,
):
    channels = x_ref.shape[3]
    nx = 2 * x_low
    unit = REGION // (nx * side)
    tile = lax.axis_index("tile")
    date = lax.axis_index("date")
    place_of_tile = lax.div(tile, 2)
    ty, tx = lax.div(place_of_tile, side), lax.rem(place_of_tile, side)
    core = lax.rem(date, 2)
    mx = lax.rem(tile, 2) * x_low + lax.div(date, 2)

    def device(x, y, z, c):
        return ((y * side + z) * 2 + lax.div(x, x_low), lax.rem(x, x_low) * 2 + c)

    def moved(dx, dy, dz):
        x = lax.rem(mx + dx, nx) if dx else mx
        y = lax.rem(ty + dy, side) if dy else ty
        z = lax.rem(tx + dz, side) if dz else tx
        return x, y, z

    def offset(dx, dy, dz):
        return device(*moved(dx, dy, dz), core)

    sibling = device(mx, ty, tx, 1 - core)
    across = device(mx, tx, ty, core)
    top, bottom = ty == 0, ty == side - 1
    west, east = tx == 0, tx == side - 1
    has_across = jnp.logical_and(
        ty != tx,
        jnp.logical_or(jnp.logical_or(top, bottom), jnp.logical_or(west, east)),
    )

    def far(step):
        dx, dy, dz = step
        return min(dx, nx - dx) + min(dy, side - dy) + min(dz, side - dz)

    xy_steps = [(dx, dy, 0) for dx in range(nx) for dy in range(side) if dx or dy]
    xz_steps = [(dx, 0, dz) for dx in range(nx) for dz in range(side) if dx or dz]
    xy_steps.sort(key=far, reverse=True)
    xz_steps.sort(key=far, reverse=True)
    x_steps = [(dx, 0, 0) for dx in range(1, nx)]
    y_steps = [(0, dy, 0) for dy in range(1, side)]
    z_steps = [(0, 0, dz) for dz in range(1, side)]

    barrier = pltpu.get_barrier_semaphore()

    @pl.when(has_across)
    def _():
        pl.semaphore_signal(barrier, inc=1, device_id=across, device_id_type=MESH)

    loads = [
        pltpu.make_async_copy(src, dst, load_sem.at[number])
        for number, (src, dst) in enumerate(
            (
                (x_in, x_ref),
                (taps_in, taps_ref),
                (adj_in, adj),
                (w_gates_in, w_gates),
                (w_cand_in, w_cand_t),
                (gain_in, gain_ref),
                (b_up_in, b_up_ref),
                (b_down_in, b_down_ref),
                (b_gates_in, b_gates_ref),
                (b_cand_in, b_cand_ref),
                (w_up_in, w_up),
                (w_down_in, w_down_t),
                (h_in, h_ref),
                (g_in, g_ref),
            )
        )
    ]
    loads[0].start()
    peers = [offset(*step) for step in sorted(xy_steps, key=far)]
    peers += [offset(*step) for step in sorted(xz_steps, key=far) if step[2]]
    peers.append(sibling)
    for peer in peers:
        pl.semaphore_signal(barrier, inc=1, device_id=peer, device_id_type=MESH)
    for load in loads[1:]:
        load.start()

    def tap(axis, number):
        row = ROW_TAPS + 3 * axis + number
        return par[row : row + 1, :channels].reshape(1, 1, channels)

    def set_columns(value, i):
        columns[0, :, pl.ds(i, 1), :] = value[:, 0:1, :]
        columns[1, :, pl.ds(i, 1), :] = value[:, 7:8, :]

    def put_line(exchange, kind, value):
        snd[exchange, kind] = value.reshape(FACES * SIDE, channels).astype(BF16)

    def rounded(value):
        return value.astype(BF16).astype(F32)

    def put_columns(exchange):
        put_line(exchange, FIRST_COL, columns[0])
        put_line(exchange, LAST_COL, columns[1])

    loads[0].wait()

    def x_row(i):
        return x_ref[:, pl.ds(i, 1)].astype(F32).reshape(FACES, SIDE, channels)

    def x_lines(i, carry):
        value = x_row(i)
        set_columns(value, i)
        columns[2, :, pl.ds(i, 1), :] = value[:, 1:2, :]
        columns[3, :, pl.ds(i, 1), :] = value[:, 6:7, :]
        return carry

    lax.fori_loop(0, 8, x_lines, 0)
    put_columns(0)
    put_line(0, FIRST_ROW, x_row(0))
    put_line(0, LAST_ROW, x_row(7))
    for number, order in enumerate(((0, 2), (3, 1))):
        for position, column in enumerate(order):
            far_snd[number, position * 96 : position * 96 + 96] = (
                columns[column].reshape(FACES * SIDE, channels).astype(BF16)
            )

    @pl.when(has_across)
    def _():
        pl.semaphore_wait(barrier, len(peers) + 1)

    @pl.when(jnp.logical_not(has_across))
    def _():
        pl.semaphore_wait(barrier, len(peers))

    row_first = jnp.logical_and(top, jnp.logical_not(west))
    row_last = jnp.logical_and(bottom, jnp.logical_not(east))
    col_first = jnp.logical_and(west, jnp.logical_not(top))
    col_last = jnp.logical_and(east, jnp.logical_not(bottom))
    corners = (jnp.logical_and(top, west), jnp.logical_and(bottom, east))

    far_copies = [
        pltpu.make_async_remote_copy(
            src_ref=far_snd.at[number],
            dst_ref=far_rcv.at[number],
            send_sem=far_send.at[number],
            recv_sem=far_recv.at[number],
            device_id=across,
            device_id_type=MESH,
        )
        for number in range(2)
    ]
    far_sends, far_receives = (col_first, col_last), (row_first, row_last)

    def halo_copies(exchange):
        on_columns = exchange in (0, 3)
        rows_turn = exchange in (0, 2)
        last, first = (LAST_COL, FIRST_COL) if on_columns else (LAST_ROW, FIRST_ROW)
        t_first, t_last = (FIRST_ROW, LAST_ROW) if rows_turn else (FIRST_COL, LAST_COL)
        if rows_turn:
            sends, receives = (row_first, row_last), (col_first, col_last)
        else:
            sends, receives = (col_first, col_last), (row_first, row_last)
        if on_columns:
            ahead, behind = offset(0, 0, 1), offset(0, 0, side - 1)
        else:
            ahead, behind = offset(0, 1, 0), offset(0, side - 1, 0)
        targets = (ahead, behind, across, across)
        return [
            (
                pltpu.make_async_remote_copy(
                    src_ref=snd.at[exchange, line],
                    dst_ref=rcv.at[exchange, kind],
                    send_sem=halo_send.at[exchange, kind],
                    recv_sem=halo_recv.at[exchange, kind],
                    device_id=target,
                    device_id_type=MESH,
                ),
                None if kind < 2 else sends[kind - 2],
                None if kind < 2 else receives[kind - 2],
                line,
            )
            for kind, (line, target) in enumerate(zip((last, first, t_first, t_last), targets))
            if kind < 2 or exchange != 1
        ]

    def start_halos(exchange):
        for copy, sends, _, _ in reversed(halo_copies(exchange)):
            if sends is None:
                copy.start()
            else:
                pl.when(sends)(copy.start)

    def finish_halo_sends(exchange):
        for copy, sends, _, _ in halo_copies(exchange):
            if sends is None:
                copy.wait_send()
            else:
                pl.when(sends)(copy.wait_send)

    def receive_halos(exchange):
        copies = halo_copies(exchange)

        def spread(ref, at):
            pool[at[0], at[1] : at[1] + 12] = (
                ref[...].astype(F32).reshape(FACES, SIDE, channels)
            )

        for kind, (copy, _, receives, line) in enumerate(copies):
            if kind < 2:
                copy.wait_recv()
                spread(rcv.at[exchange, kind], (kind, 0))
            else:

                @pl.when(receives)
                def _():
                    copy.wait_recv()
                    spread(rcv.at[exchange, kind], (kind - 2, 12))

                @pl.when(corners[kind - 2])
                def _():
                    spread(snd.at[exchange, line], (kind - 2, 12))

    def gather(to, which, edge, on_border, mode):
        for face in range(FACES):
            neighbour = adj[edge, 0, face]
            turned = adj[edge, 1, face] != (edge + 2) % 4
            if mode == "both":
                there = jnp.where(turned, 12 + neighbour, neighbour)
                index = jnp.where(on_border, there, face)
            elif mode == "straight":
                index = jnp.where(on_border, jnp.where(turned, 24, neighbour), face)
            else:
                index = jnp.where(jnp.logical_and(on_border, turned), 12 + neighbour, 24)
            to[face] = pool[which, index]

    def border_lines(to, which, edge, on_border, row):
        def spread(ref):
            far_pool[which] = ref[...].astype(F32).reshape(2, FACES, SIDE, channels)

        @pl.when(far_receives[which])
        def _():
            far_copies[which].wait_recv()
            spread(far_rcv.at[which])

        @pl.when(corners[which])
        def _():
            spread(far_snd.at[which])

        own = x_row(row)
        for face in range(FACES):
            neighbour = adj[edge, 0, face]
            turned = jnp.logical_and(on_border, adj[edge, 1, face] != (edge + 2) % 4)
            straight = jnp.where(on_border, jnp.where(turned, 24, neighbour), face)
            low, high = far_pool[which, 0, neighbour], far_pool[which, 1, neighbour]
            lines = (own[face], low, high) if edge == 0 else (low, high, own[face])
            made = sum(tap(0, number)[0] * lines[number] for number in range(3))
            to[face] = jnp.where(turned, rounded(made), pool[which, straight])

    place = lax.broadcasted_iota(jnp.int32, (FACES, SIDE, channels), 1)

    def upright(which, i):
        return jnp.broadcast_to(halo[which, :, pl.ds(i, 1), :], (FACES, SIDE, channels))

    def column_shifts(value, west_lines, east_lines, i):
        left = jnp.where(place == 0, upright(west_lines, i), pltpu.roll(value, 1, 1))
        right = jnp.where(place == 7, upright(east_lines, i), pltpu.roll(value, 7, 1))
        return left, right

    start_halos(0)
    for number in range(2):
        pl.when(far_sends[number])(far_copies[number].start)
    pool[...] = jnp.zeros_like(pool)
    far_pool[...] = jnp.zeros_like(far_pool)
    small[...] = jnp.zeros_like(small)
    slab[SMALL_AT : 2 * HALF] = jnp.zeros((2 * HALF - SMALL_AT, 16, 128), BF16)
    for load in loads[1:10]:
        load.wait()
    for axis in range(2):
        for number in range(3):
            row = ROW_TAPS + 3 * axis + number
            par[row : row + 1, :channels] = taps_ref[number, axis : axis + 1, :].astype(F32)
    for row, ref in (
        (ROW_GAIN, gain_ref),
        (ROW_BUP, b_up_ref),
        (ROW_BDOWN, b_down_ref),
        (ROW_BGATES, b_gates_ref),
        (ROW_BCAND, b_cand_ref),
    ):
        size = ref.shape[0]
        par[row : row + 1, :size] = ref[...].astype(F32).reshape(1, size)
    wg_u[...] = w_gates[:, :channels]
    wg_r[...] = w_gates[:, channels:]
    wc_m[...] = w_cand_t[:, :channels]
    wc_r[...] = w_cand_t[:, channels:]
    for load in loads[10:]:
        load.wait()

    receive_halos(0)
    gather(halo.at[0], 0, 3, west, "both")
    gather(halo.at[1], 1, 1, east, "both")

    def first_pass(i, carry):
        value = x_row(i)
        left, right = column_shifts(value, 0, 1, i)
        first = rounded(tap(0, 0) * left + tap(0, 1) * value + tap(0, 2) * right)
        field[i + 1] = first
        set_columns(first, i)
        return carry

    lax.fori_loop(0, 8, first_pass, 0)
    put_columns(1)
    put_line(1, FIRST_ROW, field[1])
    put_line(1, LAST_ROW, field[8])
    start_halos(1)

    def vector(row, start, size):
        return par[row : row + 1, start : start + size]

    def cell(b, sums):
        rows = pl.ds(pl.multiple_of(b * 192, 192), 192)
        pair = (2 * b + 1, lax.rem(2 * b + 2, 8))

        @pl.when(b == 3)
        def _():
            receive_halos(1)
            border_lines(field.at[0], 0, 0, top, 0)
            border_lines(field.at[9], 1, 2, bottom, 7)

        def both(read):
            return jnp.concatenate(
                [read(i).reshape(FACES * SIDE, channels) for i in pair], axis=0
            )

        def second_row(i):
            return tap(1, 0) * field[i] + tap(1, 1) * field[i + 1] + tap(1, 2) * field[i + 2]

        def row_of(ref):
            return lambda i: ref[:, pl.ds(i, 1)].astype(F32)

        gain = vector(ROW_GAIN, 0, channels)
        centred = both(second_row)
        centred = centred - jnp.mean(centred, axis=-1, keepdims=True)
        inv_scale = lax.rsqrt(jnp.mean(centred * centred, axis=-1, keepdims=True) + EPSILON)
        standard = centred * inv_scale
        normed = (standard * gain).astype(BF16)
        normed_s[rows, :] = normed
        pre = nn(normed, w_up[...]) + vector(ROW_BUP, 0, w_up.shape[1])
        square = pre * pre
        curve = jnp.tanh(pre * (GELU_A + (GELU_A * GELU_B) * square))
        rise = 1.0 + curve
        half = 0.5 * pre
        hid = (half * rise).astype(BF16)
        hid_s[rows, :] = hid
        slope = rise * (
            0.5 + half * (1.0 - curve) * (GELU_A + (3.0 * GELU_A * GELU_B) * square)
        )
        mixed = (
            both(row_of(x_ref)) + nt(hid, w_down_t[...]) + vector(ROW_BDOWN, 0, channels)
        ).astype(BF16)
        joined_s[rows, :channels] = mixed
        prior = both(row_of(h_ref))
        prior_b = prior.astype(BF16)
        prior_s[rows, :] = prior_b
        update = sigmoid(
            nn(mixed, wg_u[:channels])
            + nn(prior_b, wg_u[channels:])
            + vector(ROW_BGATES, 0, channels)
        )
        reset = sigmoid(
            nn(mixed, wg_r[:channels])
            + nn(prior_b, wg_r[channels:])
            + vector(ROW_BGATES, channels, channels)
        )
        reset_state = (reset * prior).astype(BF16)
        joined_s[rows, channels:] = reset_state
        candidate = jnp.tanh(
            nt(mixed, wc_m[...]) + nt(reset_state, wc_r[...]) + vector(ROW_BCAND, 0, channels)
        )
        new = ((1.0 - update) * candidate + update * prior).astype(BF16)
        upstream = both(row_of(g_ref))
        kept = upstream * (1.0 - update)
        d_cand = (kept * (1.0 - candidate * candidate)).astype(BF16)
        d_cand_s[rows, :] = d_cand
        d_update = (kept * (prior - candidate) * update).astype(BF16)
        d_reset = (nn(d_cand, wc_r[...]) * prior * reset * (1.0 - reset)).astype(BF16)
        d_gate_s[rows, :channels] = d_update
        d_gate_s[rows, channels:] = d_reset
        d_mixed = (
            nn(d_cand, wc_m[...])
            + nt(d_update, wg_u[:channels])
            + nt(d_reset, wg_r[:channels])
        ).astype(BF16)
        d_mix_s[rows, :] = d_mixed
        d_pre = (nn(d_mixed, w_down_t[...]) * slope).astype(BF16)
        d_pre_s[rows, :] = d_pre
        d_normed = nt(d_pre, w_up[...])
        d_standard = d_normed * gain
        d_second = rounded(
            inv_scale
            * (
                d_standard
                - jnp.mean(d_standard, axis=-1, keepdims=True)
                - standard * jnp.mean(d_standard * standard, axis=-1, keepdims=True)
            )
        )
        new = new.astype(F32)
        for number, i in enumerate(pair):
            part = slice(number * 96, number * 96 + 96)
            d_sec[i + 1] = d_second[part].reshape(FACES, SIDE, channels)
            ns_out[:, pl.ds(i, 1)] = (
                new[part].reshape(FACES, 1, SIDE, channels).astype(BF16)
            )

        def total(value):
            return jnp.sum(value.astype(F32), axis=0, keepdims=True)

        extras = (
            total(d_pre),
            total(d_update),
            total(d_reset),
            total(d_normed * standard),
            total(d_mixed),
            total(d_cand),
        )
        return tuple(old + new_sum for old, new_sum in zip(sums, extras))

    zeros = jnp.zeros((1, channels), F32)
    sums = lax.fori_loop(
        0,
        4,
        cell,
        (jnp.zeros((1, w_up.shape[1]), F32), zeros, zeros, zeros, zeros, zeros),
    )
    put_line(2, FIRST_ROW, d_sec[1])
    put_line(2, LAST_ROW, d_sec[8])
    start_halos(2)
    small[ROW_BUP : ROW_BUP + 1, :] = sums[0]
    small[ROW_BGATES : ROW_BGATES + 1, :channels] = sums[1]
    small[ROW_BGATES : ROW_BGATES + 1, channels : 2 * channels] = sums[2]
    small[ROW_GAIN : ROW_GAIN + 1, :channels] = sums[3]
    small[ROW_BDOWN : ROW_BDOWN + 1, :channels] = sums[4]
    small[ROW_BCAND : ROW_BCAND + 1, :channels] = sums[5]

    def remote(src, dst, stage, target):
        return pltpu.make_async_remote_copy(
            src_ref=src,
            dst_ref=dst,
            send_sem=red_send.at[stage],
            recv_sem=red_recv.at[stage],
            device_id=target,
            device_id_type=MESH,
        )

    def whole_wait(ref, sem):
        pltpu.make_async_copy(ref, ref, sem).wait()

    def core_copy(region):
        return remote(
            slab.at[pl.ds((1 - core) * HALF + region * REGION, REGION)],
            core_rcv.at[pl.ds(region * REGION, REGION)],
            region,
            sibling,
        )

    store_tiles(slab, CAND_AT, tn(d_cand_s[...], joined_s[...]))
    store_tiles(slab, GATES_AT, tn(joined_s[:, :channels], d_gate_s[...]))
    store_tiles(slab, GATES_AT + 36, tn(prior_s[...], d_gate_s[...]))
    store_tiles(slab, DOWN_AT, tn(d_mix_s[...], hid_s[...]))
    core_copy(0).start()
    store_tiles(slab, UP_AT, tn(normed_s[...], d_pre_s[...]))
    core_copy(1).start()

    def add_cores(region):
        core_copy(region).wait_recv()

        def some(step, carry):
            here = region * REGION + step * 8
            total = slab[pl.ds(core * HALF + here, 8)].astype(F32)
            t1[pl.ds(here, 8)] = (total + core_rcv[pl.ds(here, 8)].astype(F32)).astype(BF16)
            return carry

        lax.fori_loop(0, REGION // 8, some, 0)

    def scatter(region, steps, received, stage):
        for number, step in enumerate(steps):
            x, y, z = moved(*step)
            other = z if region else y
            remote(
                t1.at[pl.ds(region * REGION + (x * side + other) * unit, unit)],
                received.at[number],
                stage,
                device(x, y, z, core),
            ).start()

    add_cores(0)
    scatter(0, xy_steps, xy_rcv, 2)
    add_cores(1)
    scatter(1, xz_steps, xz_rcv, 3)

    receive_halos(2)
    gather(d_sec.at[0], 0, 0, top, "straight")
    gather(d_sec.at[9], 1, 2, bottom, "straight")
    gather(halo.at[2], 0, 3, west, "turned")
    gather(halo.at[3], 1, 1, east, "turned")

    def first_back(i, sums):
        value = d_sec[i + 1]
        d_first = tap(1, 0) * d_sec[i + 2] + tap(1, 1) * value + tap(1, 2) * d_sec[i]
        d_first += jnp.where(place == 0, tap(1, 0) * upright(2, i), 0.0)
        d_first += jnp.where(place == 7, tap(1, 2) * upright(3, i), 0.0)
        d_first = rounded(d_first)
        d_first_s[i] = d_first
        set_columns(d_first, i)
        x_value = x_row(i)
        left, right = column_shifts(x_value, 0, 1, i)
        pairs = (
            (d_first, left),
            (d_first, x_value),
            (d_first, right),
            (value, field[i]),
            (value, field[i + 1]),
            (value, field[i + 2]),
        )
        return tuple(old + jnp.sum(a * c, axis=0) for old, (a, c) in zip(sums, pairs))

    tap_sums = lax.fori_loop(
        0, 8, first_back, tuple(jnp.zeros((SIDE, channels), F32) for _ in range(6))
    )
    put_columns(3)
    start_halos(3)

    for number, tap_sum in enumerate(tap_sums):
        row = ROW_TAPS + number
        small[row : row + 1, :channels] = jnp.sum(tap_sum, axis=0, keepdims=True)
    tile32[...] = jnp.zeros_like(tile32)
    line = 0
    for row, count in SMALL_ROWS:
        for number in range(count):
            tile32[line : line + 1, :] = small[row : row + 1, number * 128 : number * 128 + 128]
            line += 1
    small_c[0] = tile32[...].astype(BF16)
    small_core = remote(small_c.at[0], small_c.at[1], 4, sibling)
    small_core.start()

    def spread_slot(slots, me, steps, stage):
        for step in steps:
            remote(slots.at[me], slots.at[me], stage, offset(*step)).start()

    def sum_slots(slots, stage):
        count = slots.shape[0]
        whole_wait(slots.at[pl.ds(0, count - 1)], red_recv.at[stage])
        total = slots[0].astype(F32)
        for number in range(1, count):
            total += slots[number].astype(F32)
        return total

    def add_scattered(region, at, received, slots, slot, stage):
        whole_wait(received, red_recv.at[stage])
        total = t1[pl.ds(region * REGION + at * unit, unit)].astype(F32)
        for number in range(received.shape[0]):
            total += received[number].astype(F32)
        slots[slot] = total.astype(BF16)

    add_scattered(0, mx * side + ty, xy_rcv, cz, tx, 2)
    spread_slot(cz, tx, z_steps, 5)
    add_scattered(1, mx * side + tx, xz_rcv, cy, ty, 3)
    spread_slot(cy, ty, y_steps, 6)
    small_core.wait_recv()
    small_x[mx] = (small_c[0].astype(F32) + small_c[1].astype(F32)).astype(BF16)
    spread_slot(small_x, mx, x_steps, 7)
    small_y[ty] = sum_slots(small_x, 7).astype(BF16)
    spread_slot(small_y, ty, y_steps, 8)

    base = core * HALF

    def share(region, at, slots, stage, steps, out_stage):
        at = base + region * REGION + at * unit
        gathered[pl.ds(at, unit)] = (sum_slots(slots, stage) * norm_factor).astype(BF16)
        piece = gathered.at[pl.ds(at, unit)]
        for step in steps:
            remote(piece, piece, out_stage, offset(*step)).start()

    share(0, mx * side + ty, cz, 5, xy_steps, 10)
    share(1, mx * side + tx, cy, 6, xz_steps, 11)

    receive_halos(3)
    gather(halo.at[2], 0, 3, west, "straight")
    gather(halo.at[3], 1, 1, east, "straight")
    gather(halo.at[4], 0, 0, top, "turned")
    gather(halo.at[5], 1, 2, bottom, "turned")

    def input_back(i, carry):
        value = d_first_s[i]
        left, right = column_shifts(value, 2, 3, i)
        d_input = tap(0, 0) * right + tap(0, 1) * value + tap(0, 2) * left
        on_top = jnp.where(i == 0, 1.0, 0.0)
        on_bottom = jnp.where(i == 7, 1.0, 0.0)
        d_input += on_top * (tap(0, 0) * halo[4]) + on_bottom * (tap(0, 2) * halo[5])
        at = pl.multiple_of(lax.rem(i + 7, 8) * 96, 96)
        d_mixed = d_mix_s[pl.ds(at, 96), :].astype(F32).reshape(FACES, SIDE, channels)
        gi_out[:, pl.ds(i, 1)] = (
            (d_input + d_mixed).reshape(FACES, 1, SIDE, channels).astype(BF16)
        )
        return carry

    lax.fori_loop(0, 8, input_back, 0)

    small_z[tx] = sum_slots(small_y, 8).astype(BF16)
    spread_slot(small_z, tx, z_steps, 9)
    tile32[...] = sum_slots(small_z, 9) * norm_factor

    def row_at(line, size):
        pieces = [tile32[line + number : line + number + 1, :] for number in range(-(-size // 128))]
        return jnp.concatenate(pieces, axis=1)[:, :size].astype(BF16)

    for axis in range(2):
        for number in range(3):
            taps_out[number, axis : axis + 1, :] = row_at(9 + 2 * (3 * axis + number), channels)
    for out, line in (
        (b_up_out, 0),
        (b_gates_out, 6),
        (gain_out, 21),
        (b_down_out, 23),
        (b_cand_out, 25),
    ):
        out[...] = row_at(line, out.shape[0]).reshape(out.shape)

    def core_back(region):
        piece = gathered.at[pl.ds(base + region * REGION, REGION)]
        return remote(piece, piece, 12 + region, sibling)

    shares = nx * side - 1
    for region in range(2):
        whole_wait(gathered.at[pl.ds(0, unit * shares)], red_recv.at[10 + region])
        core_back(region).start()
    for region in range(2):
        core_back(region).wait_recv()

    def unpack(at, out):
        columns_of_tiles = out.shape[1] // 128
        for row in range(out.shape[0] // 16):
            for column in range(columns_of_tiles):
                out[row * 16 : row * 16 + 16, column * 128 : column * 128 + 128] = gathered[
                    tile_place(at + row * columns_of_tiles + column)
                ]

    unpack(CAND_AT, cand_out)
    unpack(GATES_AT, gates_out)
    unpack(DOWN_AT, down_out)
    unpack(UP_AT, up_out)

    for exchange in range(4):
        finish_halo_sends(exchange)
    for number in range(2):
        pl.when(far_sends[number])(far_copies[number].wait_send)
    small_core.wait_send()
    for region in range(2):
        core_copy(region).wait_send()
        core_back(region).wait_send()
    for ref, stage in (
        (xy_rcv, 2),
        (xz_rcv, 3),
        (cz.at[pl.ds(0, side - 1)], 5),
        (cy.at[pl.ds(0, side - 1)], 6),
        (small_x.at[pl.ds(0, nx - 1)], 7),
        (small_y.at[pl.ds(0, side - 1)], 8),
        (small_z.at[pl.ds(0, side - 1)], 9),
        (gathered.at[pl.ds(0, unit * shares)], 10),
        (gathered.at[pl.ds(0, unit * shares)], 11),
    ):
        whole_wait(ref, red_send.at[stage])


def relay_kernel(*refs):
    count = (len(refs) - 1) // 2
    sems = refs[-1]
    copies = [
        pltpu.make_async_copy(refs[number], refs[count + number], sems.at[number])
        for number in range(count)
    ]
    for copy in copies:
        copy.start()
    for copy in copies:
        copy.wait()


def on_device(
    inputs,
    state,
    cotangent,
    adjacency,
    taps,
    gain,
    w_up,
    b_up,
    w_down,
    b_down,
    w_gates,
    b_gates,
    w_cand,
    b_cand,
):
    channels = inputs.shape[-1]
    wide = w_up.shape[1]
    tokens = FACES * SIDE * SIDE
    lines = FACES * SIDE
    tile_count, date_count = lax.axis_size("tile"), lax.axis_size("date")
    side = 2 ** ((tile_count.bit_length() - 2) // 2)
    x_low = date_count // 2
    nx = 2 * x_low
    unit = REGION // (nx * side)
    norm_factor = float(tokens * tile_count * date_count) ** (-0.5)
    vmem = pl.BlockSpec(memory_space=pltpu.VMEM)
    hbm = pl.BlockSpec(memory_space=pltpu.HBM)
    grid_shape = (FACES, SIDE, SIDE, channels)

    def buf(*shape):
        return pltpu.VMEM(shape, BF16)

    def wide_buf(*shape):
        return pltpu.VMEM(shape, F32)

    def arr(*shape):
        return jax.ShapeDtypeStruct(shape, BF16)

    shares = nx * side - 1
    results = (
        arr(*grid_shape),
        arr(*grid_shape),
        arr(3, 2, channels),
        arr(channels),
        arr(channels, wide),
        arr(wide),
        arr(channels, wide),
        arr(channels),
        arr(2 * channels, 2 * channels),
        arr(2 * channels),
        arr(channels, 2 * channels),
        arr(channels),
    )
    made = pl.pallas_call(
        functools.partial(level_kernel, side, x_low, norm_factor),
        name="level",
        out_shape=results,
        in_specs=[hbm] * 14,
        out_specs=[vmem] * 12,
        scratch_shapes=[
            pltpu.SMEM((4, 2, FACES), jnp.int32),
            buf(*grid_shape),
            buf(*grid_shape),
            buf(*grid_shape),
            buf(3, 2, channels),
            buf(channels),
            buf(wide),
            buf(channels),
            buf(2 * channels),
            buf(channels),
            buf(channels, wide),
            buf(channels, wide),
            buf(2 * channels, 2 * channels),
            buf(channels, 2 * channels),
            wide_buf(16, wide),
            buf(4, 4, lines, channels),
            buf(4, 4, lines, channels),
            buf(2, 2 * lines, channels),
            buf(2, 2 * lines, channels),
            wide_buf(2, 2, FACES, SIDE, channels),
            wide_buf(2, 25, SIDE, channels),
            wide_buf(6, FACES, SIDE, channels),
            wide_buf(4, FACES, SIDE, channels),
            wide_buf(10, FACES, SIDE, channels),
            wide_buf(10, FACES, SIDE, channels),
            wide_buf(8, FACES, SIDE, channels),
            buf(2 * channels, channels),
            buf(2 * channels, channels),
            buf(channels, channels),
            buf(channels, channels),
            buf(tokens, channels),
            buf(tokens, channels),
            buf(tokens, wide),
            buf(tokens, wide),
            buf(tokens, channels),
            buf(tokens, 2 * channels),
            buf(tokens, 2 * channels),
            buf(tokens, channels),
            wide_buf(16, wide),
            wide_buf(32, 128),
            buf(2, 32, 128),
            buf(nx, 32, 128),
            buf(side, 32, 128),
            buf(side, 32, 128),
            buf(2 * HALF, 16, 128),
            buf(HALF, 16, 128),
            buf(HALF, 16, 128),
            buf(shares, unit, 16, 128),
            buf(shares, unit, 16, 128),
            buf(side, unit, 16, 128),
            buf(side, unit, 16, 128),
            buf(2 * HALF, 16, 128),
            pltpu.SemaphoreType.DMA((14,)),
            pltpu.SemaphoreType.DMA((4, 4)),
            pltpu.SemaphoreType.DMA((4, 4)),
            pltpu.SemaphoreType.DMA((2,)),
            pltpu.SemaphoreType.DMA((2,)),
            pltpu.SemaphoreType.DMA((14,)),
            pltpu.SemaphoreType.DMA((14,)),
        ],
        compiler_params=pltpu.CompilerParams(
            collective_id=0, has_side_effects=True, vmem_limit_bytes=60 * 2**20
        ),
    )(
        adjacency.transpose(1, 2, 0),
        inputs.reshape(grid_shape),
        state.reshape(grid_shape),
        cotangent.reshape(grid_shape),
        taps.transpose(1, 0, 2),
        gain,
        b_up,
        b_down,
        b_gates,
        b_cand,
        w_up,
        w_down.T,
        w_gates,
        w_cand.T,
    )
    new_rows, grad_rows, g_taps, g_gain, g_up, g_bup, g_down, g_bdown, g_gates, g_bgates, g_cand, g_bcand = (
        pl.pallas_call(
            relay_kernel,
            name="relay",
            out_shape=results,
            in_specs=[hbm] * 12,
            out_specs=[hbm] * 12,
            scratch_shapes=[pltpu.SemaphoreType.DMA((12,))],
            compiler_params=pltpu.CompilerParams(vmem_limit_bytes=60 * 2**20),
        )(*made)
    )
    return (
        new_rows.reshape(inputs.shape),
        grad_rows.reshape(inputs.shape),
        g_taps.transpose(1, 0, 2),
        g_gain,
        g_up,
        g_bup,
        g_down.T,
        g_bdown,
        g_gates,
        g_bgates,
        g_cand.T,
        g_bcand,
    )


def solution(mesh):
    field = P("tile", "date", None, None, None, None)
    return jax.shard_map(
        on_device,
        mesh=mesh,
        in_specs=(field,) * 3 + (P(),) * 11,
        out_specs=(field,) * 2 + (P(),) * 10,
        check_vma=False,
    )
```

```python
import functools
import math

import jax
import jax.numpy as jnp
from jax import lax
from jax.experimental import pallas as pl
from jax.experimental.pallas import tpu as pltpu
from jax.sharding import PartitionSpec as P

EPSILON = 1e-06
MESH = pl.DeviceIdType.MESH
F32 = jnp.float32
BF16 = jnp.bfloat16
FACES = 12
SIDE = 8
HALF = 128
REGION = 64
TURNED = 4
ZERO_LINE = FACES + TURNED
GELU_A = math.sqrt(2.0 / math.pi)
GELU_B = 0.044715
ROW_BUP, ROW_BGATES, ROW_TAPS, ROW_GAIN, ROW_BDOWN, ROW_BCAND = 0, 1, 2, 8, 9, 10
SMALL_ROWS = ((0, 6), (1, 3)) + tuple((row, 2) for row in range(2, 11))
CAND_AT, GATES_AT, DOWN_AT, UP_AT, SMALL_AT = 0, 36, 108, 180, 252


def nn(left, right):
    return jnp.dot(left, right, preferred_element_type=F32)


def nt(left, right):
    return lax.dot_general(left, right, (((1,), (1,)), ((), ())), preferred_element_type=F32)


def tn(left, right):
    return lax.dot_general(left, right, (((0,), (0,)), ((), ())), preferred_element_type=F32)


def sigmoid(value):
    return 0.5 + 0.5 * jnp.tanh(0.5 * value)


def tile_place(number):
    if 64 <= number < 128:
        return number + 64
    if 128 <= number < 192:
        return number - 64
    return number


def store_tiles(slab, at, matrix):
    rows, columns = matrix.shape
    packed = matrix.astype(BF16)
    across = columns // 128
    for row in range(rows // 16):
        for column in range(across):
            slab[tile_place(at + row * across + column)] = packed[
                row * 16 : row * 16 + 16, column * 128 : column * 128 + 128
            ]


def level_kernel(
    side,
    x_low,
    norm_factor,
    adj_in,
    x_in,
    h_in,
    g_in,
    taps_in,
    gain_in,
    b_up_in,
    b_down_in,
    b_gates_in,
    b_cand_in,
    w_up_in,
    w_down_in,
    w_gates_in,
    w_cand_in,
    ns_out,
    gi_out,
    taps_out,
    gain_out,
    up_out,
    b_up_out,
    down_out,
    b_down_out,
    gates_out,
    b_gates_out,
    cand_out,
    b_cand_out,
    adj,
    x_ref,
    h_ref,
    g_ref,
    taps_ref,
    gain_ref,
    b_up_ref,
    b_down_ref,
    b_gates_ref,
    b_cand_ref,
    w_up,
    w_down_t,
    w_gates,
    w_cand_t,
    par,
    rank_of,
    snd,
    rcv,
    turn_snd,
    turn_rcv,
    far_snd,
    far_rcv,
    far_pool,
    pool,
    halo,
    columns,
    field,
    d_sec,
    d_first_s,
    wg_u,
    wg_r,
    wc_m,
    wc_r,
    prior_s,
    normed_s,
    hid_s,
    d_pre_s,
    d_mix_s,
    d_gate_s,
    joined_s,
    d_cand_s,
    small,
    tile32,
    small_c,
    small_x,
    small_y,
    small_z,
    slab,
    core_rcv,
    t1,
    xy_rcv,
    xz_rcv,
    cz,
    cy,
    gathered,
    load_sem,
    halo_send,
    halo_recv,
    far_send,
    far_recv,
    red_send,
    red_recv,
):
    channels = x_ref.shape[3]
    nx = 2 * x_low
    unit = REGION // (nx * side)
    tile = lax.axis_index("tile")
    date = lax.axis_index("date")
    place_of_tile = lax.div(tile, 2)
    ty, tx = lax.div(place_of_tile, side), lax.rem(place_of_tile, side)
    core = lax.rem(date, 2)
    mx = lax.rem(tile, 2) * x_low + lax.div(date, 2)

    def device(x, y, z, c):
        return ((y * side + z) * 2 + lax.div(x, x_low), lax.rem(x, x_low) * 2 + c)

    def moved(dx, dy, dz):
        x = lax.rem(mx + dx, nx) if dx else mx
        y = lax.rem(ty + dy, side) if dy else ty
        z = lax.rem(tx + dz, side) if dz else tx
        return x, y, z

    def offset(dx, dy, dz):
        return device(*moved(dx, dy, dz), core)

    sibling = device(mx, ty, tx, 1 - core)
    across = device(mx, tx, ty, core)
    top, bottom = ty == 0, ty == side - 1
    west, east = tx == 0, tx == side - 1
    has_across = jnp.logical_and(
        ty != tx,
        jnp.logical_or(jnp.logical_or(top, bottom), jnp.logical_or(west, east)),
    )

    def far(step):
        dx, dy, dz = step
        return min(dx, nx - dx) + min(dy, side - dy) + min(dz, side - dz)

    xy_steps = [(dx, dy, 0) for dx in range(nx) for dy in range(side) if dx or dy]
    xz_steps = [(dx, 0, dz) for dx in range(nx) for dz in range(side) if dx or dz]
    xy_steps.sort(key=far, reverse=True)
    xz_steps.sort(key=far, reverse=True)
    x_steps = [(dx, 0, 0) for dx in range(1, nx)]
    y_steps = [(0, dy, 0) for dy in range(1, side)]
    z_steps = [(0, 0, dz) for dz in range(1, side)]

    barrier = pltpu.get_barrier_semaphore()

    @pl.when(has_across)
    def _():
        pl.semaphore_signal(barrier, inc=1, device_id=across, device_id_type=MESH)

    loads = [
        pltpu.make_async_copy(src, dst, load_sem.at[number])
        for number, (src, dst) in enumerate(
            (
                (x_in, x_ref),
                (taps_in, taps_ref),
                (adj_in, adj),
                (w_gates_in, w_gates),
                (w_cand_in, w_cand_t),
                (gain_in, gain_ref),
                (b_up_in, b_up_ref),
                (b_down_in, b_down_ref),
                (b_gates_in, b_gates_ref),
                (b_cand_in, b_cand_ref),
                (w_up_in, w_up),
                (w_down_in, w_down_t),
                (h_in, h_ref),
                (g_in, g_ref),
            )
        )
    ]
    loads[0].start()
    peers = [offset(*step) for step in sorted(xy_steps, key=far)]
    peers += [offset(*step) for step in sorted(xz_steps, key=far) if step[2]]
    peers.append(sibling)
    for peer in peers:
        pl.semaphore_signal(barrier, inc=1, device_id=peer, device_id_type=MESH)
    for load in loads[1:]:
        load.start()

    def tap(axis, number):
        row = ROW_TAPS + 3 * axis + number
        return par[row : row + 1, :channels].reshape(1, 1, channels)

    def set_columns(value, i):
        columns[0, :, pl.ds(i, 1), :] = value[:, 0:1, :]
        columns[1, :, pl.ds(i, 1), :] = value[:, 7:8, :]

    def rounded(value):
        return value.astype(BF16).astype(F32)

    def put_line(exchange, kind, value):
        snd[exchange, kind] = value.reshape(FACES * SIDE, channels).astype(BF16)

    def put_columns(exchange):
        put_line(exchange, 0, columns[1])
        put_line(exchange, 1, columns[0])

    def put_turned(ref, faces, line_of):
        lines = [line_of(face).astype(F32) for face in faces]
        ref[...] = jnp.concatenate(lines, axis=0).astype(BF16)

    def is_turned(edge, face):
        return adj[edge, 1, face] != (edge + 2) % 4

    loads[0].wait()

    def x_row(i):
        return x_ref[:, pl.ds(i, 1)].astype(F32).reshape(FACES, SIDE, channels)

    def x_lines(i, carry):
        value = x_row(i)
        set_columns(value, i)
        columns[2, :, pl.ds(i, 1), :] = value[:, 1:2, :]
        columns[3, :, pl.ds(i, 1), :] = value[:, 6:7, :]
        return carry

    lax.fori_loop(0, 8, x_lines, 0)
    put_columns(0)

    loads[2].wait()
    turned_faces = []
    for edge in range(4):
        count = jnp.int32(0)
        chosen = [jnp.int32(0)] * TURNED
        for face in range(FACES):
            rank_of[edge, face] = count
            here = is_turned(edge, face)
            chosen = [
                jnp.where(jnp.logical_and(here, count == slot), face, old)
                for slot, old in enumerate(chosen)
            ]
            count = count + jnp.where(here, 1, 0)
        turned_faces.append(chosen)

    put_turned(turn_snd.at[0, 0], turned_faces[0], lambda face: x_ref[face, 0])
    put_turned(turn_snd.at[0, 1], turned_faces[2], lambda face: x_ref[face, 7])
    for which, edge, order in ((0, 3, (0, 2)), (1, 1, (3, 1))):
        for position, column in enumerate(order):
            part = pl.ds(position * TURNED * SIDE, TURNED * SIDE)
            put_turned(
                far_snd.at[which, part],
                turned_faces[edge],
                lambda face, column=column: columns[column, face],
            )

    @pl.when(has_across)
    def _():
        pl.semaphore_wait(barrier, len(peers) + 1)

    @pl.when(jnp.logical_not(has_across))
    def _():
        pl.semaphore_wait(barrier, len(peers))

    row_first = jnp.logical_and(top, jnp.logical_not(west))
    row_last = jnp.logical_and(bottom, jnp.logical_not(east))
    col_first = jnp.logical_and(west, jnp.logical_not(top))
    col_last = jnp.logical_and(east, jnp.logical_not(bottom))
    corners = (jnp.logical_and(top, west), jnp.logical_and(bottom, east))

    far_copies = [
        pltpu.make_async_remote_copy(
            src_ref=far_snd.at[number],
            dst_ref=far_rcv.at[number],
            send_sem=far_send.at[number],
            recv_sem=far_recv.at[number],
            device_id=across,
            device_id_type=MESH,
        )
        for number in range(2)
    ]
    far_sends, far_receives = (col_first, col_last), (row_first, row_last)

    def halo_copies(exchange):
        if exchange in (0, 3):
            ahead, behind = offset(0, 0, 1), offset(0, 0, side - 1)
        else:
            ahead, behind = offset(0, 1, 0), offset(0, side - 1, 0)
        if exchange in (0, 2):
            sends, receives = (row_first, row_last), (col_first, col_last)
        else:
            sends, receives = (col_first, col_last), (row_first, row_last)
        copies = []
        for kind, target in enumerate((ahead, behind, across, across)):
            turns = kind >= 2
            if turns and exchange == 1:
                continue
            number = kind % 2
            copy = pltpu.make_async_remote_copy(
                src_ref=(turn_snd if turns else snd).at[exchange, number],
                dst_ref=(turn_rcv if turns else rcv).at[exchange, number],
                send_sem=halo_send.at[exchange, kind],
                recv_sem=halo_recv.at[exchange, kind],
                device_id=target,
                device_id_type=MESH,
            )
            copies.append(
                (copy, sends[number] if turns else None, receives[number] if turns else None)
            )
        return copies

    def start_halos(exchange):
        for copy, sends, _ in reversed(halo_copies(exchange)):
            if sends is None:
                copy.start()
            else:
                pl.when(sends)(copy.start)

    def finish_halo_sends(exchange):
        for copy, sends, _ in halo_copies(exchange):
            if sends is None:
                copy.wait_send()
            else:
                pl.when(sends)(copy.wait_send)

    def receive_halos(exchange):
        for kind, (copy, _, receives) in enumerate(halo_copies(exchange)):
            number = kind % 2
            if kind < 2:
                copy.wait_recv()
                pool[number, :FACES] = (
                    rcv[exchange, number].astype(F32).reshape(FACES, SIDE, channels)
                )
                continue

            def spread(ref):
                pool[number, FACES:ZERO_LINE] = (
                    ref[exchange, number].astype(F32).reshape(TURNED, SIDE, channels)
                )

            @pl.when(receives)
            def _():
                copy.wait_recv()
                spread(turn_rcv)

            @pl.when(corners[number])
            def _():
                spread(turn_snd)

    def gather(to, which, edge, on_border, mode):
        for face in range(FACES):
            neighbour = adj[edge, 0, face]
            turned = is_turned(edge, face)
            across_line = FACES + rank_of[3 - edge, neighbour]
            if mode == "both":
                there = jnp.where(turned, across_line, neighbour)
                index = jnp.where(on_border, there, face)
            elif mode == "straight":
                index = jnp.where(on_border, jnp.where(turned, ZERO_LINE, neighbour), face)
            else:
                index = jnp.where(jnp.logical_and(on_border, turned), across_line, ZERO_LINE)
            to[face] = pool[which, index]

    def border_lines(to, which, edge, on_border, row):
        def spread(ref):
            far_pool[which, :, :TURNED] = (
                ref[...].astype(F32).reshape(2, TURNED, SIDE, channels)
            )

        @pl.when(far_receives[which])
        def _():
            far_copies[which].wait_recv()
            spread(far_rcv.at[which])

        @pl.when(corners[which])
        def _():
            spread(far_snd.at[which])

        own = x_row(row)
        for face in range(FACES):
            neighbour = adj[edge, 0, face]
            turned = jnp.logical_and(on_border, is_turned(edge, face))
            straight = jnp.where(on_border, jnp.where(turned, ZERO_LINE, neighbour), face)
            slot = rank_of[3 - edge, neighbour]
            low, high = far_pool[which, 0, slot], far_pool[which, 1, slot]
            lines = (own[face], low, high) if edge == 0 else (low, high, own[face])
            made = sum(tap(0, number)[0] * lines[number] for number in range(3))
            to[face] = jnp.where(turned, rounded(made), pool[which, straight])

    place = lax.broadcasted_iota(jnp.int32, (FACES, SIDE, channels), 1)

    def upright(which, i):
        return jnp.broadcast_to(halo[which, :, pl.ds(i, 1), :], (FACES, SIDE, channels))

    def column_shifts(value, west_lines, east_lines, i):
        left = jnp.where(place == 0, upright(west_lines, i), pltpu.roll(value, 1, 1))
        right = jnp.where(place == 7, upright(east_lines, i), pltpu.roll(value, 7, 1))
        return left, right

    start_halos(0)
    for number in range(2):
        pl.when(far_sends[number])(far_copies[number].start)
    pool[...] = jnp.zeros_like(pool)
    far_pool[...] = jnp.zeros_like(far_pool)
    small[...] = jnp.zeros_like(small)
    slab[SMALL_AT : 2 * HALF] = jnp.zeros((2 * HALF - SMALL_AT, 16, 128), BF16)
    for number in (1, 3, 4, 5, 6, 7, 8, 9):
        loads[number].wait()
    for axis in range(2):
        for number in range(3):
            row = ROW_TAPS + 3 * axis + number
            par[row : row + 1, :channels] = taps_ref[number, axis : axis + 1, :].astype(F32)
    for row, ref in (
        (ROW_GAIN, gain_ref),
        (ROW_BUP, b_up_ref),
        (ROW_BDOWN, b_down_ref),
        (ROW_BGATES, b_gates_ref),
        (ROW_BCAND, b_cand_ref),
    ):
        size = ref.shape[0]
        par[row : row + 1, :size] = ref[...].astype(F32).reshape(1, size)
    wg_u[...] = w_gates[:, :channels]
    wg_r[...] = w_gates[:, channels:]
    wc_m[...] = w_cand_t[:, :channels]
    wc_r[...] = w_cand_t[:, channels:]
    for load in loads[10:]:
        load.wait()

    receive_halos(0)
    gather(halo.at[0], 0, 3, west, "both")
    gather(halo.at[1], 1, 1, east, "both")

    def first_pass(i, carry):
        value = x_row(i)
        left, right = column_shifts(value, 0, 1, i)
        first = rounded(tap(0, 0) * left + tap(0, 1) * value + tap(0, 2) * right)
        field[i + 1] = first
        return carry

    lax.fori_loop(0, 8, first_pass, 0)
    put_line(1, 0, field[8])
    put_line(1, 1, field[1])
    start_halos(1)

    def vector(row, start, size):
        return par[row : row + 1, start : start + size]

    def cell(blocks, sums):
        gain = vector(ROW_GAIN, 0, channels)

        def second_row(i):
            return tap(1, 0) * field[i] + tap(1, 1) * field[i + 1] + tap(1, 2) * field[i + 2]

        def row_of(ref):
            return lambda i: ref[:, pl.ds(i, 1)].astype(F32)

        def joint(block, read):
            parts = [read(i).reshape(FACES * SIDE, channels) for i in block[1]]
            return parts[0] if len(parts) == 1 else jnp.concatenate(parts, axis=0)

        def rows(block):
            return pl.ds(pl.multiple_of(block[0] * 96, 96), 96 * len(block[1]))

        states = [{"block": block} for block in blocks]

        def norm(at):
            centred = joint(at["block"], second_row)
            centred = centred - jnp.mean(centred, axis=-1, keepdims=True)
            at["inv"] = lax.rsqrt(jnp.mean(centred * centred, axis=-1, keepdims=True) + EPSILON)
            at["standard"] = centred * at["inv"]
            at["normed"] = (at["standard"] * gain).astype(BF16)
            normed_s[rows(at["block"]), :] = at["normed"]

        def up(at):
            at["pre"] = nn(at["normed"], w_up[...]) + vector(ROW_BUP, 0, w_up.shape[1])

        def bend(at):
            pre = at["pre"]
            square = pre * pre
            curve = jnp.tanh(pre * (GELU_A + (GELU_A * GELU_B) * square))
            rise = 1.0 + curve
            half = 0.5 * pre
            at["hid"] = (half * rise).astype(BF16)
            hid_s[rows(at["block"]), :] = at["hid"]
            at["slope"] = rise * (
                0.5 + half * (1.0 - curve) * (GELU_A + (3.0 * GELU_A * GELU_B) * square)
            )

        def down(at):
            mixed = (
                joint(at["block"], row_of(x_ref))
                + nt(at["hid"], w_down_t[...])
                + vector(ROW_BDOWN, 0, channels)
            )
            at["mixed"] = mixed.astype(BF16)
            joined_s[rows(at["block"]), :channels] = at["mixed"]

        def gates(at):
            mixed = at["mixed"]
            at["prior"] = joint(at["block"], row_of(h_ref))
            prior_b = at["prior"].astype(BF16)
            prior_s[rows(at["block"]), :] = prior_b
            at["reset"] = sigmoid(
                nn(mixed, wg_r[:channels])
                + nn(prior_b, wg_r[channels:])
                + vector(ROW_BGATES, channels, channels)
            )
            at["update"] = sigmoid(
                nn(mixed, wg_u[:channels])
                + nn(prior_b, wg_u[channels:])
                + vector(ROW_BGATES, 0, channels)
            )

        def propose(at):
            reset_state = (at["reset"] * at["prior"]).astype(BF16)
            joined_s[rows(at["block"]), channels:] = reset_state
            at["candidate"] = jnp.tanh(
                nt(at["mixed"], wc_m[...])
                + nt(reset_state, wc_r[...])
                + vector(ROW_BCAND, 0, channels)
            )

        def renew(at):
            update, candidate, prior = at["update"], at["candidate"], at["prior"]
            new = rounded((1.0 - update) * candidate + update * prior)
            for number, i in enumerate(at["block"][1]):
                ns_out[:, pl.ds(i, 1)] = (
                    new[number * 96 : number * 96 + 96]
                    .reshape(FACES, 1, SIDE, channels)
                    .astype(BF16)
                )
            kept = joint(at["block"], row_of(g_ref)) * (1.0 - update)
            at["d_cand"] = (kept * (1.0 - candidate * candidate)).astype(BF16)
            d_cand_s[rows(at["block"]), :] = at["d_cand"]
            at["d_update"] = (kept * (prior - candidate) * update).astype(BF16)
            d_gate_s[rows(at["block"]), :channels] = at["d_update"]

        def gates_back(at):
            reset = at["reset"]
            at["d_reset"] = (
                nn(at["d_cand"], wc_r[...]) * at["prior"] * reset * (1.0 - reset)
            ).astype(BF16)
            d_gate_s[rows(at["block"]), channels:] = at["d_reset"]

        def mixed_back(at):
            at["d_mixed"] = (
                nn(at["d_cand"], wc_m[...])
                + nt(at["d_update"], wg_u[:channels])
                + nt(at["d_reset"], wg_r[:channels])
            ).astype(BF16)
            d_mix_s[rows(at["block"]), :] = at["d_mixed"]

        def hidden_back(at):
            at["d_pre"] = (nn(at["d_mixed"], w_down_t[...]) * at["slope"]).astype(BF16)
            d_pre_s[rows(at["block"]), :] = at["d_pre"]

        def norm_back(at):
            d_normed = nt(at["d_pre"], w_up[...])
            standard = at["standard"]
            d_standard = d_normed * gain
            d_second = rounded(
                at["inv"]
                * (
                    d_standard
                    - jnp.mean(d_standard, axis=-1, keepdims=True)
                    - standard * jnp.mean(d_standard * standard, axis=-1, keepdims=True)
                )
            )
            for number, i in enumerate(at["block"][1]):
                d_sec[i + 1] = d_second[number * 96 : number * 96 + 96].reshape(
                    FACES, SIDE, channels
                )
            at["gain"] = d_normed * standard

        for stage in (
            norm, up, bend, down, gates, propose, renew, gates_back, mixed_back, hidden_back, norm_back,
        ):
            for at in states:
                stage(at)

        def total(value):
            return jnp.sum(value.astype(F32), axis=0, keepdims=True)

        for at in states:
            extras = [
                total(at[name]) for name in ("d_pre", "d_update", "d_reset", "gain", "d_mixed", "d_cand")
            ]
            sums = tuple(old + extra for old, extra in zip(sums, extras))
        return sums

    zeros = jnp.zeros((1, channels), F32)
    sums = (jnp.zeros((1, w_up.shape[1]), F32), zeros, zeros, zeros, zeros, zeros)
    sums = cell([(0, (1, 2, 3, 4, 5, 6))], sums)
    receive_halos(1)
    border_lines(field.at[0], 0, 0, top, 0)
    border_lines(field.at[9], 1, 2, bottom, 7)
    sums = cell([(6, (7, 0))], sums)
    put_line(2, 0, d_sec[8])
    put_line(2, 1, d_sec[1])
    put_turned(turn_snd.at[2, 0], turned_faces[0], lambda face: d_sec[1, face])
    put_turned(turn_snd.at[2, 1], turned_faces[2], lambda face: d_sec[8, face])
    start_halos(2)
    small[ROW_BUP : ROW_BUP + 1, :] = sums[0]
    small[ROW_BGATES : ROW_BGATES + 1, :channels] = sums[1]
    small[ROW_BGATES : ROW_BGATES + 1, channels : 2 * channels] = sums[2]
    small[ROW_GAIN : ROW_GAIN + 1, :channels] = sums[3]
    small[ROW_BDOWN : ROW_BDOWN + 1, :channels] = sums[4]
    small[ROW_BCAND : ROW_BCAND + 1, :channels] = sums[5]

    def remote(src, dst, stage, target):
        return pltpu.make_async_remote_copy(
            src_ref=src,
            dst_ref=dst,
            send_sem=red_send.at[stage],
            recv_sem=red_recv.at[stage],
            device_id=target,
            device_id_type=MESH,
        )

    def whole_wait(ref, sem):
        pltpu.make_async_copy(ref, ref, sem).wait()

    def core_copy(region):
        return remote(
            slab.at[pl.ds((1 - core) * HALF + region * REGION, REGION)],
            core_rcv.at[pl.ds(region * REGION, REGION)],
            region,
            sibling,
        )

    store_tiles(slab, CAND_AT, tn(d_cand_s[...], joined_s[...]))
    store_tiles(slab, GATES_AT, tn(joined_s[:, :channels], d_gate_s[...]))
    store_tiles(slab, GATES_AT + 36, tn(prior_s[...], d_gate_s[...]))
    store_tiles(slab, DOWN_AT, tn(d_mix_s[...], hid_s[...]))
    core_copy(0).start()
    store_tiles(slab, UP_AT, tn(normed_s[...], d_pre_s[...]))
    core_copy(1).start()

    def add_cores(region):
        core_copy(region).wait_recv()

        def some(step, carry):
            here = region * REGION + step * 8
            total = slab[pl.ds(core * HALF + here, 8)].astype(F32)
            t1[pl.ds(here, 8)] = (total + core_rcv[pl.ds(here, 8)].astype(F32)).astype(BF16)
            return carry

        lax.fori_loop(0, REGION // 8, some, 0)

    def scatter(region, steps, received, stage):
        for number, step in enumerate(steps):
            x, y, z = moved(*step)
            other = z if region else y
            remote(
                t1.at[pl.ds(region * REGION + (x * side + other) * unit, unit)],
                received.at[number],
                stage,
                device(x, y, z, core),
            ).start()

    add_cores(0)
    scatter(0, xy_steps, xy_rcv, 2)
    add_cores(1)
    scatter(1, xz_steps, xz_rcv, 3)

    receive_halos(2)
    gather(d_sec.at[0], 0, 0, top, "straight")
    gather(d_sec.at[9], 1, 2, bottom, "straight")
    gather(halo.at[2], 0, 3, west, "turned")
    gather(halo.at[3], 1, 1, east, "turned")

    def first_back(i, sums):
        value = d_sec[i + 1]
        d_first = tap(1, 0) * d_sec[i + 2] + tap(1, 1) * value + tap(1, 2) * d_sec[i]
        d_first += jnp.where(place == 0, tap(1, 0) * upright(2, i), 0.0)
        d_first += jnp.where(place == 7, tap(1, 2) * upright(3, i), 0.0)
        d_first = rounded(d_first)
        d_first_s[i] = d_first
        set_columns(d_first, i)
        x_value = x_row(i)
        left, right = column_shifts(x_value, 0, 1, i)
        pairs = (
            (d_first, left),
            (d_first, x_value),
            (d_first, right),
            (value, field[i]),
            (value, field[i + 1]),
            (value, field[i + 2]),
        )
        return tuple(old + jnp.sum(a * c, axis=0) for old, (a, c) in zip(sums, pairs))

    tap_sums = lax.fori_loop(
        0, 8, first_back, tuple(jnp.zeros((SIDE, channels), F32) for _ in range(6))
    )
    put_columns(3)
    put_turned(turn_snd.at[3, 0], turned_faces[3], lambda face: columns[0, face])
    put_turned(turn_snd.at[3, 1], turned_faces[1], lambda face: columns[1, face])
    start_halos(3)

    for number, tap_sum in enumerate(tap_sums):
        row = ROW_TAPS + number
        small[row : row + 1, :channels] = jnp.sum(tap_sum, axis=0, keepdims=True)
    tile32[...] = jnp.zeros_like(tile32)
    line = 0
    for row, count in SMALL_ROWS:
        for number in range(count):
            tile32[line : line + 1, :] = small[row : row + 1, number * 128 : number * 128 + 128]
            line += 1
    small_c[0] = tile32[...].astype(BF16)
    small_core = remote(small_c.at[0], small_c.at[1], 4, sibling)
    small_core.start()

    def spread_slot(slots, me, steps, stage):
        for step in steps:
            remote(slots.at[me], slots.at[me], stage, offset(*step)).start()

    def sum_slots(slots, stage):
        count = slots.shape[0]
        whole_wait(slots.at[pl.ds(0, count - 1)], red_recv.at[stage])
        total = slots[0].astype(F32)
        for number in range(1, count):
            total += slots[number].astype(F32)
        return total

    def add_scattered(region, at, received, slots, slot, stage):
        whole_wait(received, red_recv.at[stage])
        total = t1[pl.ds(region * REGION + at * unit, unit)].astype(F32)
        for number in range(received.shape[0]):
            total += received[number].astype(F32)
        slots[slot] = total.astype(BF16)

    add_scattered(0, mx * side + ty, xy_rcv, cz, tx, 2)
    spread_slot(cz, tx, z_steps, 5)
    add_scattered(1, mx * side + tx, xz_rcv, cy, ty, 3)
    spread_slot(cy, ty, y_steps, 6)
    small_core.wait_recv()
    small_x[mx] = (small_c[0].astype(F32) + small_c[1].astype(F32)).astype(BF16)
    spread_slot(small_x, mx, x_steps, 7)
    small_y[ty] = sum_slots(small_x, 7).astype(BF16)
    spread_slot(small_y, ty, y_steps, 8)

    base = core * HALF

    def share(region, at, slots, stage, steps, out_stage):
        at = base + region * REGION + at * unit
        gathered[pl.ds(at, unit)] = (sum_slots(slots, stage) * norm_factor).astype(BF16)
        piece = gathered.at[pl.ds(at, unit)]
        for step in steps:
            remote(piece, piece, out_stage, offset(*step)).start()

    share(0, mx * side + ty, cz, 5, xy_steps, 10)
    share(1, mx * side + tx, cy, 6, xz_steps, 11)

    receive_halos(3)
    gather(halo.at[2], 0, 3, west, "straight")
    gather(halo.at[3], 1, 1, east, "straight")
    gather(halo.at[4], 0, 0, top, "turned")
    gather(halo.at[5], 1, 2, bottom, "turned")

    def input_back(i, carry):
        value = d_first_s[i]
        left, right = column_shifts(value, 2, 3, i)
        d_input = tap(0, 0) * right + tap(0, 1) * value + tap(0, 2) * left
        on_top = jnp.where(i == 0, 1.0, 0.0)
        on_bottom = jnp.where(i == 7, 1.0, 0.0)
        d_input += on_top * (tap(0, 0) * halo[4]) + on_bottom * (tap(0, 2) * halo[5])
        at = pl.multiple_of(lax.rem(i + 7, 8) * 96, 96)
        d_mixed = d_mix_s[pl.ds(at, 96), :].astype(F32).reshape(FACES, SIDE, channels)
        gi_out[:, pl.ds(i, 1)] = (
            (d_input + d_mixed).reshape(FACES, 1, SIDE, channels).astype(BF16)
        )
        return carry

    lax.fori_loop(0, 8, input_back, 0)

    small_z[tx] = sum_slots(small_y, 8).astype(BF16)
    spread_slot(small_z, tx, z_steps, 9)
    tile32[...] = sum_slots(small_z, 9) * norm_factor

    def row_at(line, size):
        pieces = [tile32[line + number : line + number + 1, :] for number in range(-(-size // 128))]
        return jnp.concatenate(pieces, axis=1)[:, :size].astype(BF16)

    for axis in range(2):
        for number in range(3):
            taps_out[number, axis : axis + 1, :] = row_at(9 + 2 * (3 * axis + number), channels)
    for out, line in (
        (b_up_out, 0),
        (b_gates_out, 6),
        (gain_out, 21),
        (b_down_out, 23),
        (b_cand_out, 25),
    ):
        out[...] = row_at(line, out.shape[0]).reshape(out.shape)

    def core_back(region):
        piece = gathered.at[pl.ds(base + region * REGION, REGION)]
        return remote(piece, piece, 12 + region, sibling)

    shares = nx * side - 1
    for region in range(2):
        whole_wait(gathered.at[pl.ds(0, unit * shares)], red_recv.at[10 + region])
        core_back(region).start()
    for region in range(2):
        core_back(region).wait_recv()

    def unpack(at, out):
        columns_of_tiles = out.shape[1] // 128
        for row in range(out.shape[0] // 16):
            for column in range(columns_of_tiles):
                out[row * 16 : row * 16 + 16, column * 128 : column * 128 + 128] = gathered[
                    tile_place(at + row * columns_of_tiles + column)
                ]

    unpack(CAND_AT, cand_out)
    unpack(GATES_AT, gates_out)
    unpack(DOWN_AT, down_out)
    unpack(UP_AT, up_out)

    for exchange in range(4):
        finish_halo_sends(exchange)
    for number in range(2):
        pl.when(far_sends[number])(far_copies[number].wait_send)
    small_core.wait_send()
    for region in range(2):
        core_copy(region).wait_send()
        core_back(region).wait_send()
    for ref, stage in (
        (xy_rcv, 2),
        (xz_rcv, 3),
        (cz.at[pl.ds(0, side - 1)], 5),
        (cy.at[pl.ds(0, side - 1)], 6),
        (small_x.at[pl.ds(0, nx - 1)], 7),
        (small_y.at[pl.ds(0, side - 1)], 8),
        (small_z.at[pl.ds(0, side - 1)], 9),
        (gathered.at[pl.ds(0, unit * shares)], 10),
        (gathered.at[pl.ds(0, unit * shares)], 11),
    ):
        whole_wait(ref, red_send.at[stage])


def relay_kernel(count, *refs):
    loads, stores = refs[3 * count :]
    ins = [
        pltpu.make_async_copy(refs[number], refs[2 * count + number], loads.at[number])
        for number in range(count)
    ]
    outs = [
        pltpu.make_async_copy(refs[2 * count + number], refs[count + number], stores.at[number])
        for number in range(count)
    ]
    for copy in ins:
        copy.start()
    for load, store in zip(ins, outs):
        load.wait()
        store.start()
    for copy in outs:
        copy.wait()


def on_device(
    inputs,
    state,
    cotangent,
    adjacency,
    taps,
    gain,
    w_up,
    b_up,
    w_down,
    b_down,
    w_gates,
    b_gates,
    w_cand,
    b_cand,
):
    channels = inputs.shape[-1]
    wide = w_up.shape[1]
    tokens = FACES * SIDE * SIDE
    lines = FACES * SIDE
    tile_count, date_count = lax.axis_size("tile"), lax.axis_size("date")
    side = 2 ** ((tile_count.bit_length() - 2) // 2)
    x_low = date_count // 2
    nx = 2 * x_low
    unit = REGION // (nx * side)
    norm_factor = float(tokens * tile_count * date_count) ** (-0.5)
    vmem = pl.BlockSpec(memory_space=pltpu.VMEM)
    hbm = pl.BlockSpec(memory_space=pltpu.HBM)
    grid_shape = (FACES, SIDE, SIDE, channels)

    def buf(*shape):
        return pltpu.VMEM(shape, BF16)

    def wide_buf(*shape):
        return pltpu.VMEM(shape, F32)

    def arr(*shape):
        return jax.ShapeDtypeStruct(shape, BF16)

    shares = nx * side - 1
    results = (
        arr(*grid_shape),
        arr(*grid_shape),
        arr(3, 2, channels),
        arr(channels),
        arr(channels, wide),
        arr(wide),
        arr(channels, wide),
        arr(channels),
        arr(2 * channels, 2 * channels),
        arr(2 * channels),
        arr(channels, 2 * channels),
        arr(channels),
    )
    made = pl.pallas_call(
        functools.partial(level_kernel, side, x_low, norm_factor),
        name="level",
        out_shape=results,
        in_specs=[hbm] * 14,
        out_specs=[vmem] * 12,
        scratch_shapes=[
            pltpu.SMEM((4, 2, FACES), jnp.int32),
            buf(*grid_shape),
            buf(*grid_shape),
            buf(*grid_shape),
            buf(3, 2, channels),
            buf(channels),
            buf(wide),
            buf(channels),
            buf(2 * channels),
            buf(channels),
            buf(channels, wide),
            buf(channels, wide),
            buf(2 * channels, 2 * channels),
            buf(channels, 2 * channels),
            wide_buf(16, wide),
            pltpu.SMEM((4, FACES), jnp.int32),
            buf(4, 2, lines, channels),
            buf(4, 2, lines, channels),
            buf(4, 2, TURNED * SIDE, channels),
            buf(4, 2, TURNED * SIDE, channels),
            buf(2, 2 * TURNED * SIDE, channels),
            buf(2, 2 * TURNED * SIDE, channels),
            wide_buf(2, 2, TURNED + 1, SIDE, channels),
            wide_buf(2, ZERO_LINE + 1, SIDE, channels),
            wide_buf(6, FACES, SIDE, channels),
            wide_buf(4, FACES, SIDE, channels),
            wide_buf(10, FACES, SIDE, channels),
            wide_buf(10, FACES, SIDE, channels),
            wide_buf(8, FACES, SIDE, channels),
            buf(2 * channels, channels),
            buf(2 * channels, channels),
            buf(channels, channels),
            buf(channels, channels),
            buf(tokens, channels),
            buf(tokens, channels),
            buf(tokens, wide),
            buf(tokens, wide),
            buf(tokens, channels),
            buf(tokens, 2 * channels),
            buf(tokens, 2 * channels),
            buf(tokens, channels),
            wide_buf(16, wide),
            wide_buf(32, 128),
            buf(2, 32, 128),
            buf(nx, 32, 128),
            buf(side, 32, 128),
            buf(side, 32, 128),
            buf(2 * HALF, 16, 128),
            buf(HALF, 16, 128),
            buf(HALF, 16, 128),
            buf(shares, unit, 16, 128),
            buf(shares, unit, 16, 128),
            buf(side, unit, 16, 128),
            buf(side, unit, 16, 128),
            buf(2 * HALF, 16, 128),
            pltpu.SemaphoreType.DMA((14,)),
            pltpu.SemaphoreType.DMA((4, 4)),
            pltpu.SemaphoreType.DMA((4, 4)),
            pltpu.SemaphoreType.DMA((2,)),
            pltpu.SemaphoreType.DMA((2,)),
            pltpu.SemaphoreType.DMA((14,)),
            pltpu.SemaphoreType.DMA((14,)),
        ],
        compiler_params=pltpu.CompilerParams(
            collective_id=0, has_side_effects=True, vmem_limit_bytes=60 * 2**20
        ),
    )(
        adjacency.transpose(1, 2, 0),
        inputs.reshape(grid_shape),
        state.reshape(grid_shape),
        cotangent.reshape(grid_shape),
        taps.transpose(1, 0, 2),
        gain,
        b_up,
        b_down,
        b_gates,
        b_cand,
        w_up,
        w_down.T,
        w_gates,
        w_cand.T,
    )
    new_rows, grad_rows, g_taps, g_gain, g_up, g_bup, g_down, g_bdown, g_gates, g_bgates, g_cand, g_bcand = (
        pl.pallas_call(
            functools.partial(relay_kernel, len(results)),
            name="relay",
            out_shape=results,
            in_specs=[hbm] * 12,
            out_specs=[hbm] * 12,
            scratch_shapes=[buf(*result.shape) for result in results]
            + [pltpu.SemaphoreType.DMA((12,))] * 2,
            compiler_params=pltpu.CompilerParams(vmem_limit_bytes=60 * 2**20),
        )(*made)
    )
    return (
        new_rows.reshape(inputs.shape),
        grad_rows.reshape(inputs.shape),
        g_taps.transpose(1, 0, 2),
        g_gain,
        g_up,
        g_bup,
        g_down.T,
        g_bdown,
        g_gates,
        g_bgates,
        g_cand.T,
        g_bcand,
    )


def solution(mesh):
    field = P("tile", "date", None, None, None, None)
    return jax.shard_map(
        on_device,
        mesh=mesh,
        in_specs=(field,) * 3 + (P(),) * 11,
        out_specs=(field,) * 2 + (P(),) * 10,
        check_vma=False,
    )
```

```python
import functools
import math

import jax
import jax.numpy as jnp
from jax import lax
from jax.experimental import pallas as pl
from jax.experimental.pallas import tpu as pltpu
from jax.sharding import PartitionSpec as P

EPSILON = 1e-06
MESH = pl.DeviceIdType.MESH
F32 = jnp.float32
BF16 = jnp.bfloat16
FACES = 12
SIDE = 8
HALF = 128
REGION = 64
TURNED = 4
ZERO_LINE = FACES + TURNED
GELU_A = math.sqrt(2.0 / math.pi)
GELU_B = 0.044715
ROW_BUP, ROW_BGATES, ROW_TAPS, ROW_GAIN, ROW_BDOWN, ROW_BCAND = 0, 1, 2, 8, 9, 10
SMALL_ROWS = ((0, 6), (1, 3)) + tuple((row, 2) for row in range(2, 11))
CAND_AT, GATES_AT, DOWN_AT, UP_AT, SMALL_AT = 0, 36, 108, 180, 252


def nn(left, right):
    return jnp.dot(left, right, preferred_element_type=F32)


def nt(left, right):
    return lax.dot_general(left, right, (((1,), (1,)), ((), ())), preferred_element_type=F32)


def tn(left, right):
    return lax.dot_general(left, right, (((0,), (0,)), ((), ())), preferred_element_type=F32)


def sigmoid(value):
    return 0.5 + 0.5 * jnp.tanh(0.5 * value)


def tile_place(number):
    if 64 <= number < 128:
        return number + 64
    if 128 <= number < 192:
        return number - 64
    return number


def store_tiles(slab, at, matrix):
    rows, columns = matrix.shape
    packed = matrix.astype(BF16)
    across = columns // 128
    for row in range(rows // 16):
        for column in range(across):
            slab[tile_place(at + row * across + column)] = packed[
                row * 16 : row * 16 + 16, column * 128 : column * 128 + 128
            ]


def level_kernel(
    side,
    x_low,
    norm_factor,
    adj_in,
    x_in,
    h_in,
    g_in,
    taps_in,
    gain_in,
    b_up_in,
    b_down_in,
    b_gates_in,
    b_cand_in,
    w_up_in,
    w_down_in,
    w_gates_in,
    w_cand_in,
    ns_out,
    gi_out,
    taps_out,
    gain_out,
    up_out,
    b_up_out,
    down_out,
    b_down_out,
    gates_out,
    b_gates_out,
    cand_out,
    b_cand_out,
    adj,
    x_ref,
    h_ref,
    g_ref,
    taps_ref,
    gain_ref,
    b_up_ref,
    b_down_ref,
    b_gates_ref,
    b_cand_ref,
    w_up,
    w_down_t,
    w_gates,
    w_cand_t,
    par,
    rank_of,
    snd,
    rcv,
    turn_snd,
    turn_rcv,
    far_snd,
    far_rcv,
    far_pool,
    pool,
    halo,
    columns,
    field,
    d_sec,
    d_first_s,
    wg_u,
    wg_r,
    wc_m,
    wc_r,
    prior_s,
    normed_s,
    hid_s,
    d_pre_s,
    d_mix_s,
    d_gate_s,
    joined_s,
    d_cand_s,
    small,
    tile32,
    small_c,
    small_x,
    small_y,
    small_z,
    slab,
    core_rcv,
    t1,
    xy_rcv,
    xz_rcv,
    cz,
    cy,
    gathered,
    load_sem,
    halo_send,
    halo_recv,
    far_send,
    far_recv,
    red_send,
    red_recv,
):
    channels = x_ref.shape[3]
    nx = 2 * x_low
    unit = REGION // (nx * side)
    tile = lax.axis_index("tile")
    date = lax.axis_index("date")
    place_of_tile = lax.div(tile, 2)
    ty, tx = lax.div(place_of_tile, side), lax.rem(place_of_tile, side)
    core = lax.rem(date, 2)
    mx = lax.rem(tile, 2) * x_low + lax.div(date, 2)

    def device(x, y, z, c):
        return ((y * side + z) * 2 + lax.div(x, x_low), lax.rem(x, x_low) * 2 + c)

    x_at = [lax.rem(mx + step, nx) if step else mx for step in range(nx)]
    y_at = [lax.rem(ty + step, side) if step else ty for step in range(side)]
    z_at = [lax.rem(tx + step, side) if step else tx for step in range(side)]
    x_tile = [lax.div(x, x_low) for x in x_at]
    x_date = [lax.rem(x, x_low) * 2 + core for x in x_at]
    y_tile = [y * (2 * side) for y in y_at]
    z_tile = [z * 2 for z in z_at]
    xy_tile = [[x + y for y in y_tile] for x in x_tile]
    xz_tile = [[x + z for z in z_tile] for x in x_tile]

    def offset(dx, dy, dz):
        if not dz:
            return xy_tile[dx][dy] + z_tile[0], x_date[dx]
        if not dy:
            return xz_tile[dx][dz] + y_tile[0], x_date[dx]
        return x_tile[dx] + y_tile[dy] + z_tile[dz], x_date[dx]

    sibling = device(mx, ty, tx, 1 - core)
    across = device(mx, tx, ty, core)
    top, bottom = ty == 0, ty == side - 1
    west, east = tx == 0, tx == side - 1
    has_across = jnp.logical_and(
        ty != tx,
        jnp.logical_or(jnp.logical_or(top, bottom), jnp.logical_or(west, east)),
    )

    def far(step):
        dx, dy, dz = step
        return min(dx, nx - dx) + min(dy, side - dy) + min(dz, side - dz)

    xy_steps = [(dx, dy, 0) for dx in range(nx) for dy in range(side) if dx or dy]
    xz_steps = [(dx, 0, dz) for dx in range(nx) for dz in range(side) if dx or dz]
    xy_steps.sort(key=far, reverse=True)
    xz_steps.sort(key=far, reverse=True)
    x_steps = [(dx, 0, 0) for dx in range(1, nx)]
    y_steps = [(0, dy, 0) for dy in range(1, side)]
    z_steps = [(0, 0, dz) for dz in range(1, side)]

    barrier = pltpu.get_barrier_semaphore()

    @pl.when(has_across)
    def _():
        pl.semaphore_signal(barrier, inc=1, device_id=across, device_id_type=MESH)

    loads = [
        pltpu.make_async_copy(src, dst, load_sem.at[number])
        for number, (src, dst) in enumerate(
            (
                (x_in, x_ref),
                (taps_in, taps_ref),
                (adj_in, adj),
                (w_gates_in, w_gates),
                (w_cand_in, w_cand_t),
                (gain_in, gain_ref),
                (b_up_in, b_up_ref),
                (b_down_in, b_down_ref),
                (b_gates_in, b_gates_ref),
                (b_cand_in, b_cand_ref),
                (w_up_in, w_up),
                (w_down_in, w_down_t),
                (h_in, h_ref),
                (g_in, g_ref),
            )
        )
    ]
    loads[0].start()
    peers = [offset(*step) for step in sorted(xy_steps, key=far)]
    peers += [offset(*step) for step in sorted(xz_steps, key=far) if step[2]]
    peers.append(sibling)
    for peer in peers:
        pl.semaphore_signal(barrier, inc=1, device_id=peer, device_id_type=MESH)
    for load in loads[1:]:
        load.start()

    def tap(axis, number):
        row = ROW_TAPS + 3 * axis + number
        return par[row : row + 1, :channels].reshape(1, 1, channels)

    def set_columns(value, i):
        columns[0, :, pl.ds(i, 1), :] = value[:, 0:1, :]
        columns[1, :, pl.ds(i, 1), :] = value[:, 7:8, :]

    def rounded(value):
        return value.astype(BF16).astype(F32)

    def put_line(exchange, kind, value):
        snd[exchange, kind] = value.reshape(FACES * SIDE, channels).astype(BF16)

    def put_columns(exchange):
        put_line(exchange, 0, columns[1])
        put_line(exchange, 1, columns[0])

    def put_turned(ref, faces, line_of):
        lines = [line_of(face).astype(F32) for face in faces]
        ref[...] = jnp.concatenate(lines, axis=0).astype(BF16)

    def is_turned(edge, face):
        return adj[edge, 1, face] != (edge + 2) % 4

    loads[0].wait()

    def x_row(i):
        return x_ref[:, pl.ds(i, 1)].astype(F32).reshape(FACES, SIDE, channels)

    def x_lines(i, carry):
        value = x_row(i)
        set_columns(value, i)
        columns[2, :, pl.ds(i, 1), :] = value[:, 1:2, :]
        columns[3, :, pl.ds(i, 1), :] = value[:, 6:7, :]
        return carry

    lax.fori_loop(0, 8, x_lines, 0)
    put_columns(0)

    loads[2].wait()
    turned_faces = []
    for edge in range(4):
        count = jnp.int32(0)
        chosen = [jnp.int32(0)] * TURNED
        for face in range(FACES):
            rank_of[edge, face] = count
            here = is_turned(edge, face)
            chosen = [
                jnp.where(jnp.logical_and(here, count == slot), face, old)
                for slot, old in enumerate(chosen)
            ]
            count = count + jnp.where(here, 1, 0)
        turned_faces.append(chosen)

    put_turned(turn_snd.at[0, 0], turned_faces[0], lambda face: x_ref[face, 0])
    put_turned(turn_snd.at[0, 1], turned_faces[2], lambda face: x_ref[face, 7])
    for which, edge, order in ((0, 3, (0, 2)), (1, 1, (3, 1))):
        for position, column in enumerate(order):
            part = pl.ds(position * TURNED * SIDE, TURNED * SIDE)
            put_turned(
                far_snd.at[which, part],
                turned_faces[edge],
                lambda face, column=column: columns[column, face],
            )

    @pl.when(has_across)
    def _():
        pl.semaphore_wait(barrier, len(peers) + 1)

    @pl.when(jnp.logical_not(has_across))
    def _():
        pl.semaphore_wait(barrier, len(peers))

    row_first = jnp.logical_and(top, jnp.logical_not(west))
    row_last = jnp.logical_and(bottom, jnp.logical_not(east))
    col_first = jnp.logical_and(west, jnp.logical_not(top))
    col_last = jnp.logical_and(east, jnp.logical_not(bottom))
    corners = (jnp.logical_and(top, west), jnp.logical_and(bottom, east))

    far_copies = [
        pltpu.make_async_remote_copy(
            src_ref=far_snd.at[number],
            dst_ref=far_rcv.at[number],
            send_sem=far_send.at[number],
            recv_sem=far_recv.at[number],
            device_id=across,
            device_id_type=MESH,
        )
        for number in range(2)
    ]
    far_sends, far_receives = (col_first, col_last), (row_first, row_last)

    def halo_copies(exchange):
        if exchange in (0, 3):
            ahead, behind = offset(0, 0, 1), offset(0, 0, side - 1)
        else:
            ahead, behind = offset(0, 1, 0), offset(0, side - 1, 0)
        if exchange in (0, 2):
            sends, receives = (row_first, row_last), (col_first, col_last)
        else:
            sends, receives = (col_first, col_last), (row_first, row_last)
        copies = []
        for kind, target in enumerate((ahead, behind, across, across)):
            turns = kind >= 2
            if turns and exchange == 1:
                continue
            number = kind % 2
            copy = pltpu.make_async_remote_copy(
                src_ref=(turn_snd if turns else snd).at[exchange, number],
                dst_ref=(turn_rcv if turns else rcv).at[exchange, number],
                send_sem=halo_send.at[exchange, kind],
                recv_sem=halo_recv.at[exchange, kind],
                device_id=target,
                device_id_type=MESH,
            )
            copies.append(
                (copy, sends[number] if turns else None, receives[number] if turns else None)
            )
        return copies

    def start_halos(exchange):
        for copy, sends, _ in reversed(halo_copies(exchange)):
            if sends is None:
                copy.start()
            else:
                pl.when(sends)(copy.start)

    def finish_halo_sends(exchange):
        for copy, sends, _ in halo_copies(exchange):
            if sends is None:
                copy.wait_send()
            else:
                pl.when(sends)(copy.wait_send)

    def receive_halos(exchange):
        for kind, (copy, _, receives) in enumerate(halo_copies(exchange)):
            number = kind % 2
            if kind < 2:
                copy.wait_recv()
                pool[number, :FACES] = (
                    rcv[exchange, number].astype(F32).reshape(FACES, SIDE, channels)
                )
                continue

            def spread(ref):
                pool[number, FACES:ZERO_LINE] = (
                    ref[exchange, number].astype(F32).reshape(TURNED, SIDE, channels)
                )

            @pl.when(receives)
            def _():
                copy.wait_recv()
                spread(turn_rcv)

            @pl.when(corners[number])
            def _():
                spread(turn_snd)

    def gather(to, which, edge, on_border, mode):
        for face in range(FACES):
            neighbour = adj[edge, 0, face]
            turned = is_turned(edge, face)
            across_line = FACES + rank_of[3 - edge, neighbour]
            if mode == "both":
                there = jnp.where(turned, across_line, neighbour)
                index = jnp.where(on_border, there, face)
            elif mode == "straight":
                index = jnp.where(on_border, jnp.where(turned, ZERO_LINE, neighbour), face)
            else:
                index = jnp.where(jnp.logical_and(on_border, turned), across_line, ZERO_LINE)
            to[face] = pool[which, index]

    def border_lines(to, which, edge, on_border, row):
        def spread(ref):
            far_pool[which, :, :TURNED] = (
                ref[...].astype(F32).reshape(2, TURNED, SIDE, channels)
            )

        @pl.when(far_receives[which])
        def _():
            far_copies[which].wait_recv()
            spread(far_rcv.at[which])

        @pl.when(corners[which])
        def _():
            spread(far_snd.at[which])

        own = x_row(row)
        for face in range(FACES):
            neighbour = adj[edge, 0, face]
            turned = jnp.logical_and(on_border, is_turned(edge, face))
            straight = jnp.where(on_border, jnp.where(turned, ZERO_LINE, neighbour), face)
            slot = rank_of[3 - edge, neighbour]
            low, high = far_pool[which, 0, slot], far_pool[which, 1, slot]
            lines = (own[face], low, high) if edge == 0 else (low, high, own[face])
            made = sum(tap(0, number)[0] * lines[number] for number in range(3))
            to[face] = jnp.where(turned, rounded(made), pool[which, straight])

    place = lax.broadcasted_iota(jnp.int32, (FACES, SIDE, channels), 1)

    def upright(which, i):
        return jnp.broadcast_to(halo[which, :, pl.ds(i, 1), :], (FACES, SIDE, channels))

    def column_shifts(value, west_lines, east_lines, i):
        left = jnp.where(place == 0, upright(west_lines, i), pltpu.roll(value, 1, 1))
        right = jnp.where(place == 7, upright(east_lines, i), pltpu.roll(value, 7, 1))
        return left, right

    start_halos(0)
    for number in range(2):
        pl.when(far_sends[number])(far_copies[number].start)
    pool[...] = jnp.zeros_like(pool)
    far_pool[...] = jnp.zeros_like(far_pool)
    small[...] = jnp.zeros_like(small)
    slab[SMALL_AT : 2 * HALF] = jnp.zeros((2 * HALF - SMALL_AT, 16, 128), BF16)
    for number in (1, 3, 4, 5, 6, 7, 8, 9):
        loads[number].wait()
    for axis in range(2):
        for number in range(3):
            row = ROW_TAPS + 3 * axis + number
            par[row : row + 1, :channels] = taps_ref[number, axis : axis + 1, :].astype(F32)
    for row, ref in (
        (ROW_GAIN, gain_ref),
        (ROW_BUP, b_up_ref),
        (ROW_BDOWN, b_down_ref),
        (ROW_BGATES, b_gates_ref),
        (ROW_BCAND, b_cand_ref),
    ):
        size = ref.shape[0]
        par[row : row + 1, :size] = ref[...].astype(F32).reshape(1, size)
    wg_u[...] = w_gates[:, :channels]
    wg_r[...] = w_gates[:, channels:]
    wc_m[...] = w_cand_t[:, :channels]
    wc_r[...] = w_cand_t[:, channels:]
    for load in loads[10:]:
        load.wait()

    receive_halos(0)
    gather(halo.at[0], 0, 3, west, "both")
    gather(halo.at[1], 1, 1, east, "both")

    def first_pass(i, carry):
        value = x_row(i)
        left, right = column_shifts(value, 0, 1, i)
        first = rounded(tap(0, 0) * left + tap(0, 1) * value + tap(0, 2) * right)
        field[i + 1] = first
        return carry

    lax.fori_loop(0, 8, first_pass, 0)
    put_line(1, 0, field[8])
    put_line(1, 1, field[1])
    start_halos(1)

    def vector(row, start, size):
        return par[row : row + 1, start : start + size]

    def cell(blocks, sums, before_norm_back=None):
        gain = vector(ROW_GAIN, 0, channels)

        def second_row(i):
            return tap(1, 0) * field[i] + tap(1, 1) * field[i + 1] + tap(1, 2) * field[i + 2]

        def row_of(ref):
            return lambda i: ref[:, pl.ds(i, 1)].astype(F32)

        def joint(block, read):
            parts = [read(i).reshape(FACES * SIDE, channels) for i in block[1]]
            return parts[0] if len(parts) == 1 else jnp.concatenate(parts, axis=0)

        def rows(block):
            return pl.ds(pl.multiple_of(block[0] * 96, 96), 96 * len(block[1]))

        states = [{"block": block} for block in blocks]

        def norm(at):
            centred = joint(at["block"], second_row)
            centred = centred - jnp.mean(centred, axis=-1, keepdims=True)
            at["inv"] = lax.rsqrt(jnp.mean(centred * centred, axis=-1, keepdims=True) + EPSILON)
            at["standard"] = centred * at["inv"]
            at["normed"] = (at["standard"] * gain).astype(BF16)
            normed_s[rows(at["block"]), :] = at["normed"]

        def up(at):
            at["pre"] = nn(at["normed"], w_up[...]) + vector(ROW_BUP, 0, w_up.shape[1])

        def bend(at):
            pre = at["pre"]
            square = pre * pre
            curve = jnp.tanh(pre * (GELU_A + (GELU_A * GELU_B) * square))
            rise = 1.0 + curve
            half = 0.5 * pre
            at["hid"] = (half * rise).astype(BF16)
            hid_s[rows(at["block"]), :] = at["hid"]
            at["slope"] = rise * (
                0.5 + half * (1.0 - curve) * (GELU_A + (3.0 * GELU_A * GELU_B) * square)
            )

        def down(at):
            mixed = (
                joint(at["block"], row_of(x_ref))
                + nt(at["hid"], w_down_t[...])
                + vector(ROW_BDOWN, 0, channels)
            )
            at["mixed"] = mixed.astype(BF16)
            joined_s[rows(at["block"]), :channels] = at["mixed"]

        def gates(at):
            mixed = at["mixed"]
            at["prior"] = joint(at["block"], row_of(h_ref))
            prior_b = at["prior"].astype(BF16)
            prior_s[rows(at["block"]), :] = prior_b
            at["reset"] = sigmoid(
                nn(mixed, wg_r[:channels])
                + nn(prior_b, wg_r[channels:])
                + vector(ROW_BGATES, channels, channels)
            )
            at["update"] = sigmoid(
                nn(mixed, wg_u[:channels])
                + nn(prior_b, wg_u[channels:])
                + vector(ROW_BGATES, 0, channels)
            )

        def propose(at):
            reset_state = (at["reset"] * at["prior"]).astype(BF16)
            joined_s[rows(at["block"]), channels:] = reset_state
            at["candidate"] = jnp.tanh(
                nt(at["mixed"], wc_m[...])
                + nt(reset_state, wc_r[...])
                + vector(ROW_BCAND, 0, channels)
            )

        def renew(at):
            update, candidate, prior = at["update"], at["candidate"], at["prior"]
            new = rounded((1.0 - update) * candidate + update * prior)
            for number, i in enumerate(at["block"][1]):
                ns_out[:, pl.ds(i, 1)] = (
                    new[number * 96 : number * 96 + 96]
                    .reshape(FACES, 1, SIDE, channels)
                    .astype(BF16)
                )
            kept = joint(at["block"], row_of(g_ref)) * (1.0 - update)
            at["d_cand"] = (kept * (1.0 - candidate * candidate)).astype(BF16)
            d_cand_s[rows(at["block"]), :] = at["d_cand"]
            at["d_update"] = (kept * (prior - candidate) * update).astype(BF16)
            d_gate_s[rows(at["block"]), :channels] = at["d_update"]

        def gates_back(at):
            reset = at["reset"]
            at["d_reset"] = (
                nn(at["d_cand"], wc_r[...]) * at["prior"] * reset * (1.0 - reset)
            ).astype(BF16)
            d_gate_s[rows(at["block"]), channels:] = at["d_reset"]

        def mixed_back(at):
            at["d_mixed"] = (
                nn(at["d_cand"], wc_m[...])
                + nt(at["d_update"], wg_u[:channels])
                + nt(at["d_reset"], wg_r[:channels])
            ).astype(BF16)
            d_mix_s[rows(at["block"]), :] = at["d_mixed"]

        def hidden_back(at):
            at["d_pre"] = (nn(at["d_mixed"], w_down_t[...]) * at["slope"]).astype(BF16)
            d_pre_s[rows(at["block"]), :] = at["d_pre"]

        def norm_back(at):
            d_normed = nt(at["d_pre"], w_up[...])
            standard = at["standard"]
            d_standard = d_normed * gain
            d_second = rounded(
                at["inv"]
                * (
                    d_standard
                    - jnp.mean(d_standard, axis=-1, keepdims=True)
                    - standard * jnp.mean(d_standard * standard, axis=-1, keepdims=True)
                )
            )
            for number, i in enumerate(at["block"][1]):
                d_sec[i + 1] = d_second[number * 96 : number * 96 + 96].reshape(
                    FACES, SIDE, channels
                )
            at["gain"] = d_normed * standard

        for stage in (
            norm, up, bend, down, gates, propose, renew, gates_back, mixed_back, hidden_back,
        ):
            for at in states:
                stage(at)
        if before_norm_back is not None:
            before_norm_back()
        for at in states:
            norm_back(at)

        def total(value):
            return jnp.sum(value.astype(F32), axis=0, keepdims=True)

        for at in states:
            extras = [
                total(at[name]) for name in ("d_pre", "d_update", "d_reset", "gain", "d_mixed", "d_cand")
            ]
            sums = tuple(old + extra for old, extra in zip(sums, extras))
        return sums

    def remote(src, dst, stage, target):
        return pltpu.make_async_remote_copy(
            src_ref=src,
            dst_ref=dst,
            send_sem=red_send.at[stage],
            recv_sem=red_recv.at[stage],
            device_id=target,
            device_id_type=MESH,
        )

    def whole_wait(ref, sem):
        pltpu.make_async_copy(ref, ref, sem).wait()

    def core_copy(region):
        return remote(
            slab.at[pl.ds((1 - core) * HALF + region * REGION, REGION)],
            core_rcv.at[pl.ds(region * REGION, REGION)],
            region,
            sibling,
        )

    def products():
        store_tiles(slab, CAND_AT, tn(d_cand_s[...], joined_s[...]))
        store_tiles(slab, GATES_AT, tn(joined_s[:, :channels], d_gate_s[...]))
        store_tiles(slab, GATES_AT + 36, tn(prior_s[...], d_gate_s[...]))
        store_tiles(slab, DOWN_AT, tn(d_mix_s[...], hid_s[...]))
        core_copy(0).start()
        store_tiles(slab, UP_AT, tn(normed_s[...], d_pre_s[...]))
        core_copy(1).start()

    zeros = jnp.zeros((1, channels), F32)
    sums = (jnp.zeros((1, w_up.shape[1]), F32), zeros, zeros, zeros, zeros, zeros)
    sums = cell([(0, (1, 2, 3, 4, 5, 6))], sums)
    receive_halos(1)
    border_lines(field.at[0], 0, 0, top, 0)
    border_lines(field.at[9], 1, 2, bottom, 7)
    sums = cell([(6, (7, 0))], sums, products)
    put_line(2, 0, d_sec[8])
    put_line(2, 1, d_sec[1])
    put_turned(turn_snd.at[2, 0], turned_faces[0], lambda face: d_sec[1, face])
    put_turned(turn_snd.at[2, 1], turned_faces[2], lambda face: d_sec[8, face])
    start_halos(2)
    small[ROW_BUP : ROW_BUP + 1, :] = sums[0]
    small[ROW_BGATES : ROW_BGATES + 1, :channels] = sums[1]
    small[ROW_BGATES : ROW_BGATES + 1, channels : 2 * channels] = sums[2]
    small[ROW_GAIN : ROW_GAIN + 1, :channels] = sums[3]
    small[ROW_BDOWN : ROW_BDOWN + 1, :channels] = sums[4]
    small[ROW_BCAND : ROW_BCAND + 1, :channels] = sums[5]

    def add_cores(region):
        core_copy(region).wait_recv()

        def some(step, carry):
            here = region * REGION + step * 8
            total = slab[pl.ds(core * HALF + here, 8)].astype(F32)
            t1[pl.ds(here, 8)] = (total + core_rcv[pl.ds(here, 8)].astype(F32)).astype(BF16)
            return carry

        lax.fori_loop(0, REGION // 8, some, 0)

    def scatter(region, steps, received, stage):
        for number, step in enumerate(steps):
            dx, dy, dz = step
            other = z_at[dz] if region else y_at[dy]
            remote(
                t1.at[pl.ds(region * REGION + (x_at[dx] * side + other) * unit, unit)],
                received.at[number],
                stage,
                offset(dx, dy, dz),
            ).start()

    add_cores(0)
    scatter(0, xy_steps, xy_rcv, 2)
    add_cores(1)
    scatter(1, xz_steps, xz_rcv, 3)

    receive_halos(2)
    gather(d_sec.at[0], 0, 0, top, "straight")
    gather(d_sec.at[9], 1, 2, bottom, "straight")
    gather(halo.at[2], 0, 3, west, "turned")
    gather(halo.at[3], 1, 1, east, "turned")

    def first_back(i, sums):
        value = d_sec[i + 1]
        d_first = tap(1, 0) * d_sec[i + 2] + tap(1, 1) * value + tap(1, 2) * d_sec[i]
        d_first += jnp.where(place == 0, tap(1, 0) * upright(2, i), 0.0)
        d_first += jnp.where(place == 7, tap(1, 2) * upright(3, i), 0.0)
        d_first = rounded(d_first)
        d_first_s[i] = d_first
        set_columns(d_first, i)
        x_value = x_row(i)
        left, right = column_shifts(x_value, 0, 1, i)
        pairs = (
            (d_first, left),
            (d_first, x_value),
            (d_first, right),
            (value, field[i]),
            (value, field[i + 1]),
            (value, field[i + 2]),
        )
        return tuple(old + jnp.sum(a * c, axis=0) for old, (a, c) in zip(sums, pairs))

    tap_sums = lax.fori_loop(
        0, 8, first_back, tuple(jnp.zeros((SIDE, channels), F32) for _ in range(6))
    )
    put_columns(3)
    put_turned(turn_snd.at[3, 0], turned_faces[3], lambda face: columns[0, face])
    put_turned(turn_snd.at[3, 1], turned_faces[1], lambda face: columns[1, face])
    start_halos(3)

    for number, tap_sum in enumerate(tap_sums):
        row = ROW_TAPS + number
        small[row : row + 1, :channels] = jnp.sum(tap_sum, axis=0, keepdims=True)
    tile32[...] = jnp.zeros_like(tile32)
    line = 0
    for row, count in SMALL_ROWS:
        for number in range(count):
            tile32[line : line + 1, :] = small[row : row + 1, number * 128 : number * 128 + 128]
            line += 1
    small_c[0] = tile32[...].astype(BF16)
    small_core = remote(small_c.at[0], small_c.at[1], 4, sibling)
    small_core.start()

    def spread_slot(slots, me, steps, stage):
        for step in steps:
            remote(slots.at[me], slots.at[me], stage, offset(*step)).start()

    def sum_slots(slots, stage):
        count = slots.shape[0]
        whole_wait(slots.at[pl.ds(0, count - 1)], red_recv.at[stage])
        total = slots[0].astype(F32)
        for number in range(1, count):
            total += slots[number].astype(F32)
        return total

    def add_scattered(region, at, received, slots, slot, stage):
        whole_wait(received, red_recv.at[stage])
        total = t1[pl.ds(region * REGION + at * unit, unit)].astype(F32)
        for number in range(received.shape[0]):
            total += received[number].astype(F32)
        slots[slot] = total.astype(BF16)

    add_scattered(0, mx * side + ty, xy_rcv, cz, tx, 2)
    spread_slot(cz, tx, z_steps, 5)
    add_scattered(1, mx * side + tx, xz_rcv, cy, ty, 3)
    spread_slot(cy, ty, y_steps, 6)
    small_core.wait_recv()
    small_x[mx] = (small_c[0].astype(F32) + small_c[1].astype(F32)).astype(BF16)
    spread_slot(small_x, mx, x_steps, 7)
    small_y[ty] = sum_slots(small_x, 7).astype(BF16)
    spread_slot(small_y, ty, y_steps, 8)

    base = core * HALF

    def share(region, at, slots, stage, steps, out_stage):
        at = base + region * REGION + at * unit
        gathered[pl.ds(at, unit)] = (sum_slots(slots, stage) * norm_factor).astype(BF16)
        piece = gathered.at[pl.ds(at, unit)]
        for step in steps:
            remote(piece, piece, out_stage, offset(*step)).start()

    share(0, mx * side + ty, cz, 5, xy_steps, 10)
    share(1, mx * side + tx, cy, 6, xz_steps, 11)

    receive_halos(3)
    gather(halo.at[2], 0, 3, west, "straight")
    gather(halo.at[3], 1, 1, east, "straight")
    gather(halo.at[4], 0, 0, top, "turned")
    gather(halo.at[5], 1, 2, bottom, "turned")

    def input_back(i, carry):
        value = d_first_s[i]
        left, right = column_shifts(value, 2, 3, i)
        d_input = tap(0, 0) * right + tap(0, 1) * value + tap(0, 2) * left
        on_top = jnp.where(i == 0, 1.0, 0.0)
        on_bottom = jnp.where(i == 7, 1.0, 0.0)
        d_input += on_top * (tap(0, 0) * halo[4]) + on_bottom * (tap(0, 2) * halo[5])
        at = pl.multiple_of(lax.rem(i + 7, 8) * 96, 96)
        d_mixed = d_mix_s[pl.ds(at, 96), :].astype(F32).reshape(FACES, SIDE, channels)
        gi_out[:, pl.ds(i, 1)] = (
            (d_input + d_mixed).reshape(FACES, 1, SIDE, channels).astype(BF16)
        )
        return carry

    lax.fori_loop(0, 8, input_back, 0)

    small_z[tx] = sum_slots(small_y, 8).astype(BF16)
    spread_slot(small_z, tx, z_steps, 9)
    tile32[...] = sum_slots(small_z, 9) * norm_factor

    def row_at(line, size):
        pieces = [tile32[line + number : line + number + 1, :] for number in range(-(-size // 128))]
        return jnp.concatenate(pieces, axis=1)[:, :size].astype(BF16)

    for axis in range(2):
        for number in range(3):
            taps_out[number, axis : axis + 1, :] = row_at(9 + 2 * (3 * axis + number), channels)
    for out, line in (
        (b_up_out, 0),
        (b_gates_out, 6),
        (gain_out, 21),
        (b_down_out, 23),
        (b_cand_out, 25),
    ):
        out[...] = row_at(line, out.shape[0]).reshape(out.shape)

    def core_back(region):
        piece = gathered.at[pl.ds(base + region * REGION, REGION)]
        return remote(piece, piece, 12 + region, sibling)

    shares = nx * side - 1
    for region in range(2):
        whole_wait(gathered.at[pl.ds(0, unit * shares)], red_recv.at[10 + region])
        core_back(region).start()
    for region in range(2):
        core_back(region).wait_recv()

    def unpack(at, out):
        columns_of_tiles = out.shape[1] // 128
        for row in range(out.shape[0] // 16):
            for column in range(columns_of_tiles):
                out[row * 16 : row * 16 + 16, column * 128 : column * 128 + 128] = gathered[
                    tile_place(at + row * columns_of_tiles + column)
                ]

    unpack(CAND_AT, cand_out)
    unpack(GATES_AT, gates_out)
    unpack(DOWN_AT, down_out)
    unpack(UP_AT, up_out)

    for exchange in range(4):
        finish_halo_sends(exchange)
    for number in range(2):
        pl.when(far_sends[number])(far_copies[number].wait_send)
    small_core.wait_send()
    for region in range(2):
        core_copy(region).wait_send()
        core_back(region).wait_send()
    for ref, stage in (
        (xy_rcv, 2),
        (xz_rcv, 3),
        (cz.at[pl.ds(0, side - 1)], 5),
        (cy.at[pl.ds(0, side - 1)], 6),
        (small_x.at[pl.ds(0, nx - 1)], 7),
        (small_y.at[pl.ds(0, side - 1)], 8),
        (small_z.at[pl.ds(0, side - 1)], 9),
        (gathered.at[pl.ds(0, unit * shares)], 10),
        (gathered.at[pl.ds(0, unit * shares)], 11),
    ):
        whole_wait(ref, red_send.at[stage])


def relay_kernel(count, *refs):
    copies = [
        pltpu.make_async_copy(refs[number], refs[count + number], refs[-1].at[number])
        for number in range(count)
    ]
    for copy in copies:
        copy.start()
    for copy in copies:
        copy.wait()


def on_device(
    inputs,
    state,
    cotangent,
    adjacency,
    taps,
    gain,
    w_up,
    b_up,
    w_down,
    b_down,
    w_gates,
    b_gates,
    w_cand,
    b_cand,
):
    channels = inputs.shape[-1]
    wide = w_up.shape[1]
    tokens = FACES * SIDE * SIDE
    lines = FACES * SIDE
    tile_count, date_count = lax.axis_size("tile"), lax.axis_size("date")
    side = 2 ** ((tile_count.bit_length() - 2) // 2)
    x_low = date_count // 2
    nx = 2 * x_low
    unit = REGION // (nx * side)
    norm_factor = float(tokens * tile_count * date_count) ** (-0.5)
    vmem = pl.BlockSpec(memory_space=pltpu.VMEM)
    hbm = pl.BlockSpec(memory_space=pltpu.HBM)
    grid_shape = (FACES, SIDE, SIDE, channels)

    def buf(*shape):
        return pltpu.VMEM(shape, BF16)

    def wide_buf(*shape):
        return pltpu.VMEM(shape, F32)

    def arr(*shape):
        return jax.ShapeDtypeStruct(shape, BF16)

    shares = nx * side - 1
    results = (
        arr(*grid_shape),
        arr(*grid_shape),
        arr(3, 2, channels),
        arr(channels),
        arr(channels, wide),
        arr(wide),
        arr(channels, wide),
        arr(channels),
        arr(2 * channels, 2 * channels),
        arr(2 * channels),
        arr(channels, 2 * channels),
        arr(channels),
    )
    made = pl.pallas_call(
        functools.partial(level_kernel, side, x_low, norm_factor),
        name="level",
        out_shape=tuple(pltpu.VMEM(result.shape, result.dtype) for result in results),
        in_specs=[hbm] * 14,
        out_specs=[vmem] * 12,
        scratch_shapes=[
            pltpu.SMEM((4, 2, FACES), jnp.int32),
            buf(*grid_shape),
            buf(*grid_shape),
            buf(*grid_shape),
            buf(3, 2, channels),
            buf(channels),
            buf(wide),
            buf(channels),
            buf(2 * channels),
            buf(channels),
            buf(channels, wide),
            buf(channels, wide),
            buf(2 * channels, 2 * channels),
            buf(channels, 2 * channels),
            wide_buf(16, wide),
            pltpu.SMEM((4, FACES), jnp.int32),
            buf(4, 2, lines, channels),
            buf(4, 2, lines, channels),
            buf(4, 2, TURNED * SIDE, channels),
            buf(4, 2, TURNED * SIDE, channels),
            buf(2, 2 * TURNED * SIDE, channels),
            buf(2, 2 * TURNED * SIDE, channels),
            wide_buf(2, 2, TURNED + 1, SIDE, channels),
            wide_buf(2, ZERO_LINE + 1, SIDE, channels),
            wide_buf(6, FACES, SIDE, channels),
            wide_buf(4, FACES, SIDE, channels),
            wide_buf(10, FACES, SIDE, channels),
            wide_buf(10, FACES, SIDE, channels),
            wide_buf(8, FACES, SIDE, channels),
            buf(2 * channels, channels),
            buf(2 * channels, channels),
            buf(channels, channels),
            buf(channels, channels),
            buf(tokens, channels),
            buf(tokens, channels),
            buf(tokens, wide),
            buf(tokens, wide),
            buf(tokens, channels),
            buf(tokens, 2 * channels),
            buf(tokens, 2 * channels),
            buf(tokens, channels),
            wide_buf(16, wide),
            wide_buf(32, 128),
            buf(2, 32, 128),
            buf(nx, 32, 128),
            buf(side, 32, 128),
            buf(side, 32, 128),
            buf(2 * HALF, 16, 128),
            buf(HALF, 16, 128),
            buf(HALF, 16, 128),
            buf(shares, unit, 16, 128),
            buf(shares, unit, 16, 128),
            buf(side, unit, 16, 128),
            buf(side, unit, 16, 128),
            buf(2 * HALF, 16, 128),
            pltpu.SemaphoreType.DMA((14,)),
            pltpu.SemaphoreType.DMA((4, 4)),
            pltpu.SemaphoreType.DMA((4, 4)),
            pltpu.SemaphoreType.DMA((2,)),
            pltpu.SemaphoreType.DMA((2,)),
            pltpu.SemaphoreType.DMA((14,)),
            pltpu.SemaphoreType.DMA((14,)),
        ],
        compiler_params=pltpu.CompilerParams(
            collective_id=0, has_side_effects=True, vmem_limit_bytes=60 * 2**20
        ),
    )(
        adjacency.transpose(1, 2, 0),
        inputs.reshape(grid_shape),
        state.reshape(grid_shape),
        cotangent.reshape(grid_shape),
        taps.transpose(1, 0, 2),
        gain,
        b_up,
        b_down,
        b_gates,
        b_cand,
        w_up,
        w_down.T,
        w_gates,
        w_cand.T,
    )
    new_rows, grad_rows, g_taps, g_gain, g_up, g_bup, g_down, g_bdown, g_gates, g_bgates, g_cand, g_bcand = (
        pl.pallas_call(
            functools.partial(relay_kernel, len(results)),
            name="relay",
            out_shape=results,
            in_specs=[vmem] * 12,
            out_specs=[hbm] * 12,
            scratch_shapes=[pltpu.SemaphoreType.DMA((12,))],
            compiler_params=pltpu.CompilerParams(vmem_limit_bytes=32 * 2**20),
        )(*made)
    )
    return (
        new_rows.reshape(inputs.shape),
        grad_rows.reshape(inputs.shape),
        g_taps.transpose(1, 0, 2),
        g_gain,
        g_up,
        g_bup,
        g_down.T,
        g_bdown,
        g_gates,
        g_bgates,
        g_cand.T,
        g_bcand,
    )


def solution(mesh):
    field = P("tile", "date", None, None, None, None)
    return jax.shard_map(
        on_device,
        mesh=mesh,
        in_specs=(field,) * 3 + (P(),) * 11,
        out_specs=(field,) * 2 + (P(),) * 10,
        check_vma=False,
    )
```

```python
import functools
import math

import jax
import jax.numpy as jnp
from jax import lax
from jax.experimental import pallas as pl
from jax.experimental.pallas import tpu as pltpu
from jax.sharding import PartitionSpec as P

EPSILON = 1e-06
MESH = pl.DeviceIdType.MESH
F32 = jnp.float32
BF16 = jnp.bfloat16
FACES = 12
SIDE = 8
HALF = 128
REGION = 64
TURNED = 4
ZERO_LINE = FACES + TURNED
GELU_A = math.sqrt(2.0 / math.pi)
GELU_B = 0.044715
ROW_BUP, ROW_BGATES, ROW_TAPS, ROW_GAIN, ROW_BDOWN, ROW_BCAND = 0, 1, 2, 8, 9, 10
SMALL_ROWS = ((0, 6), (1, 3)) + tuple((row, 2) for row in range(2, 11))
CAND_AT, GATES_AT, DOWN_AT, UP_AT, SMALL_AT = 0, 36, 108, 180, 252


def nn(left, right):
    return jnp.dot(left, right, preferred_element_type=F32)


def nt(left, right):
    return lax.dot_general(left, right, (((1,), (1,)), ((), ())), preferred_element_type=F32)


def tn(left, right):
    return lax.dot_general(left, right, (((0,), (0,)), ((), ())), preferred_element_type=F32)


def sigmoid(value):
    return 0.5 + 0.5 * jnp.tanh(0.5 * value)


def tile_place(number):
    if 64 <= number < 128:
        return number + 64
    if 128 <= number < 192:
        return number - 64
    return number


def store_tiles(slab, at, matrix):
    rows, columns = matrix.shape
    packed = matrix.astype(BF16)
    across = columns // 128
    for row in range(rows // 16):
        for column in range(across):
            slab[tile_place(at + row * across + column)] = packed[
                row * 16 : row * 16 + 16, column * 128 : column * 128 + 128
            ]


def level_kernel(
    side,
    x_low,
    norm_factor,
    adj_in,
    x_in,
    h_in,
    g_in,
    taps_in,
    gain_in,
    b_up_in,
    b_down_in,
    b_gates_in,
    b_cand_in,
    w_up_in,
    w_down_in,
    w_gates_in,
    w_cand_in,
    ns_out,
    gi_out,
    taps_out,
    gain_out,
    up_out,
    b_up_out,
    down_out,
    b_down_out,
    gates_out,
    b_gates_out,
    cand_out,
    b_cand_out,
    adj,
    x_ref,
    h_ref,
    g_ref,
    taps_ref,
    gain_ref,
    b_up_ref,
    b_down_ref,
    b_gates_ref,
    b_cand_ref,
    w_up,
    w_down_t,
    w_gates,
    w_cand_t,
    par,
    rank_of,
    snd,
    rcv,
    turn_snd,
    turn_rcv,
    far_snd,
    far_rcv,
    far_pool,
    pool,
    halo,
    columns,
    field,
    d_sec,
    d_first_s,
    wg_u,
    wg_r,
    wc_m,
    wc_r,
    prior_s,
    normed_s,
    hid_s,
    d_pre_s,
    d_mix_s,
    d_gate_s,
    joined_s,
    d_cand_s,
    small,
    tile32,
    small_c,
    small_x,
    small_y,
    small_z,
    slab,
    core_rcv,
    t1,
    xy_rcv,
    xz_rcv,
    cz,
    cy,
    gathered,
    load_sem,
    halo_send,
    halo_recv,
    far_send,
    far_recv,
    red_send,
    red_recv,
):
    channels = x_ref.shape[3]
    nx = 2 * x_low
    unit = REGION // (nx * side)
    tile = lax.axis_index("tile")
    date = lax.axis_index("date")
    place_of_tile = lax.div(tile, 2)
    ty, tx = lax.div(place_of_tile, side), lax.rem(place_of_tile, side)
    core = lax.rem(date, 2)
    mx = lax.rem(tile, 2) * x_low + lax.div(date, 2)

    def device(x, y, z, c):
        return ((y * side + z) * 2 + lax.div(x, x_low), lax.rem(x, x_low) * 2 + c)

    x_at = [lax.rem(mx + step, nx) if step else mx for step in range(nx)]
    y_at = [lax.rem(ty + step, side) if step else ty for step in range(side)]
    z_at = [lax.rem(tx + step, side) if step else tx for step in range(side)]
    x_tile = [lax.div(x, x_low) for x in x_at]
    x_date = [lax.rem(x, x_low) * 2 + core for x in x_at]
    y_tile = [y * (2 * side) for y in y_at]
    z_tile = [z * 2 for z in z_at]
    xy_tile = [[x + y for y in y_tile] for x in x_tile]
    xz_tile = [[x + z for z in z_tile] for x in x_tile]

    def offset(dx, dy, dz):
        if not dz:
            return xy_tile[dx][dy] + z_tile[0], x_date[dx]
        if not dy:
            return xz_tile[dx][dz] + y_tile[0], x_date[dx]
        return x_tile[dx] + y_tile[dy] + z_tile[dz], x_date[dx]

    sibling = device(mx, ty, tx, 1 - core)
    across = device(mx, tx, ty, core)
    top, bottom = ty == 0, ty == side - 1
    west, east = tx == 0, tx == side - 1
    has_across = jnp.logical_and(
        ty != tx,
        jnp.logical_or(jnp.logical_or(top, bottom), jnp.logical_or(west, east)),
    )

    def far(step):
        dx, dy, dz = step
        return min(dx, nx - dx) + min(dy, side - dy) + min(dz, side - dz)

    xy_steps = [(dx, dy, 0) for dx in range(nx) for dy in range(side) if dx or dy]
    xz_steps = [(dx, 0, dz) for dx in range(nx) for dz in range(side) if dx or dz]
    xy_steps.sort(key=far, reverse=True)
    xz_steps.sort(key=far, reverse=True)
    x_steps = [(dx, 0, 0) for dx in range(1, nx)]
    y_steps = [(0, dy, 0) for dy in range(1, side)]
    z_steps = [(0, 0, dz) for dz in range(1, side)]

    barrier = pltpu.get_barrier_semaphore()

    @pl.when(has_across)
    def _():
        pl.semaphore_signal(barrier, inc=1, device_id=across, device_id_type=MESH)

    loads = [
        pltpu.make_async_copy(src, dst, load_sem.at[number])
        for number, (src, dst) in enumerate(
            (
                (x_in, x_ref),
                (adj_in, adj),
                (taps_in, taps_ref),
                (w_gates_in, w_gates),
                (w_cand_in, w_cand_t),
                (gain_in, gain_ref),
                (b_up_in, b_up_ref),
                (b_down_in, b_down_ref),
                (b_gates_in, b_gates_ref),
                (b_cand_in, b_cand_ref),
                (w_up_in, w_up),
                (w_down_in, w_down_t),
                (h_in, h_ref),
                (g_in, g_ref),
            )
        )
    ]
    loads[0].start()
    loads[1].start()
    peers = [offset(*step) for step in sorted(xy_steps, key=far)]
    peers += [offset(*step) for step in sorted(xz_steps, key=far) if step[2]]
    peers.append(sibling)
    for peer in peers:
        pl.semaphore_signal(barrier, inc=1, device_id=peer, device_id_type=MESH)
    for load in loads[2:]:
        load.start()

    def tap(axis, number):
        row = ROW_TAPS + 3 * axis + number
        return par[row : row + 1, :channels].reshape(1, 1, channels)

    def set_columns(value, i):
        columns[0, :, pl.ds(i, 1), :] = value[:, 0:1, :]
        columns[1, :, pl.ds(i, 1), :] = value[:, 7:8, :]

    def rounded(value):
        return value.astype(BF16).astype(F32)

    def put_line(exchange, kind, value):
        snd[exchange, kind] = value.reshape(FACES * SIDE, channels).astype(BF16)

    def put_columns(exchange):
        put_line(exchange, 0, columns[1])
        put_line(exchange, 1, columns[0])

    def put_turned(ref, faces, line_of):
        lines = [line_of(face).astype(F32) for face in faces]
        ref[...] = jnp.concatenate(lines, axis=0).astype(BF16)

    def is_turned(edge, face):
        return adj[edge, 1, face] != (edge + 2) % 4

    loads[1].wait()
    turned_faces = []
    for edge in range(4):
        count = jnp.int32(0)
        chosen = [jnp.int32(0)] * TURNED
        for face in range(FACES):
            rank_of[edge, face] = count
            here = is_turned(edge, face)
            chosen = [
                jnp.where(jnp.logical_and(here, count == slot), face, old)
                for slot, old in enumerate(chosen)
            ]
            count = count + jnp.where(here, 1, 0)
        turned_faces.append(chosen)

    loads[0].wait()

    def x_row(i):
        return x_ref[:, pl.ds(i, 1)].astype(F32).reshape(FACES, SIDE, channels)

    def x_lines(i, carry):
        value = x_row(i)
        set_columns(value, i)
        columns[2, :, pl.ds(i, 1), :] = value[:, 1:2, :]
        columns[3, :, pl.ds(i, 1), :] = value[:, 6:7, :]
        return carry

    lax.fori_loop(0, 8, x_lines, 0)
    put_columns(0)

    put_turned(turn_snd.at[0, 0], turned_faces[0], lambda face: x_ref[face, 0])
    put_turned(turn_snd.at[0, 1], turned_faces[2], lambda face: x_ref[face, 7])
    for which, edge, order in ((0, 3, (0, 2)), (1, 1, (3, 1))):
        for position, column in enumerate(order):
            part = pl.ds(position * TURNED * SIDE, TURNED * SIDE)
            put_turned(
                far_snd.at[which, part],
                turned_faces[edge],
                lambda face, column=column: columns[column, face],
            )

    @pl.when(has_across)
    def _():
        pl.semaphore_wait(barrier, len(peers) + 1)

    @pl.when(jnp.logical_not(has_across))
    def _():
        pl.semaphore_wait(barrier, len(peers))

    row_first = jnp.logical_and(top, jnp.logical_not(west))
    row_last = jnp.logical_and(bottom, jnp.logical_not(east))
    col_first = jnp.logical_and(west, jnp.logical_not(top))
    col_last = jnp.logical_and(east, jnp.logical_not(bottom))
    corners = (jnp.logical_and(top, west), jnp.logical_and(bottom, east))

    far_copies = [
        pltpu.make_async_remote_copy(
            src_ref=far_snd.at[number],
            dst_ref=far_rcv.at[number],
            send_sem=far_send.at[number],
            recv_sem=far_recv.at[number],
            device_id=across,
            device_id_type=MESH,
        )
        for number in range(2)
    ]
    far_sends, far_receives = (col_first, col_last), (row_first, row_last)

    def halo_copies(exchange):
        if exchange in (0, 3):
            ahead, behind = offset(0, 0, 1), offset(0, 0, side - 1)
        else:
            ahead, behind = offset(0, 1, 0), offset(0, side - 1, 0)
        if exchange in (0, 2):
            sends, receives = (row_first, row_last), (col_first, col_last)
        else:
            sends, receives = (col_first, col_last), (row_first, row_last)
        copies = []
        for kind, target in enumerate((ahead, behind, across, across)):
            turns = kind >= 2
            if turns and exchange == 1:
                continue
            number = kind % 2
            copy = pltpu.make_async_remote_copy(
                src_ref=(turn_snd if turns else snd).at[exchange, number],
                dst_ref=(turn_rcv if turns else rcv).at[exchange, number],
                send_sem=halo_send.at[exchange, kind],
                recv_sem=halo_recv.at[exchange, kind],
                device_id=target,
                device_id_type=MESH,
            )
            copies.append(
                (copy, sends[number] if turns else None, receives[number] if turns else None)
            )
        return copies

    def start_halos(exchange):
        for copy, sends, _ in reversed(halo_copies(exchange)):
            if sends is None:
                copy.start()
            else:
                pl.when(sends)(copy.start)

    def finish_halo_sends(exchange):
        for copy, sends, _ in halo_copies(exchange):
            if sends is None:
                copy.wait_send()
            else:
                pl.when(sends)(copy.wait_send)

    def receive_halos(exchange):
        for kind, (copy, _, receives) in enumerate(halo_copies(exchange)):
            number = kind % 2
            if kind < 2:
                copy.wait_recv()
                pool[number, :FACES] = (
                    rcv[exchange, number].astype(F32).reshape(FACES, SIDE, channels)
                )
                continue

            def spread(ref):
                pool[number, FACES:ZERO_LINE] = (
                    ref[exchange, number].astype(F32).reshape(TURNED, SIDE, channels)
                )

            @pl.when(receives)
            def _():
                copy.wait_recv()
                spread(turn_rcv)

            @pl.when(corners[number])
            def _():
                spread(turn_snd)

    def gather(to, which, edge, on_border, mode):
        for face in range(FACES):
            neighbour = adj[edge, 0, face]
            turned = is_turned(edge, face)
            across_line = FACES + rank_of[3 - edge, neighbour]
            if mode == "both":
                there = jnp.where(turned, across_line, neighbour)
                index = jnp.where(on_border, there, face)
            elif mode == "straight":
                index = jnp.where(on_border, jnp.where(turned, ZERO_LINE, neighbour), face)
            else:
                index = jnp.where(jnp.logical_and(on_border, turned), across_line, ZERO_LINE)
            to[face] = pool[which, index]

    def border_lines(to, which, edge, on_border, row):
        def spread(ref):
            far_pool[which, :, :TURNED] = (
                ref[...].astype(F32).reshape(2, TURNED, SIDE, channels)
            )

        @pl.when(far_receives[which])
        def _():
            far_copies[which].wait_recv()
            spread(far_rcv.at[which])

        @pl.when(corners[which])
        def _():
            spread(far_snd.at[which])

        own = x_row(row)
        for face in range(FACES):
            neighbour = adj[edge, 0, face]
            turned = jnp.logical_and(on_border, is_turned(edge, face))
            straight = jnp.where(on_border, jnp.where(turned, ZERO_LINE, neighbour), face)
            slot = rank_of[3 - edge, neighbour]
            low, high = far_pool[which, 0, slot], far_pool[which, 1, slot]
            lines = (own[face], low, high) if edge == 0 else (low, high, own[face])
            made = sum(tap(0, number)[0] * lines[number] for number in range(3))
            to[face] = jnp.where(turned, rounded(made), pool[which, straight])

    place = lax.broadcasted_iota(jnp.int32, (FACES, SIDE, channels), 1)

    def upright(which, i):
        return jnp.broadcast_to(halo[which, :, pl.ds(i, 1), :], (FACES, SIDE, channels))

    def column_shifts(value, west_lines, east_lines, i):
        left = jnp.where(place == 0, upright(west_lines, i), pltpu.roll(value, 1, 1))
        right = jnp.where(place == 7, upright(east_lines, i), pltpu.roll(value, 7, 1))
        return left, right

    start_halos(0)
    for number in range(2):
        pl.when(far_sends[number])(far_copies[number].start)
    pool[...] = jnp.zeros_like(pool)
    far_pool[...] = jnp.zeros_like(far_pool)
    small[...] = jnp.zeros_like(small)
    slab[SMALL_AT : 2 * HALF] = jnp.zeros((2 * HALF - SMALL_AT, 16, 128), BF16)
    for number in range(2, 10):
        loads[number].wait()
    for axis in range(2):
        for number in range(3):
            row = ROW_TAPS + 3 * axis + number
            par[row : row + 1, :channels] = taps_ref[number, axis : axis + 1, :].astype(F32)
    for row, ref in (
        (ROW_GAIN, gain_ref),
        (ROW_BUP, b_up_ref),
        (ROW_BDOWN, b_down_ref),
        (ROW_BGATES, b_gates_ref),
        (ROW_BCAND, b_cand_ref),
    ):
        size = ref.shape[0]
        par[row : row + 1, :size] = ref[...].astype(F32).reshape(1, size)
    wg_u[...] = w_gates[:, :channels]
    wg_r[...] = w_gates[:, channels:]
    wc_m[...] = w_cand_t[:, :channels]
    wc_r[...] = w_cand_t[:, channels:]
    for load in loads[10:]:
        load.wait()

    receive_halos(0)
    gather(halo.at[0], 0, 3, west, "both")
    gather(halo.at[1], 1, 1, east, "both")

    def first_pass(i, carry):
        value = x_row(i)
        left, right = column_shifts(value, 0, 1, i)
        first = rounded(tap(0, 0) * left + tap(0, 1) * value + tap(0, 2) * right)
        field[i + 1] = first
        return carry

    lax.fori_loop(0, 8, first_pass, 0)
    put_line(1, 0, field[8])
    put_line(1, 1, field[1])
    start_halos(1)

    def vector(row, start, size):
        return par[row : row + 1, start : start + size]

    def cell(blocks, sums, hooks=None):
        gain = vector(ROW_GAIN, 0, channels)

        def second_row(i):
            return tap(1, 0) * field[i] + tap(1, 1) * field[i + 1] + tap(1, 2) * field[i + 2]

        def row_of(ref):
            return lambda i: ref[:, pl.ds(i, 1)].astype(F32)

        def joint(block, read):
            parts = [read(i).reshape(FACES * SIDE, channels) for i in block[1]]
            return parts[0] if len(parts) == 1 else jnp.concatenate(parts, axis=0)

        def rows(block):
            return pl.ds(pl.multiple_of(block[0] * 96, 96), 96 * len(block[1]))

        states = [{"block": block} for block in blocks]

        def norm(at):
            centred = joint(at["block"], second_row)
            centred = centred - jnp.mean(centred, axis=-1, keepdims=True)
            at["inv"] = lax.rsqrt(jnp.mean(centred * centred, axis=-1, keepdims=True) + EPSILON)
            at["standard"] = centred * at["inv"]
            at["normed"] = (at["standard"] * gain).astype(BF16)
            normed_s[rows(at["block"]), :] = at["normed"]

        def up(at):
            at["pre"] = nn(at["normed"], w_up[...]) + vector(ROW_BUP, 0, w_up.shape[1])

        def bend(at):
            pre = at["pre"]
            square = pre * pre
            curve = jnp.tanh(pre * (GELU_A + (GELU_A * GELU_B) * square))
            rise = 1.0 + curve
            half = 0.5 * pre
            at["hid"] = (half * rise).astype(BF16)
            hid_s[rows(at["block"]), :] = at["hid"]
            at["slope"] = rise * (
                0.5 + half * (1.0 - curve) * (GELU_A + (3.0 * GELU_A * GELU_B) * square)
            )

        def down(at):
            mixed = (
                joint(at["block"], row_of(x_ref))
                + nt(at["hid"], w_down_t[...])
                + vector(ROW_BDOWN, 0, channels)
            )
            at["mixed"] = mixed.astype(BF16)
            joined_s[rows(at["block"]), :channels] = at["mixed"]

        def gates(at):
            mixed = at["mixed"]
            at["prior"] = joint(at["block"], row_of(h_ref))
            prior_b = at["prior"].astype(BF16)
            prior_s[rows(at["block"]), :] = prior_b
            at["reset"] = sigmoid(
                nn(mixed, wg_r[:channels])
                + nn(prior_b, wg_r[channels:])
                + vector(ROW_BGATES, channels, channels)
            )
            at["update"] = sigmoid(
                nn(mixed, wg_u[:channels])
                + nn(prior_b, wg_u[channels:])
                + vector(ROW_BGATES, 0, channels)
            )

        def propose(at):
            reset_state = (at["reset"] * at["prior"]).astype(BF16)
            joined_s[rows(at["block"]), channels:] = reset_state
            at["candidate"] = jnp.tanh(
                nt(at["mixed"], wc_m[...])
                + nt(reset_state, wc_r[...])
                + vector(ROW_BCAND, 0, channels)
            )

        def renew(at):
            update, candidate, prior = at["update"], at["candidate"], at["prior"]
            new = rounded((1.0 - update) * candidate + update * prior)
            for number, i in enumerate(at["block"][1]):
                ns_out[:, pl.ds(i, 1)] = (
                    new[number * 96 : number * 96 + 96]
                    .reshape(FACES, 1, SIDE, channels)
                    .astype(BF16)
                )
            kept = joint(at["block"], row_of(g_ref)) * (1.0 - update)
            at["d_cand"] = (kept * (1.0 - candidate * candidate)).astype(BF16)
            d_cand_s[rows(at["block"]), :] = at["d_cand"]
            at["d_update"] = (kept * (prior - candidate) * update).astype(BF16)
            d_gate_s[rows(at["block"]), :channels] = at["d_update"]

        def gates_back(at):
            reset = at["reset"]
            at["d_reset"] = (
                nn(at["d_cand"], wc_r[...]) * at["prior"] * reset * (1.0 - reset)
            ).astype(BF16)
            d_gate_s[rows(at["block"]), channels:] = at["d_reset"]

        def mixed_back(at):
            at["d_mixed"] = (
                nn(at["d_cand"], wc_m[...])
                + nt(at["d_update"], wg_u[:channels])
                + nt(at["d_reset"], wg_r[:channels])
            ).astype(BF16)
            d_mix_s[rows(at["block"]), :] = at["d_mixed"]

        def hidden_back(at):
            at["d_pre"] = (nn(at["d_mixed"], w_down_t[...]) * at["slope"]).astype(BF16)
            d_pre_s[rows(at["block"]), :] = at["d_pre"]

        def norm_back(at):
            d_normed = nt(at["d_pre"], w_up[...])
            standard = at["standard"]
            d_standard = d_normed * gain
            d_second = rounded(
                at["inv"]
                * (
                    d_standard
                    - jnp.mean(d_standard, axis=-1, keepdims=True)
                    - standard * jnp.mean(d_standard * standard, axis=-1, keepdims=True)
                )
            )
            for number, i in enumerate(at["block"][1]):
                d_sec[i + 1] = d_second[number * 96 : number * 96 + 96].reshape(
                    FACES, SIDE, channels
                )
            at["gain"] = d_normed * standard

        for stage in (
            norm, up, bend, down, gates, propose, renew, gates_back, mixed_back, hidden_back, norm_back,
        ):
            for at in states:
                stage(at)
            if hooks and stage.__name__ in hooks:
                hooks[stage.__name__]()

        def total(value):
            return jnp.sum(value.astype(F32), axis=0, keepdims=True)

        for at in states:
            extras = [
                total(at[name]) for name in ("d_pre", "d_update", "d_reset", "gain", "d_mixed", "d_cand")
            ]
            sums = tuple(old + extra for old, extra in zip(sums, extras))
        return sums

    def remote(src, dst, stage, target):
        return pltpu.make_async_remote_copy(
            src_ref=src,
            dst_ref=dst,
            send_sem=red_send.at[stage],
            recv_sem=red_recv.at[stage],
            device_id=target,
            device_id_type=MESH,
        )

    def whole_wait(ref, sem):
        pltpu.make_async_copy(ref, ref, sem).wait()

    def core_copy(region):
        return remote(
            slab.at[pl.ds((1 - core) * HALF + region * REGION, REGION)],
            core_rcv.at[pl.ds(region * REGION, REGION)],
            region,
            sibling,
        )

    def add_cores(region):
        core_copy(region).wait_recv()

        def some(step, carry):
            here = region * REGION + step * 8
            total = slab[pl.ds(core * HALF + here, 8)].astype(F32)
            t1[pl.ds(here, 8)] = (total + core_rcv[pl.ds(here, 8)].astype(F32)).astype(BF16)
            return carry

        lax.fori_loop(0, REGION // 8, some, 0)

    def scatter(region, steps, received, stage):
        for number, step in enumerate(steps):
            dx, dy, dz = step
            other = z_at[dz] if region else y_at[dy]
            remote(
                t1.at[pl.ds(region * REGION + (x_at[dx] * side + other) * unit, unit)],
                received.at[number],
                stage,
                offset(dx, dy, dz),
            ).start()

    def early_products():
        store_tiles(slab, CAND_AT, tn(d_cand_s[...], joined_s[...]))
        store_tiles(slab, GATES_AT, tn(joined_s[:, :channels], d_gate_s[...]))
        store_tiles(slab, GATES_AT + 36, tn(prior_s[...], d_gate_s[...]))

    def down_product():
        store_tiles(slab, DOWN_AT, tn(d_mix_s[...], hid_s[...]))
        core_copy(0).start()

    def up_product():
        store_tiles(slab, UP_AT, tn(normed_s[...], d_pre_s[...]))
        core_copy(1).start()
        add_cores(0)
        scatter(0, xy_steps, xy_rcv, 2)

    hooks = {
        "gates_back": early_products,
        "mixed_back": down_product,
        "hidden_back": up_product,
    }

    zeros = jnp.zeros((1, channels), F32)
    sums = (jnp.zeros((1, w_up.shape[1]), F32), zeros, zeros, zeros, zeros, zeros)
    sums = cell([(0, (1, 2, 3, 4, 5, 6))], sums)
    receive_halos(1)
    border_lines(field.at[0], 0, 0, top, 0)
    border_lines(field.at[9], 1, 2, bottom, 7)
    sums = cell([(6, (7, 0))], sums, hooks)
    put_line(2, 0, d_sec[8])
    put_line(2, 1, d_sec[1])
    put_turned(turn_snd.at[2, 0], turned_faces[0], lambda face: d_sec[1, face])
    put_turned(turn_snd.at[2, 1], turned_faces[2], lambda face: d_sec[8, face])
    start_halos(2)
    small[ROW_BUP : ROW_BUP + 1, :] = sums[0]
    small[ROW_BGATES : ROW_BGATES + 1, :channels] = sums[1]
    small[ROW_BGATES : ROW_BGATES + 1, channels : 2 * channels] = sums[2]
    small[ROW_GAIN : ROW_GAIN + 1, :channels] = sums[3]
    small[ROW_BDOWN : ROW_BDOWN + 1, :channels] = sums[4]
    small[ROW_BCAND : ROW_BCAND + 1, :channels] = sums[5]

    add_cores(1)
    scatter(1, xz_steps, xz_rcv, 3)

    receive_halos(2)
    gather(d_sec.at[0], 0, 0, top, "straight")
    gather(d_sec.at[9], 1, 2, bottom, "straight")
    gather(halo.at[2], 0, 3, west, "turned")
    gather(halo.at[3], 1, 1, east, "turned")

    def first_back(i, sums):
        value = d_sec[i + 1]
        d_first = tap(1, 0) * d_sec[i + 2] + tap(1, 1) * value + tap(1, 2) * d_sec[i]
        d_first += jnp.where(place == 0, tap(1, 0) * upright(2, i), 0.0)
        d_first += jnp.where(place == 7, tap(1, 2) * upright(3, i), 0.0)
        d_first = rounded(d_first)
        d_first_s[i] = d_first
        set_columns(d_first, i)
        x_value = x_row(i)
        left, right = column_shifts(x_value, 0, 1, i)
        pairs = (
            (d_first, left),
            (d_first, x_value),
            (d_first, right),
            (value, field[i]),
            (value, field[i + 1]),
            (value, field[i + 2]),
        )
        return tuple(old + jnp.sum(a * c, axis=0) for old, (a, c) in zip(sums, pairs))

    tap_sums = lax.fori_loop(
        0, 8, first_back, tuple(jnp.zeros((SIDE, channels), F32) for _ in range(6))
    )
    put_columns(3)
    put_turned(turn_snd.at[3, 0], turned_faces[3], lambda face: columns[0, face])
    put_turned(turn_snd.at[3, 1], turned_faces[1], lambda face: columns[1, face])
    start_halos(3)

    for number, tap_sum in enumerate(tap_sums):
        row = ROW_TAPS + number
        small[row : row + 1, :channels] = jnp.sum(tap_sum, axis=0, keepdims=True)
    tile32[...] = jnp.zeros_like(tile32)
    line = 0
    for row, count in SMALL_ROWS:
        for number in range(count):
            tile32[line : line + 1, :] = small[row : row + 1, number * 128 : number * 128 + 128]
            line += 1
    small_c[0] = tile32[...].astype(BF16)
    small_core = remote(small_c.at[0], small_c.at[1], 4, sibling)
    small_core.start()

    def spread_slot(slots, me, steps, stage):
        for step in steps:
            remote(slots.at[me], slots.at[me], stage, offset(*step)).start()

    def sum_slots(slots, stage):
        count = slots.shape[0]
        whole_wait(slots.at[pl.ds(0, count - 1)], red_recv.at[stage])
        total = slots[0].astype(F32)
        for number in range(1, count):
            total += slots[number].astype(F32)
        return total

    def add_scattered(region, at, received, slots, slot, stage):
        whole_wait(received, red_recv.at[stage])
        total = t1[pl.ds(region * REGION + at * unit, unit)].astype(F32)
        for number in range(received.shape[0]):
            total += received[number].astype(F32)
        slots[slot] = total.astype(BF16)

    add_scattered(0, mx * side + ty, xy_rcv, cz, tx, 2)
    spread_slot(cz, tx, z_steps, 5)
    add_scattered(1, mx * side + tx, xz_rcv, cy, ty, 3)
    spread_slot(cy, ty, y_steps, 6)
    small_core.wait_recv()
    small_x[mx] = (small_c[0].astype(F32) + small_c[1].astype(F32)).astype(BF16)
    spread_slot(small_x, mx, x_steps, 7)
    small_y[ty] = sum_slots(small_x, 7).astype(BF16)
    spread_slot(small_y, ty, y_steps, 8)

    base = core * HALF

    def share(region, at, slots, stage, steps, out_stage):
        at = base + region * REGION + at * unit
        gathered[pl.ds(at, unit)] = (sum_slots(slots, stage) * norm_factor).astype(BF16)
        piece = gathered.at[pl.ds(at, unit)]
        for step in steps:
            remote(piece, piece, out_stage, offset(*step)).start()

    share(0, mx * side + ty, cz, 5, xy_steps, 10)
    share(1, mx * side + tx, cy, 6, xz_steps, 11)

    receive_halos(3)
    gather(halo.at[2], 0, 3, west, "straight")
    gather(halo.at[3], 1, 1, east, "straight")
    gather(halo.at[4], 0, 0, top, "turned")
    gather(halo.at[5], 1, 2, bottom, "turned")

    def input_back(i, carry):
        value = d_first_s[i]
        left, right = column_shifts(value, 2, 3, i)
        d_input = tap(0, 0) * right + tap(0, 1) * value + tap(0, 2) * left
        on_top = jnp.where(i == 0, 1.0, 0.0)
        on_bottom = jnp.where(i == 7, 1.0, 0.0)
        d_input += on_top * (tap(0, 0) * halo[4]) + on_bottom * (tap(0, 2) * halo[5])
        at = pl.multiple_of(lax.rem(i + 7, 8) * 96, 96)
        d_mixed = d_mix_s[pl.ds(at, 96), :].astype(F32).reshape(FACES, SIDE, channels)
        gi_out[:, pl.ds(i, 1)] = (
            (d_input + d_mixed).reshape(FACES, 1, SIDE, channels).astype(BF16)
        )
        return carry

    lax.fori_loop(0, 8, input_back, 0)

    small_z[tx] = sum_slots(small_y, 8).astype(BF16)
    spread_slot(small_z, tx, z_steps, 9)
    def core_back(region):
        piece = gathered.at[pl.ds(base + region * REGION, REGION)]
        return remote(piece, piece, 12 + region, sibling)

    shares = nx * side - 1
    for region in range(2):
        whole_wait(gathered.at[pl.ds(0, unit * shares)], red_recv.at[10 + region])
        core_back(region).start()
    tile32[...] = sum_slots(small_z, 9) * norm_factor

    def row_at(line, size):
        pieces = [tile32[line + number : line + number + 1, :] for number in range(-(-size // 128))]
        return jnp.concatenate(pieces, axis=1)[:, :size].astype(BF16)

    for axis in range(2):
        for number in range(3):
            taps_out[number, axis : axis + 1, :] = row_at(9 + 2 * (3 * axis + number), channels)
    for out, line in (
        (b_up_out, 0),
        (b_gates_out, 6),
        (gain_out, 21),
        (b_down_out, 23),
        (b_cand_out, 25),
    ):
        out[...] = row_at(line, out.shape[0]).reshape(out.shape)

    for region in range(2):
        core_back(region).wait_recv()

    def unpack(at, out):
        columns_of_tiles = out.shape[1] // 128
        for row in range(out.shape[0] // 16):
            for column in range(columns_of_tiles):
                out[row * 16 : row * 16 + 16, column * 128 : column * 128 + 128] = gathered[
                    tile_place(at + row * columns_of_tiles + column)
                ]

    unpack(CAND_AT, cand_out)
    unpack(GATES_AT, gates_out)
    unpack(DOWN_AT, down_out)
    unpack(UP_AT, up_out)

    for exchange in range(4):
        finish_halo_sends(exchange)
    for number in range(2):
        pl.when(far_sends[number])(far_copies[number].wait_send)
    small_core.wait_send()
    for region in range(2):
        core_copy(region).wait_send()
        core_back(region).wait_send()
    for ref, stage in (
        (xy_rcv, 2),
        (xz_rcv, 3),
        (cz.at[pl.ds(0, side - 1)], 5),
        (cy.at[pl.ds(0, side - 1)], 6),
        (small_x.at[pl.ds(0, nx - 1)], 7),
        (small_y.at[pl.ds(0, side - 1)], 8),
        (small_z.at[pl.ds(0, side - 1)], 9),
        (gathered.at[pl.ds(0, unit * shares)], 10),
        (gathered.at[pl.ds(0, unit * shares)], 11),
    ):
        whole_wait(ref, red_send.at[stage])


def relay_kernel(count, *refs):
    copies = [
        pltpu.make_async_copy(refs[number], refs[count + number], refs[-1].at[number])
        for number in range(count)
    ]
    for copy in copies:
        copy.start()
    for copy in copies:
        copy.wait()


def on_device(
    inputs,
    state,
    cotangent,
    adjacency,
    taps,
    gain,
    w_up,
    b_up,
    w_down,
    b_down,
    w_gates,
    b_gates,
    w_cand,
    b_cand,
):
    channels = inputs.shape[-1]
    wide = w_up.shape[1]
    tokens = FACES * SIDE * SIDE
    lines = FACES * SIDE
    tile_count, date_count = lax.axis_size("tile"), lax.axis_size("date")
    side = 2 ** ((tile_count.bit_length() - 2) // 2)
    x_low = date_count // 2
    nx = 2 * x_low
    unit = REGION // (nx * side)
    norm_factor = float(tokens * tile_count * date_count) ** (-0.5)
    vmem = pl.BlockSpec(memory_space=pltpu.VMEM)
    hbm = pl.BlockSpec(memory_space=pltpu.HBM)
    grid_shape = (FACES, SIDE, SIDE, channels)

    def buf(*shape):
        return pltpu.VMEM(shape, BF16)

    def wide_buf(*shape):
        return pltpu.VMEM(shape, F32)

    def arr(*shape):
        return jax.ShapeDtypeStruct(shape, BF16)

    shares = nx * side - 1
    results = (
        arr(*grid_shape),
        arr(*grid_shape),
        arr(3, 2, channels),
        arr(channels),
        arr(channels, wide),
        arr(wide),
        arr(channels, wide),
        arr(channels),
        arr(2 * channels, 2 * channels),
        arr(2 * channels),
        arr(channels, 2 * channels),
        arr(channels),
    )
    made = pl.pallas_call(
        functools.partial(level_kernel, side, x_low, norm_factor),
        name="level",
        out_shape=tuple(pltpu.VMEM(result.shape, result.dtype) for result in results),
        in_specs=[hbm] * 14,
        out_specs=[vmem] * 12,
        scratch_shapes=[
            pltpu.SMEM((4, 2, FACES), jnp.int32),
            buf(*grid_shape),
            buf(*grid_shape),
            buf(*grid_shape),
            buf(3, 2, channels),
            buf(channels),
            buf(wide),
            buf(channels),
            buf(2 * channels),
            buf(channels),
            buf(channels, wide),
            buf(channels, wide),
            buf(2 * channels, 2 * channels),
            buf(channels, 2 * channels),
            wide_buf(16, wide),
            pltpu.SMEM((4, FACES), jnp.int32),
            buf(4, 2, lines, channels),
            buf(4, 2, lines, channels),
            buf(4, 2, TURNED * SIDE, channels),
            buf(4, 2, TURNED * SIDE, channels),
            buf(2, 2 * TURNED * SIDE, channels),
            buf(2, 2 * TURNED * SIDE, channels),
            wide_buf(2, 2, TURNED + 1, SIDE, channels),
            wide_buf(2, ZERO_LINE + 1, SIDE, channels),
            wide_buf(6, FACES, SIDE, channels),
            wide_buf(4, FACES, SIDE, channels),
            wide_buf(10, FACES, SIDE, channels),
            wide_buf(10, FACES, SIDE, channels),
            wide_buf(8, FACES, SIDE, channels),
            buf(2 * channels, channels),
            buf(2 * channels, channels),
            buf(channels, channels),
            buf(channels, channels),
            buf(tokens, channels),
            buf(tokens, channels),
            buf(tokens, wide),
            buf(tokens, wide),
            buf(tokens, channels),
            buf(tokens, 2 * channels),
            buf(tokens, 2 * channels),
            buf(tokens, channels),
            wide_buf(16, wide),
            wide_buf(32, 128),
            buf(2, 32, 128),
            buf(nx, 32, 128),
            buf(side, 32, 128),
            buf(side, 32, 128),
            buf(2 * HALF, 16, 128),
            buf(HALF, 16, 128),
            buf(HALF, 16, 128),
            buf(shares, unit, 16, 128),
            buf(shares, unit, 16, 128),
            buf(side, unit, 16, 128),
            buf(side, unit, 16, 128),
            buf(2 * HALF, 16, 128),
            pltpu.SemaphoreType.DMA((14,)),
            pltpu.SemaphoreType.DMA((4, 4)),
            pltpu.SemaphoreType.DMA((4, 4)),
            pltpu.SemaphoreType.DMA((2,)),
            pltpu.SemaphoreType.DMA((2,)),
            pltpu.SemaphoreType.DMA((14,)),
            pltpu.SemaphoreType.DMA((14,)),
        ],
        compiler_params=pltpu.CompilerParams(
            collective_id=0, has_side_effects=True, vmem_limit_bytes=60 * 2**20
        ),
    )(
        adjacency.transpose(1, 2, 0),
        inputs.reshape(grid_shape),
        state.reshape(grid_shape),
        cotangent.reshape(grid_shape),
        taps.transpose(1, 0, 2),
        gain,
        b_up,
        b_down,
        b_gates,
        b_cand,
        w_up,
        w_down.T,
        w_gates,
        w_cand.T,
    )
    new_rows, grad_rows, g_taps, g_gain, g_up, g_bup, g_down, g_bdown, g_gates, g_bgates, g_cand, g_bcand = (
        pl.pallas_call(
            functools.partial(relay_kernel, len(results)),
            name="relay",
            out_shape=results,
            in_specs=[vmem] * 12,
            out_specs=[hbm] * 12,
            scratch_shapes=[pltpu.SemaphoreType.DMA((12,))],
            compiler_params=pltpu.CompilerParams(vmem_limit_bytes=32 * 2**20),
        )(*made)
    )
    return (
        new_rows.reshape(inputs.shape),
        grad_rows.reshape(inputs.shape),
        g_taps.transpose(1, 0, 2),
        g_gain,
        g_up,
        g_bup,
        g_down.T,
        g_bdown,
        g_gates,
        g_bgates,
        g_cand.T,
        g_bcand,
    )


def solution(mesh):
    field = P("tile", "date", None, None, None, None)
    return jax.shard_map(
        on_device,
        mesh=mesh,
        in_specs=(field,) * 3 + (P(),) * 11,
        out_specs=(field,) * 2 + (P(),) * 10,
        check_vma=False,
    )
```

```python
import functools
import math

import jax
import jax.numpy as jnp
from jax import lax
from jax.experimental import pallas as pl
from jax.experimental.pallas import tpu as pltpu
from jax.sharding import PartitionSpec as P

EPSILON = 1e-06
MESH = pl.DeviceIdType.MESH
F32 = jnp.float32
BF16 = jnp.bfloat16
FACES = 12
SIDE = 8
HALF = 128
REGION = 64
TURNED = 4
ZERO_LINE = FACES + TURNED
GELU_A = math.sqrt(2.0 / math.pi)
GELU_B = 0.044715
ROW_BUP, ROW_BGATES, ROW_TAPS, ROW_GAIN, ROW_BDOWN, ROW_BCAND = 0, 1, 2, 8, 9, 10
SMALL_ROWS = ((0, 6), (1, 3)) + tuple((row, 2) for row in range(2, 11))
CAND_AT, GATES_AT, DOWN_AT, UP_AT, SMALL_AT = 0, 36, 108, 180, 252


def nn(left, right):
    return jnp.dot(left, right, preferred_element_type=F32)


def nt(left, right):
    return lax.dot_general(left, right, (((1,), (1,)), ((), ())), preferred_element_type=F32)


def tn(left, right):
    return lax.dot_general(left, right, (((0,), (0,)), ((), ())), preferred_element_type=F32)


def sigmoid(value):
    return 0.5 + 0.5 * jnp.tanh(0.5 * value)


def tile_place(number):
    if 64 <= number < 128:
        return number + 64
    if 128 <= number < 192:
        return number - 64
    return number


def store_tiles(slab, at, matrix):
    rows, columns = matrix.shape
    packed = matrix.astype(BF16)
    across = columns // 128
    for row in range(rows // 16):
        for column in range(across):
            slab[tile_place(at + row * across + column)] = packed[
                row * 16 : row * 16 + 16, column * 128 : column * 128 + 128
            ]


def level_kernel(
    side,
    x_low,
    norm_factor,
    adj_in,
    x_in,
    h_in,
    g_in,
    taps_in,
    gain_in,
    b_up_in,
    b_down_in,
    b_gates_in,
    b_cand_in,
    w_up_in,
    w_down_in,
    w_gates_in,
    w_cand_in,
    ns_out,
    gi_out,
    taps_out,
    gain_out,
    up_out,
    b_up_out,
    down_out,
    b_down_out,
    gates_out,
    b_gates_out,
    cand_out,
    b_cand_out,
    adj,
    x_ref,
    h_ref,
    g_ref,
    taps_ref,
    gain_ref,
    b_up_ref,
    b_down_ref,
    b_gates_ref,
    b_cand_ref,
    w_up,
    w_down_t,
    w_gates,
    w_cand_t,
    par,
    rank_of,
    snd,
    rcv,
    turn_snd,
    turn_rcv,
    far_snd,
    far_rcv,
    far_pool,
    pool,
    halo,
    columns,
    field,
    d_sec,
    d_first_s,
    wg_u,
    wg_r,
    wc_m,
    wc_r,
    prior_s,
    normed_s,
    hid_s,
    d_pre_s,
    d_mix_s,
    d_gate_s,
    joined_s,
    d_cand_s,
    small,
    tile32,
    small_c,
    small_x,
    small_y,
    small_z,
    slab,
    core_rcv,
    t1,
    xy_rcv,
    xz_rcv,
    cz,
    cy,
    gathered,
    load_sem,
    halo_send,
    halo_recv,
    far_send,
    far_recv,
    red_send,
    red_recv,
):
    channels = x_ref.shape[3]
    nx = 2 * x_low
    unit = REGION // (nx * side)
    tile = lax.axis_index("tile")
    date = lax.axis_index("date")
    place_of_tile = lax.div(tile, 2)
    ty, tx = lax.div(place_of_tile, side), lax.rem(place_of_tile, side)
    core = lax.rem(date, 2)
    mx = lax.rem(tile, 2) * x_low + lax.div(date, 2)

    def device(x, y, z, c):
        return ((y * side + z) * 2 + lax.div(x, x_low), lax.rem(x, x_low) * 2 + c)

    x_at = [lax.rem(mx + step, nx) if step else mx for step in range(nx)]
    y_at = [lax.rem(ty + step, side) if step else ty for step in range(side)]
    z_at = [lax.rem(tx + step, side) if step else tx for step in range(side)]
    x_tile = [lax.div(x, x_low) for x in x_at]
    x_date = [lax.rem(x, x_low) * 2 + core for x in x_at]
    y_tile = [y * (2 * side) for y in y_at]
    z_tile = [z * 2 for z in z_at]
    xy_tile = [[x + y for y in y_tile] for x in x_tile]
    xz_tile = [[x + z for z in z_tile] for x in x_tile]

    def offset(dx, dy, dz):
        if not dz:
            return xy_tile[dx][dy] + z_tile[0], x_date[dx]
        if not dy:
            return xz_tile[dx][dz] + y_tile[0], x_date[dx]
        return x_tile[dx] + y_tile[dy] + z_tile[dz], x_date[dx]

    sibling = device(mx, ty, tx, 1 - core)
    across = device(mx, tx, ty, core)
    top, bottom = ty == 0, ty == side - 1
    west, east = tx == 0, tx == side - 1
    has_across = jnp.logical_and(
        ty != tx,
        jnp.logical_or(jnp.logical_or(top, bottom), jnp.logical_or(west, east)),
    )

    def far(step):
        dx, dy, dz = step
        return min(dx, nx - dx) + min(dy, side - dy) + min(dz, side - dz)

    xy_steps = [(dx, dy, 0) for dx in range(nx) for dy in range(side) if dx or dy]
    xz_steps = [(dx, 0, dz) for dx in range(nx) for dz in range(side) if dx or dz]
    xy_steps.sort(key=far, reverse=True)
    xz_steps.sort(key=far, reverse=True)
    x_steps = [(dx, 0, 0) for dx in range(1, nx)]
    y_steps = [(0, dy, 0) for dy in range(1, side)]
    z_steps = [(0, 0, dz) for dz in range(1, side)]

    barrier = pltpu.get_barrier_semaphore()

    @pl.when(has_across)
    def _():
        pl.semaphore_signal(barrier, inc=1, device_id=across, device_id_type=MESH)

    loads = [
        pltpu.make_async_copy(src, dst, load_sem.at[number])
        for number, (src, dst) in enumerate(
            (
                (x_in, x_ref),
                (adj_in, adj),
                (taps_in, taps_ref),
                (w_gates_in, w_gates),
                (w_cand_in, w_cand_t),
                (gain_in, gain_ref),
                (b_up_in, b_up_ref),
                (b_down_in, b_down_ref),
                (b_gates_in, b_gates_ref),
                (b_cand_in, b_cand_ref),
                (w_up_in, w_up),
                (w_down_in, w_down_t),
                (h_in, h_ref),
                (g_in, g_ref),
            )
        )
    ]
    loads[0].start()
    loads[1].start()
    peers = [offset(*step) for step in sorted(xy_steps, key=far)]
    peers += [offset(*step) for step in sorted(xz_steps, key=far) if step[2]]
    peers.append(sibling)
    for peer in peers:
        pl.semaphore_signal(barrier, inc=1, device_id=peer, device_id_type=MESH)
    for load in loads[2:]:
        load.start()

    def tap(axis, number):
        row = ROW_TAPS + 3 * axis + number
        return par[row : row + 1, :channels].reshape(1, 1, channels)

    def set_columns(value, i):
        columns[0, :, pl.ds(i, 1), :] = value[:, 0:1, :]
        columns[1, :, pl.ds(i, 1), :] = value[:, 7:8, :]

    def rounded(value):
        return value.astype(BF16).astype(F32)

    def put_line(exchange, kind, value):
        snd[exchange, kind] = value.reshape(FACES * SIDE, channels).astype(BF16)

    def put_columns(exchange):
        put_line(exchange, 0, columns[1])
        put_line(exchange, 1, columns[0])

    def put_turned(ref, faces, line_of):
        lines = [line_of(face).astype(F32) for face in faces]
        ref[...] = jnp.concatenate(lines, axis=0).astype(BF16)

    def is_turned(edge, face):
        return adj[edge, 1, face] != (edge + 2) % 4

    loads[1].wait()
    turned_faces = []
    for edge in range(4):
        count = jnp.int32(0)
        chosen = [jnp.int32(0)] * TURNED
        for face in range(FACES):
            rank_of[edge, face] = count
            here = is_turned(edge, face)
            chosen = [
                jnp.where(jnp.logical_and(here, count == slot), face, old)
                for slot, old in enumerate(chosen)
            ]
            count = count + jnp.where(here, 1, 0)
        turned_faces.append(chosen)

    loads[0].wait()

    def x_row(i):
        return x_ref[:, pl.ds(i, 1)].astype(F32).reshape(FACES, SIDE, channels)

    def x_lines(i, carry):
        value = x_row(i)
        set_columns(value, i)
        columns[2, :, pl.ds(i, 1), :] = value[:, 1:2, :]
        columns[3, :, pl.ds(i, 1), :] = value[:, 6:7, :]
        return carry

    lax.fori_loop(0, 8, x_lines, 0)
    put_columns(0)

    put_turned(turn_snd.at[0, 0], turned_faces[0], lambda face: x_ref[face, 0])
    put_turned(turn_snd.at[0, 1], turned_faces[2], lambda face: x_ref[face, 7])
    for which, edge, order in ((0, 3, (0, 2)), (1, 1, (3, 1))):
        for position, column in enumerate(order):
            part = pl.ds(position * TURNED * SIDE, TURNED * SIDE)
            put_turned(
                far_snd.at[which, part],
                turned_faces[edge],
                lambda face, column=column: columns[column, face],
            )

    @pl.when(has_across)
    def _():
        pl.semaphore_wait(barrier, len(peers) + 1)

    @pl.when(jnp.logical_not(has_across))
    def _():
        pl.semaphore_wait(barrier, len(peers))

    row_first = jnp.logical_and(top, jnp.logical_not(west))
    row_last = jnp.logical_and(bottom, jnp.logical_not(east))
    col_first = jnp.logical_and(west, jnp.logical_not(top))
    col_last = jnp.logical_and(east, jnp.logical_not(bottom))
    corners = (jnp.logical_and(top, west), jnp.logical_and(bottom, east))

    far_copies = [
        pltpu.make_async_remote_copy(
            src_ref=far_snd.at[number],
            dst_ref=far_rcv.at[number],
            send_sem=far_send.at[number],
            recv_sem=far_recv.at[number],
            device_id=across,
            device_id_type=MESH,
        )
        for number in range(2)
    ]
    far_sends, far_receives = (col_first, col_last), (row_first, row_last)

    def halo_copies(exchange):
        if exchange in (0, 3):
            ahead, behind = offset(0, 0, 1), offset(0, 0, side - 1)
        else:
            ahead, behind = offset(0, 1, 0), offset(0, side - 1, 0)
        if exchange in (0, 2):
            sends, receives = (row_first, row_last), (col_first, col_last)
        else:
            sends, receives = (col_first, col_last), (row_first, row_last)
        copies = []
        for kind, target in enumerate((ahead, behind, across, across)):
            turns = kind >= 2
            if turns and exchange == 1:
                continue
            number = kind % 2
            copy = pltpu.make_async_remote_copy(
                src_ref=(turn_snd if turns else snd).at[exchange, number],
                dst_ref=(turn_rcv if turns else rcv).at[exchange, number],
                send_sem=halo_send.at[exchange, kind],
                recv_sem=halo_recv.at[exchange, kind],
                device_id=target,
                device_id_type=MESH,
            )
            copies.append(
                (copy, sends[number] if turns else None, receives[number] if turns else None)
            )
        return copies

    def start_halos(exchange):
        for copy, sends, _ in reversed(halo_copies(exchange)):
            if sends is None:
                copy.start()
            else:
                pl.when(sends)(copy.start)

    def finish_halo_sends(exchange):
        for copy, sends, _ in halo_copies(exchange):
            if sends is None:
                copy.wait_send()
            else:
                pl.when(sends)(copy.wait_send)

    def receive_halos(exchange):
        for kind, (copy, _, receives) in enumerate(halo_copies(exchange)):
            number = kind % 2
            if kind < 2:
                copy.wait_recv()
                pool[number, :FACES] = (
                    rcv[exchange, number].astype(F32).reshape(FACES, SIDE, channels)
                )
                continue

            def spread(ref):
                pool[number, FACES:ZERO_LINE] = (
                    ref[exchange, number].astype(F32).reshape(TURNED, SIDE, channels)
                )

            @pl.when(receives)
            def _():
                copy.wait_recv()
                spread(turn_rcv)

            @pl.when(corners[number])
            def _():
                spread(turn_snd)

    def gather(to, which, edge, on_border, mode):
        for face in range(FACES):
            neighbour = adj[edge, 0, face]
            turned = is_turned(edge, face)
            across_line = FACES + rank_of[3 - edge, neighbour]
            if mode == "both":
                there = jnp.where(turned, across_line, neighbour)
                index = jnp.where(on_border, there, face)
            elif mode == "straight":
                index = jnp.where(on_border, jnp.where(turned, ZERO_LINE, neighbour), face)
            else:
                index = jnp.where(jnp.logical_and(on_border, turned), across_line, ZERO_LINE)
            to[face] = pool[which, index]

    def border_lines(to, which, edge, on_border, row):
        def spread(ref):
            far_pool[which, :, :TURNED] = (
                ref[...].astype(F32).reshape(2, TURNED, SIDE, channels)
            )

        @pl.when(far_receives[which])
        def _():
            far_copies[which].wait_recv()
            spread(far_rcv.at[which])

        @pl.when(corners[which])
        def _():
            spread(far_snd.at[which])

        own = x_row(row)
        for face in range(FACES):
            neighbour = adj[edge, 0, face]
            turned = jnp.logical_and(on_border, is_turned(edge, face))
            straight = jnp.where(on_border, jnp.where(turned, ZERO_LINE, neighbour), face)
            slot = rank_of[3 - edge, neighbour]
            low, high = far_pool[which, 0, slot], far_pool[which, 1, slot]
            lines = (own[face], low, high) if edge == 0 else (low, high, own[face])
            made = sum(tap(0, number)[0] * lines[number] for number in range(3))
            to[face] = jnp.where(turned, rounded(made), pool[which, straight])

    place = lax.broadcasted_iota(jnp.int32, (FACES, SIDE, channels), 1)

    def upright(which, i):
        return jnp.broadcast_to(halo[which, :, pl.ds(i, 1), :], (FACES, SIDE, channels))

    def column_shifts(value, west_lines, east_lines, i):
        left = jnp.where(place == 0, upright(west_lines, i), pltpu.roll(value, 1, 1))
        right = jnp.where(place == 7, upright(east_lines, i), pltpu.roll(value, 7, 1))
        return left, right

    start_halos(0)
    for number in range(2):
        pl.when(far_sends[number])(far_copies[number].start)
    pool[...] = jnp.zeros_like(pool)
    far_pool[...] = jnp.zeros_like(far_pool)
    small[...] = jnp.zeros_like(small)
    slab[SMALL_AT : 2 * HALF] = jnp.zeros((2 * HALF - SMALL_AT, 16, 128), BF16)
    for number in range(2, 10):
        loads[number].wait()
    for axis in range(2):
        for number in range(3):
            row = ROW_TAPS + 3 * axis + number
            par[row : row + 1, :channels] = taps_ref[number, axis : axis + 1, :].astype(F32)
    for row, ref in (
        (ROW_GAIN, gain_ref),
        (ROW_BUP, b_up_ref),
        (ROW_BDOWN, b_down_ref),
        (ROW_BGATES, b_gates_ref),
        (ROW_BCAND, b_cand_ref),
    ):
        size = ref.shape[0]
        par[row : row + 1, :size] = ref[...].astype(F32).reshape(1, size)
    wg_u[...] = w_gates[:, :channels]
    wg_r[...] = w_gates[:, channels:]
    wc_m[...] = w_cand_t[:, :channels]
    wc_r[...] = w_cand_t[:, channels:]
    for load in loads[10:]:
        load.wait()

    receive_halos(0)
    gather(halo.at[0], 0, 3, west, "both")
    gather(halo.at[1], 1, 1, east, "both")

    def first_pass(i, carry):
        value = x_row(i)
        left, right = column_shifts(value, 0, 1, i)
        first = rounded(tap(0, 0) * left + tap(0, 1) * value + tap(0, 2) * right)
        field[i + 1] = first
        return carry

    lax.fori_loop(0, 8, first_pass, 0)
    put_line(1, 0, field[8])
    put_line(1, 1, field[1])
    start_halos(1)

    def vector(row, start, size):
        return par[row : row + 1, start : start + size]

    def cell(blocks, sums, before_norm_back=None):
        gain = vector(ROW_GAIN, 0, channels)

        def second_row(i):
            return tap(1, 0) * field[i] + tap(1, 1) * field[i + 1] + tap(1, 2) * field[i + 2]

        def row_of(ref):
            return lambda i: ref[:, pl.ds(i, 1)].astype(F32)

        def joint(block, read):
            parts = [read(i).reshape(FACES * SIDE, channels) for i in block[1]]
            return parts[0] if len(parts) == 1 else jnp.concatenate(parts, axis=0)

        def rows(block):
            return pl.ds(pl.multiple_of(block[0] * 96, 96), 96 * len(block[1]))

        states = [{"block": block} for block in blocks]

        def norm(at):
            centred = joint(at["block"], second_row)
            centred = centred - jnp.mean(centred, axis=-1, keepdims=True)
            at["inv"] = lax.rsqrt(jnp.mean(centred * centred, axis=-1, keepdims=True) + EPSILON)
            at["standard"] = centred * at["inv"]
            at["normed"] = (at["standard"] * gain).astype(BF16)
            normed_s[rows(at["block"]), :] = at["normed"]

        def up(at):
            at["pre"] = nn(at["normed"], w_up[...]) + vector(ROW_BUP, 0, w_up.shape[1])

        def bend(at):
            pre = at["pre"]
            square = pre * pre
            curve = jnp.tanh(pre * (GELU_A + (GELU_A * GELU_B) * square))
            rise = 1.0 + curve
            half = 0.5 * pre
            at["hid"] = (half * rise).astype(BF16)
            hid_s[rows(at["block"]), :] = at["hid"]
            at["slope"] = rise * (
                0.5 + half * (1.0 - curve) * (GELU_A + (3.0 * GELU_A * GELU_B) * square)
            )

        def down(at):
            mixed = (
                joint(at["block"], row_of(x_ref))
                + nt(at["hid"], w_down_t[...])
                + vector(ROW_BDOWN, 0, channels)
            )
            at["mixed"] = mixed.astype(BF16)
            joined_s[rows(at["block"]), :channels] = at["mixed"]

        def gates(at):
            mixed = at["mixed"]
            at["prior"] = joint(at["block"], row_of(h_ref))
            prior_b = at["prior"].astype(BF16)
            prior_s[rows(at["block"]), :] = prior_b
            at["reset"] = sigmoid(
                nn(mixed, wg_r[:channels])
                + nn(prior_b, wg_r[channels:])
                + vector(ROW_BGATES, channels, channels)
            )
            at["update"] = sigmoid(
                nn(mixed, wg_u[:channels])
                + nn(prior_b, wg_u[channels:])
                + vector(ROW_BGATES, 0, channels)
            )

        def propose(at):
            reset_state = (at["reset"] * at["prior"]).astype(BF16)
            joined_s[rows(at["block"]), channels:] = reset_state
            at["candidate"] = jnp.tanh(
                nt(at["mixed"], wc_m[...])
                + nt(reset_state, wc_r[...])
                + vector(ROW_BCAND, 0, channels)
            )

        def renew(at):
            update, candidate, prior = at["update"], at["candidate"], at["prior"]
            new = rounded((1.0 - update) * candidate + update * prior)
            for number, i in enumerate(at["block"][1]):
                ns_out[:, pl.ds(i, 1)] = (
                    new[number * 96 : number * 96 + 96]
                    .reshape(FACES, 1, SIDE, channels)
                    .astype(BF16)
                )
            kept = joint(at["block"], row_of(g_ref)) * (1.0 - update)
            at["d_cand"] = (kept * (1.0 - candidate * candidate)).astype(BF16)
            d_cand_s[rows(at["block"]), :] = at["d_cand"]
            at["d_update"] = (kept * (prior - candidate) * update).astype(BF16)
            d_gate_s[rows(at["block"]), :channels] = at["d_update"]

        def gates_back(at):
            reset = at["reset"]
            at["d_reset"] = (
                nn(at["d_cand"], wc_r[...]) * at["prior"] * reset * (1.0 - reset)
            ).astype(BF16)
            d_gate_s[rows(at["block"]), channels:] = at["d_reset"]

        def mixed_back(at):
            at["d_mixed"] = (
                nn(at["d_cand"], wc_m[...])
                + nt(at["d_update"], wg_u[:channels])
                + nt(at["d_reset"], wg_r[:channels])
            ).astype(BF16)
            d_mix_s[rows(at["block"]), :] = at["d_mixed"]

        def hidden_back(at):
            at["d_pre"] = (nn(at["d_mixed"], w_down_t[...]) * at["slope"]).astype(BF16)
            d_pre_s[rows(at["block"]), :] = at["d_pre"]

        def norm_back(at):
            d_normed = nt(at["d_pre"], w_up[...])
            standard = at["standard"]
            d_standard = d_normed * gain
            d_second = rounded(
                at["inv"]
                * (
                    d_standard
                    - jnp.mean(d_standard, axis=-1, keepdims=True)
                    - standard * jnp.mean(d_standard * standard, axis=-1, keepdims=True)
                )
            )
            for number, i in enumerate(at["block"][1]):
                d_sec[i + 1] = d_second[number * 96 : number * 96 + 96].reshape(
                    FACES, SIDE, channels
                )
            at["gain"] = d_normed * standard

        for stage in (
            norm, up, bend, down, gates, propose, renew, gates_back, mixed_back, hidden_back,
        ):
            for at in states:
                stage(at)
        if before_norm_back is not None:
            before_norm_back()
        for at in states:
            norm_back(at)

        def total(value):
            return jnp.sum(value.astype(F32), axis=0, keepdims=True)

        for at in states:
            extras = [
                total(at[name]) for name in ("d_pre", "d_update", "d_reset", "gain", "d_mixed", "d_cand")
            ]
            sums = tuple(old + extra for old, extra in zip(sums, extras))
        return sums

    def remote(src, dst, stage, target):
        return pltpu.make_async_remote_copy(
            src_ref=src,
            dst_ref=dst,
            send_sem=red_send.at[stage],
            recv_sem=red_recv.at[stage],
            device_id=target,
            device_id_type=MESH,
        )

    def whole_wait(ref, sem):
        pltpu.make_async_copy(ref, ref, sem).wait()

    def core_copy(region):
        return remote(
            slab.at[pl.ds((1 - core) * HALF + region * REGION, REGION)],
            core_rcv.at[pl.ds(region * REGION, REGION)],
            region,
            sibling,
        )

    def products():
        store_tiles(slab, CAND_AT, tn(d_cand_s[...], joined_s[...]))
        store_tiles(slab, GATES_AT, tn(joined_s[:, :channels], d_gate_s[...]))
        store_tiles(slab, GATES_AT + 36, tn(prior_s[...], d_gate_s[...]))
        store_tiles(slab, DOWN_AT, tn(d_mix_s[...], hid_s[...]))
        core_copy(0).start()
        store_tiles(slab, UP_AT, tn(normed_s[...], d_pre_s[...]))
        core_copy(1).start()

    zeros = jnp.zeros((1, channels), F32)
    sums = (jnp.zeros((1, w_up.shape[1]), F32), zeros, zeros, zeros, zeros, zeros)
    sums = cell([(0, (1, 2, 3, 4, 5, 6))], sums)
    receive_halos(1)
    border_lines(field.at[0], 0, 0, top, 0)
    border_lines(field.at[9], 1, 2, bottom, 7)
    sums = cell([(6, (7, 0))], sums, products)
    put_line(2, 0, d_sec[8])
    put_line(2, 1, d_sec[1])
    put_turned(turn_snd.at[2, 0], turned_faces[0], lambda face: d_sec[1, face])
    put_turned(turn_snd.at[2, 1], turned_faces[2], lambda face: d_sec[8, face])
    start_halos(2)
    small[ROW_BUP : ROW_BUP + 1, :] = sums[0]
    small[ROW_BGATES : ROW_BGATES + 1, :channels] = sums[1]
    small[ROW_BGATES : ROW_BGATES + 1, channels : 2 * channels] = sums[2]
    small[ROW_GAIN : ROW_GAIN + 1, :channels] = sums[3]
    small[ROW_BDOWN : ROW_BDOWN + 1, :channels] = sums[4]
    small[ROW_BCAND : ROW_BCAND + 1, :channels] = sums[5]

    def add_cores(region):
        core_copy(region).wait_recv()

        def some(step, carry):
            here = region * REGION + step * 8
            total = slab[pl.ds(core * HALF + here, 8)].astype(F32)
            t1[pl.ds(here, 8)] = (total + core_rcv[pl.ds(here, 8)].astype(F32)).astype(BF16)
            return carry

        lax.fori_loop(0, REGION // 8, some, 0)

    def scatter(region, steps, received, stage):
        for number, step in enumerate(steps):
            dx, dy, dz = step
            other = z_at[dz] if region else y_at[dy]
            remote(
                t1.at[pl.ds(region * REGION + (x_at[dx] * side + other) * unit, unit)],
                received.at[number],
                stage,
                offset(dx, dy, dz),
            ).start()

    add_cores(0)
    scatter(0, xy_steps, xy_rcv, 2)
    add_cores(1)
    scatter(1, xz_steps, xz_rcv, 3)

    receive_halos(2)
    gather(d_sec.at[0], 0, 0, top, "straight")
    gather(d_sec.at[9], 1, 2, bottom, "straight")
    gather(halo.at[2], 0, 3, west, "turned")
    gather(halo.at[3], 1, 1, east, "turned")

    def first_back(i, sums):
        value = d_sec[i + 1]
        d_first = tap(1, 0) * d_sec[i + 2] + tap(1, 1) * value + tap(1, 2) * d_sec[i]
        d_first += jnp.where(place == 0, tap(1, 0) * upright(2, i), 0.0)
        d_first += jnp.where(place == 7, tap(1, 2) * upright(3, i), 0.0)
        d_first = rounded(d_first)
        d_first_s[i] = d_first
        set_columns(d_first, i)
        x_value = x_row(i)
        left, right = column_shifts(x_value, 0, 1, i)
        pairs = (
            (d_first, left),
            (d_first, x_value),
            (d_first, right),
            (value, field[i]),
            (value, field[i + 1]),
            (value, field[i + 2]),
        )
        return tuple(old + jnp.sum(a * c, axis=0) for old, (a, c) in zip(sums, pairs))

    tap_sums = lax.fori_loop(
        0, 8, first_back, tuple(jnp.zeros((SIDE, channels), F32) for _ in range(6))
    )
    put_columns(3)
    put_turned(turn_snd.at[3, 0], turned_faces[3], lambda face: columns[0, face])
    put_turned(turn_snd.at[3, 1], turned_faces[1], lambda face: columns[1, face])
    start_halos(3)

    for number, tap_sum in enumerate(tap_sums):
        row = ROW_TAPS + number
        small[row : row + 1, :channels] = jnp.sum(tap_sum, axis=0, keepdims=True)
    tile32[...] = jnp.zeros_like(tile32)
    line = 0
    for row, count in SMALL_ROWS:
        for number in range(count):
            tile32[line : line + 1, :] = small[row : row + 1, number * 128 : number * 128 + 128]
            line += 1
    small_c[0] = tile32[...].astype(BF16)
    small_core = remote(small_c.at[0], small_c.at[1], 4, sibling)
    small_core.start()

    def spread_slot(slots, me, steps, stage):
        for step in steps:
            remote(slots.at[me], slots.at[me], stage, offset(*step)).start()

    def sum_slots(slots, stage):
        count = slots.shape[0]
        whole_wait(slots.at[pl.ds(0, count - 1)], red_recv.at[stage])
        total = slots[0].astype(F32)
        for number in range(1, count):
            total += slots[number].astype(F32)
        return total

    def add_scattered(region, at, received, slots, slot, stage):
        whole_wait(received, red_recv.at[stage])
        total = t1[pl.ds(region * REGION + at * unit, unit)].astype(F32)
        for number in range(received.shape[0]):
            total += received[number].astype(F32)
        slots[slot] = total.astype(BF16)

    add_scattered(0, mx * side + ty, xy_rcv, cz, tx, 2)
    spread_slot(cz, tx, z_steps, 5)
    add_scattered(1, mx * side + tx, xz_rcv, cy, ty, 3)
    spread_slot(cy, ty, y_steps, 6)
    small_core.wait_recv()
    small_x[mx] = (small_c[0].astype(F32) + small_c[1].astype(F32)).astype(BF16)
    spread_slot(small_x, mx, x_steps, 7)
    small_y[ty] = sum_slots(small_x, 7).astype(BF16)
    spread_slot(small_y, ty, y_steps, 8)

    base = core * HALF

    def share(region, at, slots, stage, steps, out_stage):
        at = base + region * REGION + at * unit
        gathered[pl.ds(at, unit)] = (sum_slots(slots, stage) * norm_factor).astype(BF16)
        piece = gathered.at[pl.ds(at, unit)]
        for step in steps:
            remote(piece, piece, out_stage, offset(*step)).start()

    share(0, mx * side + ty, cz, 5, xy_steps, 10)
    share(1, mx * side + tx, cy, 6, xz_steps, 11)

    receive_halos(3)
    gather(halo.at[2], 0, 3, west, "straight")
    gather(halo.at[3], 1, 1, east, "straight")
    gather(halo.at[4], 0, 0, top, "turned")
    gather(halo.at[5], 1, 2, bottom, "turned")

    def input_back(i, carry):
        value = d_first_s[i]
        left, right = column_shifts(value, 2, 3, i)
        d_input = tap(0, 0) * right + tap(0, 1) * value + tap(0, 2) * left
        on_top = jnp.where(i == 0, 1.0, 0.0)
        on_bottom = jnp.where(i == 7, 1.0, 0.0)
        d_input += on_top * (tap(0, 0) * halo[4]) + on_bottom * (tap(0, 2) * halo[5])
        at = pl.multiple_of(lax.rem(i + 7, 8) * 96, 96)
        d_mixed = d_mix_s[pl.ds(at, 96), :].astype(F32).reshape(FACES, SIDE, channels)
        gi_out[:, pl.ds(i, 1)] = (
            (d_input + d_mixed).reshape(FACES, 1, SIDE, channels).astype(BF16)
        )
        return carry

    lax.fori_loop(0, 8, input_back, 0)

    small_z[tx] = sum_slots(small_y, 8).astype(BF16)
    spread_slot(small_z, tx, z_steps, 9)
    def core_back(region):
        piece = gathered.at[pl.ds(base + region * REGION, REGION)]
        return remote(piece, piece, 12 + region, sibling)

    shares = nx * side - 1
    for region in range(2):
        whole_wait(gathered.at[pl.ds(0, unit * shares)], red_recv.at[10 + region])
        core_back(region).start()
    tile32[...] = sum_slots(small_z, 9) * norm_factor

    def row_at(line, size):
        pieces = [tile32[line + number : line + number + 1, :] for number in range(-(-size // 128))]
        return jnp.concatenate(pieces, axis=1)[:, :size].astype(BF16)

    for axis in range(2):
        for number in range(3):
            taps_out[number, axis : axis + 1, :] = row_at(9 + 2 * (3 * axis + number), channels)
    for out, line in (
        (b_up_out, 0),
        (b_gates_out, 6),
        (gain_out, 21),
        (b_down_out, 23),
        (b_cand_out, 25),
    ):
        out[...] = row_at(line, out.shape[0]).reshape(out.shape)

    for region in range(2):
        core_back(region).wait_recv()

    def unpack(at, out):
        columns_of_tiles = out.shape[1] // 128
        for row in range(out.shape[0] // 16):
            for column in range(columns_of_tiles):
                out[row * 16 : row * 16 + 16, column * 128 : column * 128 + 128] = gathered[
                    tile_place(at + row * columns_of_tiles + column)
                ]

    unpack(CAND_AT, cand_out)
    unpack(GATES_AT, gates_out)
    unpack(DOWN_AT, down_out)
    unpack(UP_AT, up_out)

    for exchange in range(4):
        finish_halo_sends(exchange)
    for number in range(2):
        pl.when(far_sends[number])(far_copies[number].wait_send)
    small_core.wait_send()
    for region in range(2):
        core_copy(region).wait_send()
        core_back(region).wait_send()
    for ref, stage in (
        (xy_rcv, 2),
        (xz_rcv, 3),
        (cz.at[pl.ds(0, side - 1)], 5),
        (cy.at[pl.ds(0, side - 1)], 6),
        (small_x.at[pl.ds(0, nx - 1)], 7),
        (small_y.at[pl.ds(0, side - 1)], 8),
        (small_z.at[pl.ds(0, side - 1)], 9),
        (gathered.at[pl.ds(0, unit * shares)], 10),
        (gathered.at[pl.ds(0, unit * shares)], 11),
    ):
        whole_wait(ref, red_send.at[stage])


def relay_kernel(count, *refs):
    copies = [
        pltpu.make_async_copy(refs[number], refs[count + number], refs[-1].at[number])
        for number in range(count)
    ]
    for copy in copies:
        copy.start()
    for copy in copies:
        copy.wait()


def on_device(
    inputs,
    state,
    cotangent,
    adjacency,
    taps,
    gain,
    w_up,
    b_up,
    w_down,
    b_down,
    w_gates,
    b_gates,
    w_cand,
    b_cand,
):
    channels = inputs.shape[-1]
    wide = w_up.shape[1]
    tokens = FACES * SIDE * SIDE
    lines = FACES * SIDE
    tile_count, date_count = lax.axis_size("tile"), lax.axis_size("date")
    side = 2 ** ((tile_count.bit_length() - 2) // 2)
    x_low = date_count // 2
    nx = 2 * x_low
    unit = REGION // (nx * side)
    norm_factor = float(tokens * tile_count * date_count) ** (-0.5)
    vmem = pl.BlockSpec(memory_space=pltpu.VMEM)
    hbm = pl.BlockSpec(memory_space=pltpu.HBM)
    grid_shape = (FACES, SIDE, SIDE, channels)

    def buf(*shape):
        return pltpu.VMEM(shape, BF16)

    def wide_buf(*shape):
        return pltpu.VMEM(shape, F32)

    def arr(*shape):
        return jax.ShapeDtypeStruct(shape, BF16)

    shares = nx * side - 1
    results = (
        arr(*grid_shape),
        arr(*grid_shape),
        arr(3, 2, channels),
        arr(channels),
        arr(channels, wide),
        arr(wide),
        arr(channels, wide),
        arr(channels),
        arr(2 * channels, 2 * channels),
        arr(2 * channels),
        arr(channels, 2 * channels),
        arr(channels),
    )
    made = pl.pallas_call(
        functools.partial(level_kernel, side, x_low, norm_factor),
        name="level",
        out_shape=tuple(pltpu.VMEM(result.shape, result.dtype) for result in results),
        in_specs=[hbm] * 14,
        out_specs=[vmem] * 12,
        scratch_shapes=[
            pltpu.SMEM((4, 2, FACES), jnp.int32),
            buf(*grid_shape),
            buf(*grid_shape),
            buf(*grid_shape),
            buf(3, 2, channels),
            buf(channels),
            buf(wide),
            buf(channels),
            buf(2 * channels),
            buf(channels),
            buf(channels, wide),
            buf(channels, wide),
            buf(2 * channels, 2 * channels),
            buf(channels, 2 * channels),
            wide_buf(16, wide),
            pltpu.SMEM((4, FACES), jnp.int32),
            buf(4, 2, lines, channels),
            buf(4, 2, lines, channels),
            buf(4, 2, TURNED * SIDE, channels),
            buf(4, 2, TURNED * SIDE, channels),
            buf(2, 2 * TURNED * SIDE, channels),
            buf(2, 2 * TURNED * SIDE, channels),
            wide_buf(2, 2, TURNED + 1, SIDE, channels),
            wide_buf(2, ZERO_LINE + 1, SIDE, channels),
            wide_buf(6, FACES, SIDE, channels),
            wide_buf(4, FACES, SIDE, channels),
            wide_buf(10, FACES, SIDE, channels),
            wide_buf(10, FACES, SIDE, channels),
            wide_buf(8, FACES, SIDE, channels),
            buf(2 * channels, channels),
            buf(2 * channels, channels),
            buf(channels, channels),
            buf(channels, channels),
            buf(tokens, channels),
            buf(tokens, channels),
            buf(tokens, wide),
            buf(tokens, wide),
            buf(tokens, channels),
            buf(tokens, 2 * channels),
            buf(tokens, 2 * channels),
            buf(tokens, channels),
            wide_buf(16, wide),
            wide_buf(32, 128),
            buf(2, 32, 128),
            buf(nx, 32, 128),
            buf(side, 32, 128),
            buf(side, 32, 128),
            buf(2 * HALF, 16, 128),
            buf(HALF, 16, 128),
            buf(HALF, 16, 128),
            buf(shares, unit, 16, 128),
            buf(shares, unit, 16, 128),
            buf(side, unit, 16, 128),
            buf(side, unit, 16, 128),
            buf(2 * HALF, 16, 128),
            pltpu.SemaphoreType.DMA((14,)),
            pltpu.SemaphoreType.DMA((4, 4)),
            pltpu.SemaphoreType.DMA((4, 4)),
            pltpu.SemaphoreType.DMA((2,)),
            pltpu.SemaphoreType.DMA((2,)),
            pltpu.SemaphoreType.DMA((14,)),
            pltpu.SemaphoreType.DMA((14,)),
        ],
        compiler_params=pltpu.CompilerParams(
            collective_id=0, has_side_effects=True, vmem_limit_bytes=60 * 2**20
        ),
    )(
        adjacency.transpose(1, 2, 0),
        inputs.reshape(grid_shape),
        state.reshape(grid_shape),
        cotangent.reshape(grid_shape),
        taps.transpose(1, 0, 2),
        gain,
        b_up,
        b_down,
        b_gates,
        b_cand,
        w_up,
        w_down.T,
        w_gates,
        w_cand.T,
    )
    new_rows, grad_rows, g_taps, g_gain, g_up, g_bup, g_down, g_bdown, g_gates, g_bgates, g_cand, g_bcand = (
        pl.pallas_call(
            functools.partial(relay_kernel, len(results)),
            name="relay",
            out_shape=results,
            in_specs=[vmem] * 12,
            out_specs=[hbm] * 12,
            scratch_shapes=[pltpu.SemaphoreType.DMA((12,))],
            compiler_params=pltpu.CompilerParams(vmem_limit_bytes=32 * 2**20),
        )(*made)
    )
    return (
        new_rows.reshape(inputs.shape),
        grad_rows.reshape(inputs.shape),
        g_taps.transpose(1, 0, 2),
        g_gain,
        g_up,
        g_bup,
        g_down.T,
        g_bdown,
        g_gates,
        g_bgates,
        g_cand.T,
        g_bcand,
    )


def solution(mesh):
    field = P("tile", "date", None, None, None, None)
    return jax.shard_map(
        on_device,
        mesh=mesh,
        in_specs=(field,) * 3 + (P(),) * 11,
        out_specs=(field,) * 2 + (P(),) * 10,
        check_vma=False,
    )
```
